32 devices in a mesh: dp: 8 (over z, x), row: 2 (over y), col: 2 (over core).
Axes of the slice: x: 2, y: 2, z: 4, core: 2. Of those that a mesh axis runs over, the one named last changes fastest.
Arguments:
- tokens: bfloat16 [8192, 1536], P(('dp', 'row'), 'col'), may hold values from -6 to 6
- cotangent: bfloat16 [8192, 1536], P(('dp', 'row'), 'col'), may hold values from -6 to 6
- gain_one: float32 [1536], P('col'), may hold values from 0.5 to 1.5
- w_query: bfloat16 [1536, 1536], P('row', 'col'), may hold values from -0.15625 to 0.15625
- key_weight: bfloat16 [512, 1536], P('row', 'col'), may hold values from -0.15625 to 0.15625
- value_weight: bfloat16 [512, 1536], P('row', 'col'), may hold values from -0.15625 to 0.15625
- w_out: bfloat16 [1536, 1536], P('col', 'row'), may hold values from -0.875 to 0.875
- gain_two: float32 [1536], P('col'), may hold values from 0.5 to 1.5
- w_router: bfloat16 [16, 1536], P(None, 'col'), may hold values from -0.078125 to 0.078125
- w_gate: bfloat16 [16, 512, 1536], P(None, 'row', 'col'), may hold values from -0.15625 to 0.15625
- w_up: bfloat16 [16, 512, 1536], P(None, 'row', 'col'), may hold values from -0.15625 to 0.15625
- w_down: bfloat16 [16, 512, 1536], P(None, 'row', 'col'), may hold values from -1 to 1
- routes: int32 [8192, 8], P('dp'), may hold values from 0 to 15, all different within a row; in each aligned block of 1024 rows (0 to 1023, 1024 to 2047, ...) at most 768 rows name the same one
- segments: int32 [8, 1024], P('dp'), may hold values from 0 to 3, never falling along the last dimension, each value on 1 to 512 neighbouring positions
Outputs:
- output: bfloat16 [8192, 1536], P(('dp', 'row'), 'col')
- input_grad: float32 [8192, 1536], P(('dp', 'row'), 'col')
- grad_gain_one: float32 [1536], P('col')
- grad_query: float32 [1536, 1536], P('row', ('col', 'dp'))
- grad_key: float32 [512, 1536], P('row', ('col', 'dp'))
- grad_value: float32 [512, 1536], P('row', ('col', 'dp'))
- grad_out: float32 [1536, 1536], P('col', ('row', 'dp'))
- grad_gain_two: float32 [1536], P('col')
- grad_router: float32 [16, 1536], P(None, ('col', 'dp'))
- grad_gate: float32 [16, 512, 1536], P(None, 'row', ('col', 'dp'))
- grad_up: float32 [16, 512, 1536], P(None, 'row', ('col', 'dp'))
- grad_down: float32 [16, 512, 1536], P(None, 'row', ('col', 'dp'))
The draws below stay inside these ranges and needn't reach their ends.
Inputs may be any that keep to these rules, and one draw needn't show every extreme that they name: `routes`: each row names 8 different experts. In each aligned block of 1024 rows (one sequence) no expert is named by more than 768 rows, and in some block one expert is named by exactly 768 rows. `segments`: along each sequence the document numbers never fall; a document holds 1 to 512 tokens.
All inputs are finite; a program needn't handle non-finite values.
Results may differ from the reference program's by a relative error of at most 0.02.
Values may be sent and summed in bfloat16 or wider, within the bound.
A program may use at most 384 MiB of HBM per device.

```python
import math
import jax
import jax.numpy as jnp
import numpy as np
from jax import lax

MODEL_WIDTH = 1536
QUERY_HEADS = 24
KEY_VALUE_HEADS = 8
HEAD_SIZE = 64
H = 512
TOP = 8
E = 16
SEQ = 1024
CAP = 768
SEQS = 8
TOKENS = 8192


def levels(own_key, dims, split, smallest, high):
    loudness = 1.0
    for dim, parts in split:
        steps = jax.random.uniform(jax.random.fold_in(jax.random.fold_in(own_key, 6), dim), (parts,), jnp.float32, smallest / len(split), high / len(split))
        loudness = loudness * jnp.repeat(jnp.exp(steps), dims[dim] // parts).reshape((-1,) + (1,) * (len(dims) - 1 - dim))
    return loudness


def profile(amount, total, bound, slope):
    loads = [(1 << 20) // math.isqrt(standing ** slope) + 1 for standing in range(2, amount + 1)]
    spare, holding = total - bound - (amount - 1), [1] * (amount - 1)
    while spare > 0:
        free = [i for i in range(amount - 1) if holding[i] < bound]
        whole, remaining = sum([loads[i] for i in free]), spare
        for i in free:
            extra = min(bound - holding[i], max(1, remaining * loads[i] // whole), spare)
            holding[i] = holding[i] + extra
            spare = spare - extra
    return np.array([bound] + holding)


def ragged_sizes(own_key, count, total, most, slope):
    if count == 2:
        one = jax.random.randint(own_key, (), max(1, total - most), min(most, total - 1) + 1)
        return jnp.stack([one, total - one])
    sizes = jnp.asarray(profile(count, total, most, slope), jnp.int32)
    pairs = (count - 1) // 2
    source_of, receiver = sizes[1:1 + 2 * pairs:2], sizes[2:2 + 2 * pairs:2]
    room = jnp.minimum(source_of - 1, most - receiver)
    passed = jax.random.randint(jax.random.fold_in(own_key, 1), (pairs,), 0, 1 << 20) % (room + 1)
    sizes = sizes.at[1:1 + 2 * pairs:2].set(source_of - passed).at[2:2 + 2 * pairs:2].set(receiver + passed)
    return sizes[jax.random.permutation(jax.random.fold_in(own_key, 2), count)]


def shared_out(key, own, number, rows, count, top, bound, slope):
    ranking = jax.random.permutation(key, count)
    heavy_load, ordinary = portions_of(count, rows * top, bound, slope, True), portions_of(count, rows * top, bound, slope, False)
    places = jnp.arange(count)

    def named(lengths, turn):
        used = int((lengths > 0).sum())
        fixed = max(1, used // 4)
        moved = fixed + (places - fixed + turn * (used - fixed)) % max(1, count - fixed)
        return jnp.zeros((count,), jnp.int32).at[ranking[jnp.where(places < fixed, places, moved)]].set(jnp.asarray(lengths, jnp.int32))

    lengths = jnp.where(number % 4 == 0, named(heavy_load, number // 4), named(ordinary, number - number // 4 - 1))
    mixed = jax.random.permutation(jax.random.fold_in(own, 3), count)
    giver, sink = mixed[0:count // 2 * 2:2], mixed[1:count // 2 * 2:2]
    margin = jnp.minimum(lengths[giver] - 1, bound - lengths[sink]) // 2
    margin = jnp.where((giver == ranking[0]) | (sink == ranking[0]) | (lengths[sink] == 0), 0, jnp.maximum(margin, 0))
    moved = jax.random.randint(jax.random.fold_in(own, 4), (count // 2,), 0, 1 << 20) % (margin + 1)
    lengths = lengths.at[giver].add(-moved).at[sink].add(moved)
    labels = jnp.searchsorted(jnp.cumsum(lengths), jnp.arange(rows * top), side="right").astype(jnp.int32)
    table = labels.reshape(top, rows).T
    table = table[jax.random.permutation(jax.random.fold_in(own, 1), rows)]
    turn = jax.random.randint(jax.random.fold_in(own, 2), (rows, 1), 0, top)
    return jnp.take_along_axis(table, (jnp.arange(top)[None, :] + turn) % top, axis=1)


def portions_of(amount, total, reach, lean, full):
    weights = [(1 << 20) // math.isqrt(grade ** lean) + 1 for grade in range(1, amount + 1)]
    largest = reach if full else min(reach, max(-(-total // amount), total * weights[0] // sum(weights)))
    least = 1 if total - largest >= amount - 1 else 0
    given, spare = [largest] + [least] * (amount - 1), total - largest - least * (amount - 1)
    while spare > 0:
        candidates = [i for i in range(1, amount) if given[i] < largest] or [i for i in range(1, amount) if given[i] < reach]
        whole, left = sum([weights[i] for i in candidates]), spare
        for i in candidates:
            extra = min(reach - given[i], max(1, left * weights[i] // whole), spare)
            given[i] = given[i] + extra
            spare = spare - extra
    return np.array(given)


def centred(key, dims, scale, limit, cuts=(), kind=jnp.bfloat16):
    factor_of = levels(key, dims, cuts, -0.22, 0.18) if cuts else 1.0
    values = jax.random.normal(key, dims, jnp.float32) * scale * factor_of
    return jnp.minimum(jnp.maximum(values, -limit), limit).astype(kind)


def setup_inputs(seed: int = 0) -> dict:
    key_of = jax.random.split(jax.random.key(seed), 15)
    tokens = centred(key_of[0], (TOKENS, MODEL_WIDTH), 1.0, 6.0, ((0, 16), (1, 2)))
    cotangent = centred(key_of[1], (TOKENS, MODEL_WIDTH), 1.0, 6.0, ((0, 16), (1, 2)))
    gain_one = jnp.clip(1.0 + 0.1 * jax.random.normal(key_of[2], (MODEL_WIDTH,), jnp.float32), 0.5, 1.5)
    w_query = centred(key_of[3], (QUERY_HEADS * HEAD_SIZE, MODEL_WIDTH), MODEL_WIDTH ** -0.5, 0.15625, ((0, 2), (1, 2)))
    key_weight = centred(key_of[4], (KEY_VALUE_HEADS * HEAD_SIZE, MODEL_WIDTH), MODEL_WIDTH ** -0.5, 0.15625, ((0, 2), (1, 2)))
    value_weight = centred(key_of[5], (KEY_VALUE_HEADS * HEAD_SIZE, MODEL_WIDTH), MODEL_WIDTH ** -0.5, 0.15625, ((0, 2), (1, 2)))
    w_out = centred(key_of[6], (MODEL_WIDTH, QUERY_HEADS * HEAD_SIZE), (QUERY_HEADS * HEAD_SIZE // 32) ** -0.5, 0.875, ((0, 2), (1, 2)))
    gain_two = jnp.clip(1.0 + 0.1 * jax.random.normal(key_of[7], (MODEL_WIDTH,), jnp.float32), 0.5, 1.5)
    w_router = centred(key_of[8], (E, MODEL_WIDTH), (4 * MODEL_WIDTH) ** -0.5, 0.078125, ((1, 2),))
    w_gate = centred(key_of[9], (E, H, MODEL_WIDTH), MODEL_WIDTH ** -0.5, 0.15625, ((1, 2), (2, 2)))
    w_up = centred(key_of[10], (E, H, MODEL_WIDTH), MODEL_WIDTH ** -0.5, 0.15625, ((1, 2), (2, 2)))
    w_down = centred(key_of[11], (E, H, MODEL_WIDTH), (H // 16) ** -0.5, 1.0, ((1, 2), (2, 2)))
    routes_keys = jax.random.split(jax.random.fold_in(key_of[12], 1), TOKENS // SEQ)
    routes_turns = jax.random.permutation(jax.random.fold_in(key_of[12], 3), TOKENS // SEQ)
    routes = jax.vmap(lambda own, number: shared_out(jax.random.fold_in(key_of[12], 2), own, number, SEQ, E, TOP, CAP, 1))(routes_keys, routes_turns).reshape((TOKENS, TOP))
    segments = jax.vmap(lambda own: jnp.searchsorted(jnp.cumsum(ragged_sizes(own, 4, SEQ, SEQ // 2, 2)), jnp.arange(SEQ), side="right"))(jax.random.split(key_of[13], SEQS)).reshape((SEQS, SEQ)).astype(jnp.int32)
    return {"tokens": tokens, "cotangent": cotangent, "gain_one": gain_one, "w_query": w_query, "key_weight": key_weight, "value_weight": value_weight, "w_out": w_out, "gain_two": gain_two, "w_router": w_router, "w_gate": w_gate, "w_up": w_up, "w_down": w_down, "routes": routes, "segments": segments}


eps = 1e-06
precise = lax.Precision.HIGHEST

@jax.custom_vjp
def lower_precision(v):
    return lax.optimization_barrier(v.astype(jnp.bfloat16)).astype(jnp.float32)

@jax.custom_vjp
def low_back(v):
    return v

def low_keep(v):
    return (lower_precision(v), None)

def low_pass(kept, grad):
    return (grad,)

def back_keep(v):
    return (v, None)

def back_low(kept, grad):
    return (lower_precision(grad),)
lower_precision.defvjp(low_keep, low_pass)
low_back.defvjp(back_keep, back_low)

def rope_tables(segment):
    length_tokens = segment.shape[0]
    places = jnp.arange(length_tokens, dtype=jnp.int32)
    changed = jnp.concatenate([jnp.ones((1,), dtype=jnp.bool_), segment[1:] != segment[:-1]])
    starts = lax.cummax(jnp.where(changed, places, 0), axis=0)
    offsets = (places - starts).astype(jnp.float32)
    frequency = jnp.exp(jnp.arange(HEAD_SIZE // 2, dtype=jnp.float32) * (-2.0 * math.log(10000.0) / HEAD_SIZE))
    angles = offsets[:, None] * frequency[None, :]
    return (jnp.cos(angles), jnp.sin(angles))

def apply_rotary(values, cosine_table, sine_lookup):
    half_size = values.shape[-1] // 2
    first_half = values[..., :half_size]
    second_half = values[..., half_size:]
    cosine_rows = cosine_table[:, None, :]
    sine_rows = sine_lookup[:, None, :]
    return jnp.concatenate([first_half * cosine_rows - second_half * sine_rows, second_half * cosine_rows + first_half * sine_rows], axis=-1)

def rms_norm(values, gain_values):
    row_scale = lax.rsqrt(lax.optimization_barrier(jnp.mean(values * values, axis=-1, keepdims=True)) + eps)
    return values * row_scale * gain_values

def layer(tokens, weight_list, routes, segment):
    gain_one, w_query, key_weight, value_weight, w_out, gain_two, w_router, w_gate, w_up, w_down = weight_list
    cosine_table, sine_lookup = rope_tables(segment)
    length_tokens = tokens.shape[0]
    normed_one = lower_precision(rms_norm(tokens, gain_one))
    query_raw = low_back(jnp.dot(normed_one, w_query.T, precision=precise))
    key_unrotated = low_back(jnp.dot(normed_one, key_weight.T, precision=precise))
    value_projected = low_back(jnp.dot(normed_one, value_weight.T, precision=precise))
    queries = lower_precision(apply_rotary(query_raw.reshape(length_tokens, QUERY_HEADS, HEAD_SIZE), cosine_table, sine_lookup))
    keys_rotated = lower_precision(apply_rotary(key_unrotated.reshape(length_tokens, KEY_VALUE_HEADS, HEAD_SIZE), cosine_table, sine_lookup))
    values_incoming = lower_precision(value_projected).reshape(length_tokens, KEY_VALUE_HEADS, HEAD_SIZE)
    query_group_width = QUERY_HEADS // KEY_VALUE_HEADS
    keys_all = jnp.repeat(keys_rotated, query_group_width, axis=1)
    values_all = jnp.repeat(values_incoming, query_group_width, axis=1)
    raw_scores = jnp.einsum('qhd,khd->hqk', queries, keys_all, precision=precise) * HEAD_SIZE ** (-0.5)
    scores = low_back(raw_scores)
    places = jnp.arange(length_tokens, dtype=jnp.int32)
    allowed = (places[:, None] >= places[None, :]) & (segment[:, None] == segment[None, :])
    masked = jnp.where(allowed[None], scores, -1e+30)
    row_top = lax.optimization_barrier(jnp.max(masked, axis=-1, keepdims=True))
    exponent = jnp.exp(masked - row_top)
    probability = exponent / lax.optimization_barrier(jnp.sum(exponent, axis=-1, keepdims=True))
    mixed = jnp.einsum('hqk,khd->qhd', lower_precision(probability), values_all, precision=precise).reshape(length_tokens, QUERY_HEADS * HEAD_SIZE)
    mixed = low_back(lower_precision(mixed))
    attended = low_back(jnp.dot(mixed, w_out.T, precision=precise))
    middle = tokens + attended
    normed_two = lower_precision(rms_norm(middle, gain_two))
    logits = jnp.dot(normed_two, w_router.T, precision=precise)
    experts = jnp.arange(E, dtype=jnp.int32)
    picked = (routes[:, :, None] == experts[None, None, :]).astype(jnp.float32)
    chosen = lax.optimization_barrier(jnp.sum(picked * logits[:, None, :], axis=2))
    gate_weight = jax.nn.softmax(chosen, axis=-1)
    spread_weight = lax.optimization_barrier(jnp.sum(gate_weight[:, :, None] * picked, axis=1))
    gate_act = low_back(jnp.einsum('sd,ehd->seh', normed_two, w_gate, precision=precise))
    up_act = low_back(jnp.einsum('sd,ehd->seh', normed_two, w_up, precision=precise))
    hidden = lower_precision(jax.nn.silu(gate_act) * up_act)
    expert_out = low_back(jnp.einsum('seh,ehd->sed', hidden, w_down, precision=precise))
    moe_out = jnp.einsum('se,sed->sd', spread_weight, expert_out, precision=precise)
    return middle + moe_out

def reference(tokens, cotangent, gain_one, w_query, key_weight, value_weight, w_out, gain_two, w_router, w_gate, w_up, w_down, routes, segments):
    weight_list = (gain_one.astype(jnp.float32), w_query.astype(jnp.float32), key_weight.astype(jnp.float32), value_weight.astype(jnp.float32), w_out.astype(jnp.float32), gain_two.astype(jnp.float32), w_router.astype(jnp.float32), w_gate.astype(jnp.float32), w_up.astype(jnp.float32), w_down.astype(jnp.float32))
    token_rows = tokens.astype(jnp.float32).reshape(SEQS, SEQ, MODEL_WIDTH)
    grad_rows = cotangent.astype(jnp.float32).reshape(SEQS, SEQ, MODEL_WIDTH)
    route_rows = routes.reshape(SEQS, SEQ, TOP)

    def one_sequence(totals, pieces):
        tokens_in, grad_in, route_in, segment_in = pieces

        def forward(tokens_arg, weights_arg):
            return layer(tokens_arg, weights_arg, route_in, segment_in)
        result, pullback = jax.vjp(forward, tokens_in, weight_list)
        grad_tokens, grad_weights = pullback(grad_in)
        totals = jax.tree.map(lambda earlier, later: earlier + later, totals, grad_weights)
        return (totals, (result, grad_tokens))
    zeros_init = jax.tree.map(jnp.zeros_like, weight_list)
    totals, (results, grad_tokens) = lax.scan(one_sequence, zeros_init, (token_rows, grad_rows, route_rows, segments))
    return (results.reshape(TOKENS, MODEL_WIDTH).astype(jnp.bfloat16), grad_tokens.reshape(TOKENS, MODEL_WIDTH), totals[0], totals[1], totals[2], totals[3], totals[4], totals[5], totals[6], totals[7], totals[8], totals[9])
```

```python
import functools
import math

import jax
import jax.numpy as jnp
from jax import lax
from jax.experimental import pallas as pl
from jax.experimental.pallas import tpu as pltpu
from jax.sharding import PartitionSpec as P

WIDTH = 1536
HEAD = 64
E = 16
MINE = 8
EPS = 1e-06
SCALE = HEAD ** (-0.5)
NEG = -1e30
f32 = jnp.float32
bf16 = jnp.bfloat16
MIB = 1 << 20
MESH = pl.DeviceIdType.MESH
A, B = object(), object()


def dot_nt(a, b):
    return lax.dot_general(a, b, (((1,), (1,)), ((), ())), preferred_element_type=f32)


def dot_nn(a, b):
    return lax.dot_general(a, b, (((1,), (0,)), ((), ())), preferred_element_type=f32)


def dot_tn(a, b):
    return lax.dot_general(a, b, (((0,), (0,)), ((), ())), preferred_element_type=f32)


def rotate(u, cosine, sine):
    lane = lax.broadcasted_iota(jnp.int32, u.shape, 1)
    turned = jnp.where((lane & 63) < 32, pltpu.roll(u, 96, 1), pltpu.roll(u, 32, 1))
    return u * cosine + turned * sine


def paired(u, t):
    return jnp.concatenate(
        [u[:, t * 64 : t * 64 + 64], u[:, 192 + t * 64 : 192 + t * 64 + 64]], axis=1
    )


def flip_block(values):
    eye = (
        lax.broadcasted_iota(jnp.int32, (256, 256), 0)
        == lax.broadcasted_iota(jnp.int32, (256, 256), 1)
    ).astype(bf16)
    return jnp.concatenate(
        [dot_nt(eye, values[:, i * 256 : i * 256 + 256]) for i in range(3)], axis=0
    ).astype(bf16)


def load_keys(pairs):
    lane = lax.broadcasted_iota(jnp.int32, (1024, 128), 1)
    for source, first, second in pairs:
        value = source[...].astype(f32)
        first[...] = jnp.where(lane < 64, value, 0.0).astype(bf16)
        second[...] = jnp.where(lane < 64, 0.0, value).astype(bf16)


def key_bias(a, first, start):
    key = first + lax.broadcasted_iota(jnp.int32, (768, 256), 0)
    query = a * 256 + lax.broadcasted_iota(jnp.int32, (768, 256), 1)
    return jnp.where((key <= query) & (key >= start), 0.0, NEG)


def split_shards(values, part, lanes, mx, mz, keep, send):
    nz, w = keep.shape[0], keep.shape[2]
    for zz in range(nz):
        even = values[2 * zz * w : (2 * zz + 1) * w]
        odd = values[(2 * zz + 1) * w : (2 * zz + 2) * w]
        place = jnp.bitwise_xor(zz, mz)
        keep[place, part, :, lanes] = jnp.where(mx == 0, even, odd).astype(bf16)
        send[place, part, :, lanes] = jnp.where(mx == 0, odd, even).astype(bf16)


(
    TOK_C,
    WQ,
    WK,
    WV,
    GAIN,
    ROUTER,
    COT_Y,
    COT_C,
    COT_YC,
    W_PART,
    W_C,
    W_YC,
    GG_ROW,
    GG_COL,
    N_COL,
    N_ROW,
    O_COL,
    O_ROW,
    STAT_TWO,
    G_ROW,
    G_COL,
    G_ROW_COL,
    P_COL,
    P_ROW,
    STAT_ONE,
    GAIN_ROW,
    GAIN_X,
    FAR_B,
) = range(28)
TOK_Y, TOK_YC, MIX_Y, MIX_C, MIX_YC, TRADES = 28, 30, 32, 36, 40, 44


class Refs:
    def __init__(self, names, refs):
        self.__dict__.update(zip(names, refs))


def layer_kernel(n, inputs, outputs, scratch, *refs):
    nz, w = n // 2, 768 // n
    sliced = w % 16 == 0
    a = Refs(inputs, refs[: len(inputs)])
    refs = refs[len(inputs) :]
    o = Refs(outputs, refs[: len(outputs)])
    b = Refs(scratch, refs[len(outputs) :])
    i, r, c = lax.axis_index("dp"), lax.axis_index("row"), lax.axis_index("col")
    mx, mz = lax.rem(i, 2), lax.div(i, 2)

    def block(at, size):
        return pl.ds(pl.multiple_of(at * size, size), size)

    own_rows, far_rows = block(r, 512), block(1 - r, 512)
    to_x, to_row, to_col = {"dp": jnp.bitwise_xor(i, 1)}, {"row": 1 - r}, {"col": 1 - c}

    def to_dp(bits):
        return {"dp": jnp.bitwise_xor(i, bits)}

    def remote(src, dst, sems, at, target):
        return pltpu.make_async_remote_copy(
            src_ref=src,
            dst_ref=dst,
            send_sem=sems[0].at[at],
            recv_sem=sems[1].at[at],
            device_id=target,
            device_id_type=MESH,
        )

    def trade(name, src, dst, target):
        return remote(src, dst, (b.esend, b.erecv), name, target)

    def load(src, dst, at):
        return pltpu.make_async_copy(src, dst, b.lsem.at[at])

    def run(*copies):
        for copy in copies:
            copy.start()
        for copy in copies:
            copy.wait()

    vb = lambda *shape: pltpu.VMEM(shape, bf16)
    vf = lambda *shape: pltpu.VMEM(shape, f32)


    def moe_copies(e):
        return [
            remote(src.at[MINE * (1 - c) + e], dst.at[e], (b.msend, b.mrecv), 3 * e + k, to_col)
            for k, (src, dst) in enumerate(((a.wg, o.rg), (a.wu, o.ru), (a.wd, o.rd)))
        ]

    def weight_loads(e, slot):
        pairs = (
            (a.wg, MINE * c + e),
            (o.rg, e),
            (a.wu, MINE * c + e),
            (o.ru, e),
            (a.wd, MINE * c + e),
            (o.rd, e),
        )
        return [
            pltpu.make_async_copy(ref.at[at], b.weights.at[slot, k], b.wsem.at[slot, k])
            for k, (ref, at) in enumerate(pairs)
        ]


    xsems, zsems = (b.xsend, b.xarrive), (b.zsend, b.zarrive)

    def x_copy(k):
        if (k is A or k is B):
            src, dst = (o.send_a, o.xrecv_a) if k is A else (o.send_b, o.xrecv_b)
            return remote(src, dst, xsems, 8 if k is A else 9, to_x)
        return remote(o.send.at[k], o.xrecv.at[k], xsems, k, to_x)

    def z_copies(k):
        if (k is A or k is B):
            src, dst = (b.sum_a, o.zrecv_a) if k is A else (b.sum_b, o.zrecv_b)
            base = (8 if k is A else 9) * (nz - 1)
            return [
                remote(src.at[s], dst.at[s - 1], zsems, base + s - 1, to_dp(2 * s))
                for s in range(1, nz)
            ]
        return [
            remote(
                b.sums.at[lax.rem(k, 2), s],
                o.zrecv.at[k, s - 1],
                zsems,
                k * (nz - 1) + s - 1,
                to_dp(2 * s),
            )
            for s in range(1, nz)
        ]

    def buffers(k):
        if k is A:
            return b.kept_a, b.came_a, b.sum_a, o.keep_a, o.xrecv_a, o.zrecv_a
        if k is B:
            return b.kept_b, b.came_b, b.sum_b, o.keep_b, o.xrecv_b, o.zrecv_b
        return b.kept, b.came, b.sums.at[lax.rem(k, 2)], o.keep.at[k], o.xrecv.at[k], o.zrecv.at[k]

    def pump(k, again=True):
        x_copy(k).wait_recv()
        kept, came, total, keep, xrecv, _ = buffers(k)
        loads = [load(keep, kept, 4), load(xrecv, came, 5)]
        for copy in loads:
            copy.start()
        if again and not (k is A or k is B):
            for copy in z_copies(k - 2):
                copy.wait_send()
        for copy in loads:
            copy.wait()
        for s in range(1, nz):
            total[s] = (kept[s].astype(f32) + came[s].astype(f32)).astype(bf16)
        for copy in z_copies(k):
            copy.start()

    def complete(k):
        for copy in z_copies(k):
            copy.wait_recv()
        kept, came, _, keep, xrecv, zrecv = buffers(k)
        run(
            load(zrecv, kept.at[pl.ds(0, nz - 1)], 4),
            load(keep.at[0], came.at[0], 5),
            load(xrecv.at[0], came.at[1], 6),
        )
        total = came[0].astype(f32) + came[1].astype(f32)
        for s in range(nz - 1):
            total = total + kept[s].astype(f32)
        return total

    def far_copy(k):
        return remote(b.far_send.at[k % 2], o.far.at[k], (b.fsend, b.frecv), k, to_col)

    def put(values, at):
        for m in range(3):
            b.expert_out[m] = values[:, m * 256 : m * 256 + 256]
        outs = (o.grad_gate, o.grad_up, o.grad_down)
        run(*[load(b.expert_out.at[m], outs[m].at[at], 4 + m) for m in range(3)])

    def finish(k):
        total = complete(k)
        if k >= 2:
            far_copy(k - 2).wait_send()
        b.far_send[k % 2] = total[1].astype(bf16)
        far_copy(k).start()
        put(total[0], MINE * c + k)

    def finish_far(k):
        far_copy(k).wait_recv()
        run(load(o.far.at[k], b.far_here, 4))
        put(b.far_here[...].astype(f32), MINE * (1 - c) + k)


    tok_y = [
        trade(TOK_Y + h, a.tok.at[pl.ds(h * 256, 256)], b.gyo.at[pl.ds(h * 256, 256)], to_row)
        for h in range(2)
    ]
    tok_yc = [
        trade(TOK_YC + h, b.gyo.at[pl.ds(h * 256, 256)], b.gyt.at[pl.ds(h * 256, 256)], to_col)
        for h in range(2)
    ]
    tok_c = trade(TOK_C, a.tok, b.got, to_col)
    heads = [
        trade(WQ, a.wq.at[block(1 - c, 384)], b.wr.at[pl.ds(0, 384)], to_col),
        trade(WK, a.wkey.at[block(1 - c, 128)], b.wr.at[pl.ds(384, 128)], to_col),
        trade(WV, a.wval.at[block(1 - c, 128)], b.wr.at[pl.ds(512, 128)], to_col),
    ]
    gain_copy = trade(GAIN, b.gain_send, b.gain_far, to_col)
    router_copy = trade(ROUTER, a.router, b.router_far, to_col)
    cot_y = trade(COT_Y, a.cot, o.cot_y, to_row)
    cot_c = trade(COT_C, a.cot, o.cot_c, to_col)
    cot_yc = trade(COT_YC, o.cot_y, o.cot_yc, to_col)
    w_part = trade(
        W_PART,
        a.wparts.at[i] if sliced else a.wout,
        o.wy.at[i] if sliced else o.wy,
        to_row,
    )
    w_gather = [
        remote(o.wy.at[i], o.wy.at[i], (b.gsend, b.grecv), bits, to_dp(bits))
        for bits in (range(1, n) if sliced else ())
    ]
    w_c = trade(W_C, a.wout, o.wc, to_col)
    w_yc = trade(W_YC, o.wy, o.wyc, to_col)

    def front_scope(
        tok, w00, wc, wy, wyc, mixed, k0, k1, vt, n1oo, n1ot, n1yo, n1yt, mrow
    ):
        locals_ = [
            load(a.tok, tok, 0),
            load(a.wq.at[block(c, 384)], b.wk.at[pl.ds(0, 384)], 1),
            load(a.wkey.at[block(c, 128)], b.wk.at[pl.ds(384, 128)], 2),
            load(a.wval.at[block(c, 128)], b.wk.at[pl.ds(512, 128)], 3),
        ]
        late = [
            load(a.wout, w00, 10),
            load(a.cot, b.go.at[own_rows], 11),
        ]
        for copy in locals_ + late:
            copy.start()
        b.gain_send[...] = jnp.zeros_like(b.gain_send)
        b.gain_send[0:1, :] = a.g1[...].reshape(1, 768)
        b.gain_send[1:2, :] = a.g2[...].reshape(1, 768)
        barrier = pltpu.get_barrier_semaphore()
        partners = [to_row, to_col] + [to_dp(bits) for bits in range(1, n)]
        for target in partners:
            pl.semaphore_signal(barrier, inc=1, device_id=target, device_id_type=MESH)
        pl.semaphore_wait(barrier, len(partners))
        for copy in [w_part] + tok_y + [tok_c] + heads + [gain_copy, router_copy, cot_y, cot_c, w_c]:
            copy.start()
        for e in range(2):
            for copy in moe_copies(e):
                copy.start()

        w_part.wait()
        for copy in w_gather:
            copy.start()

        seg = a.seg[...].astype(f32)
        seg_column = jnp.broadcast_to(seg, (8, 1024)).T[:, 0:1]
        start, start_column = jnp.zeros_like(seg), jnp.zeros_like(seg_column)
        for number in range(1, 4):
            count = jnp.sum(jnp.where(seg < number, 1.0, 0.0), axis=1, keepdims=True)
            start = jnp.where(seg == number, count, start)
            start_column = jnp.where(seg_column == number, count, start_column)
        b.start[...] = start.astype(jnp.int32)
        lane = lax.broadcasted_iota(jnp.int32, (1024, 128), 1)
        place = lax.broadcasted_iota(jnp.int32, (1024, 128), 0).astype(f32)
        frequency = jnp.exp((lane & 31).astype(f32) * (-2.0 * math.log(10000.0) / HEAD))
        angles = (place - start_column) * frequency
        b.cs[...] = jnp.cos(angles)
        sine = jnp.sin(angles)
        b.sn[...] = jnp.where((lane & 63) < 32, -sine, sine)

        number = jnp.where(lane < MINE, lane + MINE * c, lane - MINE * c)
        number = jnp.where((lane >= MINE) & (c == 1), lane - MINE, number)
        number = jnp.where(lane < E, number, -1)
        used = jnp.zeros((1024, 128), f32)
        routes, number = a.routes[...].astype(f32).T, number.astype(f32)
        for k in range(8):
            used = jnp.where(routes[:, k : k + 1] == number, 1.0, used)
        b.gate[...] = used

        gain_copy.wait()

        def project(x_own, x_oth, place, rows, n_own, n_oth):
            u, v = x_own.astype(f32), x_oth.astype(f32)
            total = jnp.sum(u * u, axis=1, keepdims=True) + jnp.sum(v * v, axis=1, keepdims=True)
            s = lax.rsqrt(total / WIDTH + EPS)
            u = (u * s * b.gain_send[0:1, :]).astype(bf16)
            v = (v * s * b.gain_far[0:1, :]).astype(bf16)
            n_own[rows, :] = u
            n_oth[rows, :] = v
            raw = dot_nt(u, b.wk[...]) + dot_nt(v, b.wr[...])
            cs, sn = b.cs[place, :], b.sn[place, :]
            for t in range(3):
                b.q[place, t * 128 : t * 128 + 128] = rotate(paired(raw, t), cs, sn).astype(bf16)
            b.k[place, :] = rotate(raw[:, 384:512], cs, sn).astype(bf16)
            b.v[place, :] = raw[:, 512:640].astype(bf16)
            return s

        for copy in locals_ + [tok_c] + heads:
            copy.wait()
        for h in range(2):
            rows = slice(h * 256, h * 256 + 256)
            b.s1[rows, :] = project(
                tok[rows, :], b.got[rows, :], block(2 * r + h, 256), rows, n1oo, n1ot
            )
        for h in range(2):
            tok_y[h].wait()
            tok_yc[h].start()
        for h in range(2):
            rows = slice(h * 256, h * 256 + 256)
            tok_yc[h].wait()
            project(
                b.gyo[rows, :], b.gyt[rows, :], block(2 * (1 - r) + h, 256), rows, n1yo, n1yt
            )
        saves = [
            load(n1oo, o.n1oo, 12),
            load(n1ot, o.n1ot, 13),
            load(n1yo, o.n1yo, 14),
            load(n1yt, o.n1yt, 15),
        ]
        for copy in saves:
            copy.start()
        for e in range(2, 4):
            for copy in moe_copies(e):
                copy.start()

        load_keys([(b.k, k0, k1)])
        vt[...] = b.v[...].astype(f32).T.astype(bf16)
        mix_y, mix_c, mix_yc = [], [], []
        for at in range(4):
            rows = pl.ds(at * 256, 256)
            mix_y.append(
                trade(MIX_Y + at, mixed.at[rows], b.cland_n.at[rows, pl.ds(0, 384)], to_row)
            )
            mix_c.append(
                trade(MIX_C + at, mixed.at[rows], b.cland_n.at[rows, pl.ds(384, 384)], to_col)
            )
            mix_yc.append(
                trade(
                    MIX_YC + at, b.cland_n.at[rows, pl.ds(0, 384)], b.myc.at[rows], to_col
                )
            )

        def attend(at):
            rows = slice(at * 256, at * 256 + 256)
            first = max(at - 2, 0) * 256
            window = slice(first, first + 768)
            bias = key_bias(at, first, b.start[:, rows])
            outs = [None] * 6
            for t in range(3):
                q = b.q[rows, t * 128 : t * 128 + 128] * jnp.asarray(SCALE, bf16)
                for j in range(2):
                    s = dot_nt((k0, k1)[j][window, :], q) + bias
                    top = jnp.max(s, axis=0, keepdims=True)
                    p = jnp.exp(s - top)
                    total = jnp.sum(p, axis=0, keepdims=True)
                    head = t + 3 * j
                    outs[head] = dot_nn(vt[j * 64 : j * 64 + 64, window], p.astype(bf16)) / total
                    b.lse[head : head + 1, rows] = top + jnp.log(total)
            mixed[rows, :] = jnp.concatenate(outs, axis=0).T.astype(bf16)
            mix_y[at].start()
            mix_c[at].start()

        attend(0)
        attend(1)
        for copy in w_gather:
            copy.wait()
        w_yc.start()
        loads = [load(o.wy, wy, 16)]
        loads[0].start()
        attend(2)
        mix_y[0].wait()
        mix_yc[0].start()
        attend(3)
        mix_y[1].wait()
        mix_yc[1].start()

        cot_y.wait()
        cot_yc.start()
        cot_c.wait()
        w_c.wait()
        w_yc.wait()
        loads += [
            load(o.cot_y, b.go.at[far_rows], 17),
            load(o.cot_c, b.gt.at[own_rows], 18),
            load(o.wc, wc, 19),
            load(o.wyc, wyc, 20),
        ]
        for copy in loads[1:]:
            copy.start()
        cot_yc.wait()
        loads.append(load(o.cot_yc, b.gt.at[far_rows], 21))
        loads[-1].start()
        for copy in late + loads:
            copy.wait()
        for at in range(4):
            rows = slice(at * 256, at * 256 + 256)
            b.gf[0:768, rows] = flip_block(b.go[rows, :])
            b.gf[768:1536, rows] = flip_block(b.gt[rows, :])
            if at < 2:
                mix_y[2 + at].wait()
                mix_yc[2 + at].start()

        router_copy.wait()
        for source, target in ((a.router, b.wro), (b.router_far, b.wrt)):
            value = source[...].astype(f32)
            low, high = value[0:MINE], value[MINE:E]
            target[...] = jnp.concatenate(
                [
                    jnp.where(c == 0, low, high),
                    jnp.where(c == 0, high, low),
                    jnp.zeros((128 - E, 768), f32),
                ],
                axis=0,
            ).astype(bf16)

        flat = (768, 768)
        for at in range(4):
            rows = slice(at * 256, at * 256 + 256)
            mix_c[at].wait()
            mix_yc[at].wait()
            here, there = mixed[rows, :], b.cland_n[rows, 384:768]
            near = jnp.concatenate(
                [jnp.where(c == 0, here, there), jnp.where(c == 0, there, here)], axis=1
            )
            here, there = b.cland_n[rows, 0:384], b.myc[rows, :]
            far = jnp.concatenate(
                [jnp.where(c == 0, here, there), jnp.where(c == 0, there, here)], axis=1
            )
            mrow[rows, :] = near
            half = slice((at % 2) * 256, (at % 2) * 256 + 256)
            mine = (at // 2) == r
            x_own = jnp.where(mine, tok[half, :], b.gyo[half, :]).astype(f32)
            x_oth = jnp.where(mine, b.got[half, :], b.gyt[half, :]).astype(f32)
            mid_own = x_own + (
                dot_nt(near, w00[...]) + dot_nt(far, wy[...].reshape(flat))
            )
            mid_oth = x_oth + (dot_nt(near, wc[...]) + dot_nt(far, wyc[...].reshape(flat)))
            total = jnp.sum(mid_own * mid_own, axis=1, keepdims=True) + jnp.sum(
                mid_oth * mid_oth, axis=1, keepdims=True
            )
            s = lax.rsqrt(total / WIDTH + EPS)

            @pl.when(mine)
            def _():
                b.mid[half, :] = mid_own
                b.s2[half, :] = s

            no = (mid_own * s * b.gain_send[1:2, :]).astype(bf16)
            nt = (mid_oth * s * b.gain_far[1:2, :]).astype(bf16)
            b.n2o[rows, :] = no
            b.n2t[rows, :] = nt
            b.n2f[0:768, rows] = flip_block(no)
            b.n2f[768:1536, rows] = flip_block(nt)
            logits = dot_nt(no, b.wro[...]) + dot_nt(nt, b.wrt[...])
            used = b.gate[rows, :]
            top = jnp.max(jnp.where(used > 0.0, logits, NEG), axis=1, keepdims=True)
            weight = jnp.where(used > 0.0, jnp.exp(jnp.minimum(logits - top, 0.0)), 0.0)
            b.gate[rows, :] = weight / jnp.sum(weight, axis=1, keepdims=True)
        saves.append(load(mrow, o.mrow, 22))
        saves[-1].start()
        for copy in saves:
            copy.wait()
        for e in range(4, MINE):
            for copy in moe_copies(e):
                copy.start()

    pl.run_scoped(
        front_scope,
        vb(512, 768),
        vb(768, 768),
        vb(768, 768),
        vb(n, w, 768) if sliced else vb(768, 768),
        vb(n, w, 768) if sliced else vb(768, 768),
        vb(1024, 384),
        vb(1024, 128),
        vb(1024, 128),
        vb(128, 1024),
        vb(512, 768),
        vb(512, 768),
        vb(512, 768),
        vb(512, 768),
        vb(1024, 768),
    )


    n_col = trade(N_COL, b.n2t, b.cland_n, to_col)
    o_col = trade(O_COL, b.gt, o.cland_o, to_col)

    def experts_scope(
        weights, gu_all, hs_all, acc_no, acc_nt, acc_oo, acc_ot, stage_k, stage_s
    ):
        b.weights = weights
        for copy in moe_copies(0):
            copy.wait_recv()
        for copy in weight_loads(0, 0):
            copy.start()
        for total in (acc_no, acc_nt, acc_oo, acc_ot):
            total[...] = jnp.zeros_like(total)
        b.ggs[...] = jnp.zeros_like(b.ggs)

        def stage_copies(e):
            return [load(stage_k, o.keep.at[e], 8), load(stage_s, o.send.at[e], 9)]

        def one(e, carry):
            slot = lax.rem(e, 2)

            @pl.when(e < MINE - 1)
            def _():
                for copy in moe_copies(e + 1):
                    copy.wait_recv()
                for copy in weight_loads(e + 1, 1 - slot):
                    copy.start()

            for copy in weight_loads(e, slot):
                copy.wait()
            wgk, wgr, wuk, wur, wdk, wdr = [b.weights.at[slot, k] for k in range(6)]
            for t in range(2):
                rows = slice(t * 512, t * 512 + 512)
                no, nt = b.n2o[rows, :], b.n2t[rows, :]
                gate_act = dot_nt(no, wgk[...]) + dot_nt(nt, wgr[...])
                up_act = dot_nt(no, wuk[...]) + dot_nt(nt, wur[...])
                grad = dot_nt(b.go[rows, :], wdk[...]) + dot_nt(b.gt[rows, :], wdr[...])
                lane = lax.broadcasted_iota(jnp.int32, (512, 128), 1)
                weight = jnp.sum(
                    jnp.where(lane == e, b.gate[rows, :], 0.0), axis=1, keepdims=True
                )
                s = 1.0 / (1.0 + jnp.exp(-gate_act))
                silu = gate_act * s
                hidden = (silu * up_act).astype(bf16).astype(f32)
                inner = jnp.sum(hidden * grad, axis=1, keepdims=True)
                b.ggs[rows, :] += jnp.where(lane == e, inner, 0.0)
                hs_all[rows, :] = (hidden * weight).astype(bf16)
                grad = grad * weight
                gu_all[rows, 0:256] = (
                    grad * up_act * s * (1.0 + gate_act * (1.0 - s))
                ).astype(bf16)
                gu_all[rows, 256:512] = (grad * silu).astype(bf16)
            for half in range(2):
                rows = slice(half * 768, half * 768 + 768)
                split_shards(
                    dot_nn(b.n2f[rows, :], gu_all[...]),
                    half,
                    slice(0, 512),
                    mx,
                    mz,
                    stage_k,
                    stage_s,
                )
                split_shards(
                    dot_nn(b.gf[rows, :], hs_all[...]),
                    half,
                    slice(512, 768),
                    mx,
                    mz,
                    stage_k,
                    stage_s,
                )
            for copy in stage_copies(e):
                copy.start()
            gu, hs = gu_all[...], hs_all[...]
            acc_no[...] += dot_nn(gu, jnp.concatenate([wgk[...], wuk[...]], axis=0))
            acc_nt[...] += dot_nn(gu, jnp.concatenate([wgr[...], wur[...]], axis=0))
            acc_oo[...] += dot_nn(hs, wdk[...])
            acc_ot[...] += dot_nn(hs, wdr[...])
            for copy in stage_copies(e):
                copy.wait()
            x_copy(e).start()

            @pl.when(e == 4)
            def _():
                pump(0, False)

            @pl.when(e == 6)
            def _():
                pump(1, False)

            return carry

        lax.fori_loop(0, MINE, one, 0)

        b.gg_send[...] = b.ggs[...].T[0:8]
        row_copy = trade(GG_ROW, b.gg_send, b.gg_row, to_row)
        row_copy.start()
        b.n2t[...] = acc_nt[...].astype(bf16)
        n_col.start()
        b.gt[...] = acc_ot[...].astype(bf16)
        o_col.start()
        b.n2o[...] = acc_no[...].astype(bf16)
        b.go[...] = acc_oo[...].astype(bf16)
        row_copy.wait()
        b.gg_sum[...] = b.gg_send[...] + b.gg_row[...]
        col_copy = trade(GG_COL, b.gg_sum, b.gg_col, to_col)
        col_copy.start()
        col_copy.wait()
        gate_grad = jnp.concatenate(
            [b.gg_sum[...], b.gg_col[...], jnp.zeros((112, 1024), f32)], axis=0
        ).T
        weighted = b.gate[...] * gate_grad
        grad_logits = weighted - b.gate[...] * jnp.sum(weighted, axis=1, keepdims=True)
        b.ggs[...] = grad_logits
        split_shards(
            dot_nn(b.n2f[0:768, :], grad_logits.astype(bf16)),
            0,
            slice(768, 896),
            mx,
            mz,
            b.stage_ka,
            b.stage_sa,
        )

    pl.run_scoped(
        experts_scope,
        vb(2, 6, 256, 768),
        vb(1024, 512),
        vb(1024, 256),
        vf(1024, 768),
        vf(1024, 768),
        vf(1024, 768),
        vf(1024, 768),
        vb(nz, 2, w, 768),
        vb(nz, 2, w, 768),
    )


    def rest_scope(
        wmo, wmt, cot, tok, land_c, land_y, k0, k1, v0, v1, kt, sumk0, sumk1, sumv0, sumv1,
        grads, stage_kb, stage_sb, in_stage, kept_a, came_a, sum_a, kept_b, came_b,
        sum_b, far_send, far_here, expert_out, out_out, router_out,
    ):
        b.kept_a, b.came_a, b.sum_a = kept_a, came_a, sum_a
        b.kept_b, b.came_b, b.sum_b = kept_b, came_b, sum_b
        b.far_send, b.far_here, b.expert_out = far_send, far_here, expert_out
        thirds = [(pl.ds(k * 512, 512), pl.ds(0, 768)) for k in range(3)]
        n1oo, n1ot, n1yo = [b.n2f.at[at] for at in thirds]
        n1yt, mro, mry = [b.gf.at[at] for at in thirds]
        early = [load(a.cot, cot, 10), load(a.tok, tok, 11)]
        late = [
            load(o.n1oo, n1oo, 12),
            load(o.n1ot, n1ot, 13),
            load(o.n1yo, n1yo, 14),
            load(o.n1yt, n1yt, 15),
            load(o.mrow.at[own_rows], mro, 16),
            load(o.mrow.at[far_rows], mry, 17),
            load(a.wout.at[:, block(c, 384)], wmo, 18),
            load(o.wc.at[:, block(c, 384)], wmt, 19),
        ]
        for copy in early + late:
            copy.start()

        def norm_back(values, scale, gain, gradient, name, land):
            weighted = gradient * gain
            b.stat[...] = jnp.broadcast_to(
                jnp.sum(weighted * values, axis=1, keepdims=True), (512, 128)
            )
            copy = trade(name, b.stat, land, to_col)
            copy.start()
            gain_grad = jnp.sum(gradient * values * scale, axis=0, keepdims=True)
            copy.wait()
            inner = (b.stat[...] + land[...])[:, 0:1]
            grad = scale * weighted - values * (scale * scale * scale) * (inner / WIDTH)
            return grad, gain_grad

        n_col.wait()
        b.ysend_n[...] = (
            b.n2o[far_rows, :].astype(f32) + b.cland_n[far_rows, :].astype(f32)
        ).astype(bf16)
        y_n = trade(N_ROW, b.ysend_n, b.yland_n, to_row)
        y_n.start()
        gl = b.ggs[own_rows, :]
        gl_high = gl.astype(bf16)
        gl_low = (gl - gl_high.astype(f32)).astype(bf16)
        b.gmid[...] = (
            b.n2o[own_rows, :].astype(f32)
            + b.cland_n[own_rows, :].astype(f32)
            + dot_nn(gl_high, b.wro[...])
            + dot_nn(gl_low, b.wro[...])
        )
        pump(2)
        for copy in early:
            copy.wait()
        y_n.wait()
        grad, gain_grad = norm_back(
            b.mid[...],
            b.s2[...],
            b.gain_send[1:2, :],
            b.gmid[...] + b.yland_n[...].astype(f32),
            STAT_TWO,
            b.stat_two,
        )
        b.gain_part[...] = jnp.zeros_like(b.gain_part)
        b.gain_part[1:2, :] = gain_grad
        b.gmid[...] = cot[...].astype(f32) + grad
        b.goo[...] = b.gmid[...].astype(bf16)
        y_g = trade(G_ROW, b.goo, b.gyo, to_row)
        c_g = trade(G_COL, b.goo, b.got, to_col)
        y_g.start()
        c_g.start()

        o_col.wait()
        run(load(o.cland_o, land_c, 4))
        b.ysend_o[...] = (
            b.go[far_rows, :].astype(f32) + land_c[far_rows, :].astype(f32)
        ).astype(bf16)
        y_o = trade(O_ROW, b.ysend_o, o.yland_o, to_row)
        y_o.start()
        b.mid[...] = (
            b.mid[...] + b.go[own_rows, :].astype(f32) + land_c[own_rows, :].astype(f32)
        )
        pump(3)
        finish(0)

        y_g.wait()
        c_gy = trade(G_ROW_COL, b.gyo, b.gyt, to_col)
        c_gy.start()
        for copy in late:
            copy.wait()
        split_shards(
            dot_tn(mro[...], b.goo[...]) + dot_tn(mry[...], b.gyo[...]),
            0,
            slice(0, 768),
            mx,
            mz,
            b.stage_ka,
            b.stage_sa,
        )
        copies = [load(b.stage_ka, o.keep_a, 4), load(b.stage_sa, o.send_a, 5)]
        for copy in copies:
            copy.start()
        load_keys([(b.k, k0, k1), (b.v, v0, v1)])
        kt[...] = b.k[...].astype(f32).T.astype(bf16)
        for total in (sumk0, sumk1, sumv0, sumv1):
            total[...] = jnp.zeros_like(total)
        for copy in copies:
            copy.wait()
        x_copy(A).start()
        c_g.wait()
        c_gy.wait()
        pump(4)

        def one_block(at, carry):
            near = lax.div(at, 2) == r
            rows = block(lax.rem(at, 2), 256)
            place = block(at, 256)
            g_own = jnp.where(near, b.goo[rows, :], b.gyo[rows, :])
            g_oth = jnp.where(near, b.got[rows, :], b.gyt[rows, :])
            gm = (dot_nn(g_own, wmo[...]) + dot_nn(g_oth, wmt[...])).astype(bf16)
            first = pl.multiple_of(jnp.maximum(at - 2, 0) * 256, 256)
            window = pl.ds(first, 768)
            bias = key_bias(at, first, b.start[:, place])
            parts = [None] * 6
            for t in range(3):
                qt = b.q[place, t * 128 : t * 128 + 128] * jnp.asarray(SCALE, bf16)
                gmt = paired(gm, t)
                for j in range(2):
                    head = t + 3 * j
                    s = dot_nt((k0, k1)[j][window, :], qt) + bias
                    p = jnp.exp(s - b.lse[head : head + 1, place])
                    gp = dot_nt((v0, v1)[j][window, :], gmt)
                    inner = jnp.sum(p * gp, axis=0, keepdims=True)
                    gs = (p * (gp - inner)).astype(bf16)
                    (sumv0, sumv1)[j][window, :] += dot_nn(p.astype(bf16), gmt)
                    (sumk0, sumk1)[j][window, :] += dot_nn(gs, qt)
                    parts[head] = dot_nn(kt[j * 64 : j * 64 + 64, window], gs) * SCALE
            gq = jnp.concatenate(parts, axis=0).T
            cosine, sine = b.cs[place, :], b.sn[place, :]
            for t in range(3):
                grads[place, t * 128 : t * 128 + 128] = rotate(
                    gq[:, t * 128 : t * 128 + 128], cosine, -sine
                ).astype(bf16)
            return carry

        lax.fori_loop(0, 4, one_block, 0)
        lane = lax.broadcasted_iota(jnp.int32, (1024, 128), 1)
        gk = jnp.where(lane < 64, sumk0[...], sumk1[...])
        gv = jnp.where(lane < 64, sumv0[...], sumv1[...])
        grads[:, 384:512] = rotate(gk, b.cs[...], -b.sn[...]).astype(bf16)
        grads[:, 512:640] = gv.astype(bf16)

        b.n2t[...] = dot_nn(grads[...], b.wr[...]).astype(bf16)
        c_p = trade(P_COL, b.n2t, o.cland_p, to_col)
        c_p.start()
        b.n2o[...] = dot_nn(grads[...], b.wk[...]).astype(bf16)
        for part, (left, far) in enumerate(((n1oo, n1yo), (n1ot, n1yt))):
            split_shards(
                dot_tn(left[...], grads[own_rows, :]) + dot_tn(far[...], grads[far_rows, :]),
                part,
                slice(0, 640),
                mx,
                mz,
                stage_kb,
                stage_sb,
            )
        run(load(stage_kb, o.keep_b, 4), load(stage_sb, o.send_b, 5))
        x_copy(B).start()
        c_p.wait()
        run(load(o.cland_p, land_c, 4))
        b.ysend_n[...] = (
            b.n2o[far_rows, :].astype(f32) + land_c[far_rows, :].astype(f32)
        ).astype(bf16)
        y_p = trade(P_ROW, b.ysend_n, o.yland_p, to_row)
        y_p.start()
        pump(5)

        y_o.wait()
        run(load(o.yland_o, land_y, 4))
        land_y[...] = (b.mid[...] + land_y[...].astype(f32)).astype(bf16)
        run(load(land_y, o.output, 7))
        finish(1)
        finish(2)
        y_p.wait()
        run(load(o.yland_p, land_y, 4))
        grad, gain_grad = norm_back(
            tok[...].astype(f32),
            b.s1[...],
            b.gain_send[0:1, :],
            b.n2o[own_rows, :].astype(f32)
            + land_c[own_rows, :].astype(f32)
            + land_y[...].astype(f32),
            STAT_ONE,
            b.stat_one,
        )
        in_stage[...] = b.gmid[...] + grad
        last = load(in_stage, o.input_grad, 7)
        last.start()
        b.gain_part[0:1, :] = gain_grad
        pump(6)

        step = trade(GAIN_ROW, b.gain_part, b.gain_land.at[0], to_row)
        step.start()
        step.wait()
        b.gain_row[...] = b.gain_part[...] + b.gain_land[0]
        step = trade(GAIN_X, b.gain_row, b.gain_land.at[1], to_x)
        step.start()
        step.wait()
        b.gain_x[...] = b.gain_row[...] + b.gain_land[1]
        steps = [
            remote(b.gain_x, b.gain_land.at[1 + s], (b.hsend, b.hrecv), s, to_dp(2 * s))
            for s in range(1, nz)
        ]
        for step in steps:
            step.start()
        total = b.gain_x[...]
        for step in steps:
            step.wait()
        for s in range(1, nz):
            total = total + b.gain_land[1 + s]
        last.wait()
        b.gain_row[...] = total
        run(load(b.gain_row, o.gains, 7))
        finish(3)
        finish_far(0)
        finish_far(1)
        pump(7)
        finish(4)
        finish_far(2)
        pump(A)
        finish(5)
        finish_far(3)
        finish_far(4)
        pump(B)
        finish(6)
        finish_far(5)
        finish(7)
        finish_far(6)
        total = complete(A)[0]
        out_out[...] = total[:, 0:768]
        router_out[...] = total[:, 768:896]
        run(load(out_out, o.grad_out, 4), load(router_out, o.grad_router, 5))
        finish_far(7)
        total = complete(B)
        b.far_b_send[...] = total[1].astype(bf16)
        copy = trade(FAR_B, b.far_b_send, o.far_b, to_col)
        copy.start()

        def put_heads(values, which):
            out_out[:, 0:640] = values
            run(
                load(out_out.at[:, pl.ds(0, 384)], o.grad_query.at[:, block(which, 384)], 4),
                load(out_out.at[:, pl.ds(384, 128)], o.grad_key.at[:, block(which, 128)], 5),
                load(out_out.at[:, pl.ds(512, 128)], o.grad_value.at[:, block(which, 128)], 6),
            )

        put_heads(total[0], c)
        copy.wait()
        run(load(o.far_b, b.far_b_here, 4))
        put_heads(b.far_b_here[...].astype(f32), 1 - c)

        for e in range(MINE):
            for copy in moe_copies(e):
                copy.wait_send()
        for k in list(range(MINE)) + [A, B]:
            x_copy(k).wait_send()
            if (k is A or k is B) or k >= MINE - 2:
                for copy in z_copies(k):
                    copy.wait_send()
        far_copy(6).wait_send()
        far_copy(7).wait_send()

    pl.run_scoped(
        rest_scope,
        *[vb(768, 384)] * 2,
        vb(512, 768),
        vb(512, 768),
        vb(1024, 768),
        vb(512, 768),
        *[vb(1024, 128)] * 4,
        vb(128, 1024),
        *[vf(1024, 128)] * 4,
        vb(1024, 640),
        vb(nz, 2, w, 640),
        vb(nz, 2, w, 640),
        vf(512, 768),
        *[vb(nz, 1, w, 896)] * 3,
        *[vb(nz, 2, w, 640)] * 3,
        vb(2, w, 768),
        vb(w, 768),
        vf(3, w, 256),
        vf(w, 768),
        vf(w, 128),
    )


def hand_over_kernel(gains, router, *refs):
    sources, gain_one, gain_two, router_out = refs[:9], refs[9], refs[10], refs[11]
    targets, places, sems = refs[12:21], refs[21:30], refs[30]
    copies = [
        pltpu.make_async_copy(source, place, sems.at[0, k])
        for k, (source, place) in enumerate(zip(sources, places))
    ]
    for copy in copies:
        copy.start()
    gain_one[...] = gains[0, :]
    gain_two[...] = gains[1, :]
    c, w = lax.axis_index("col"), router.shape[0]
    value = jnp.concatenate([router[...], jnp.zeros((128 - w, 128), f32)], axis=0).T[0:E, 0:w]
    low, high = value[0:MINE], value[MINE:E]
    router_out[...] = jnp.concatenate(
        [jnp.where(c == 0, low, high), jnp.where(c == 0, high, low)], axis=0
    )
    for k in range(9):
        copies[k].wait()
        copies[k] = pltpu.make_async_copy(places[k], targets[k], sems.at[1, k])
        copies[k].start()
    for copy in copies:
        copy.wait()


def local(
    n,
    tokens,
    cotangent,
    gain_one,
    w_query,
    key_weight,
    value_weight,
    w_out,
    gain_two,
    w_router,
    w_gate,
    w_up,
    w_down,
    routes,
    segments,
):
    nz, w = n // 2, 768 // n
    sliced = w % 16 == 0

    def sds(shape, dtype):
        return jax.ShapeDtypeStruct(shape, dtype)

    values = dict(
        tok=tokens,
        cot=cotangent,
        wq=w_query,
        wkey=key_weight,
        wval=value_weight,
        wout=w_out,
        wparts=w_out.reshape(n, w, 768) if sliced else w_out,
        wg=w_gate,
        wu=w_up,
        wd=w_down,
        g1=gain_one,
        g2=gain_two,
        router=w_router,
        routes=routes.T,
        seg=segments,
    )
    shapes = dict(
        output=sds((512, 768), bf16),
        input_grad=sds((512, 768), f32),
        gains=sds((8, 768), f32),
        grad_query=sds((w, 768), f32),
        grad_key=sds((w, 256), f32),
        grad_value=sds((w, 256), f32),
        grad_out=sds((w, 768), f32),
        grad_router=sds((w, 128), f32),
        grad_gate=sds((E, w, 256), f32),
        grad_up=sds((E, w, 256), f32),
        grad_down=sds((E, w, 256), f32),
        far=sds((MINE, w, 768), bf16),
        far_b=sds((w, 640), bf16),
    )
    chunk, chunk_a, chunk_b = (nz, 2, w, 768), (nz, 1, w, 896), (nz, 2, w, 640)
    halves, whole = sds((512, 768), bf16), sds((1024, 768), bf16)
    expert_weight = sds((MINE, 256, 768), bf16)
    parts = sds((n, w, 768) if sliced else (768, 768), bf16)
    shapes.update(
        keep=sds((MINE,) + chunk, bf16),
        send=sds((MINE,) + chunk, bf16),
        xrecv=sds((MINE,) + chunk, bf16),
        zrecv=sds((MINE, nz - 1) + chunk[1:], bf16),
        keep_a=sds(chunk_a, bf16),
        send_a=sds(chunk_a, bf16),
        xrecv_a=sds(chunk_a, bf16),
        zrecv_a=sds((nz - 1,) + chunk_a[1:], bf16),
        keep_b=sds(chunk_b, bf16),
        send_b=sds(chunk_b, bf16),
        xrecv_b=sds(chunk_b, bf16),
        zrecv_b=sds((nz - 1,) + chunk_b[1:], bf16),
        cland_o=whole,
        cland_p=whole,
        yland_o=halves,
        yland_p=halves,
        cot_y=halves,
        cot_c=halves,
        cot_yc=halves,
        n1oo=halves,
        n1ot=halves,
        n1yo=halves,
        n1yt=halves,
        rg=expert_weight,
        ru=expert_weight,
        rd=expert_weight,
        wy=parts,
        wyc=parts,
        wc=sds((768, 768), bf16),
        mrow=whole,
    )

    vb = lambda *shape: pltpu.VMEM(shape, bf16)
    vf = lambda *shape: pltpu.VMEM(shape, f32)
    dma = pltpu.SemaphoreType.DMA
    scratch = dict(
        n2o=vb(1024, 768),
        n2t=vb(1024, 768),
        go=vb(1024, 768),
        gt=vb(1024, 768),
        n2f=vb(1536, 1024),
        gf=vb(1536, 1024),
        q=vb(1024, 384),
        k=vb(1024, 128),
        v=vb(1024, 128),
        lse=vf(8, 1024),
        start=pltpu.VMEM((1, 1024), jnp.int32),
        cs=vf(1024, 128),
        sn=vf(1024, 128),
        wk=vb(640, 768),
        wr=vb(640, 768),
        wro=vb(128, 768),
        wrt=vb(128, 768),
        router_far=vb(E, 768),
        gain_send=vf(8, 768),
        gain_far=vf(8, 768),
        mid=vf(512, 768),
        s1=vf(512, 1),
        s2=vf(512, 1),
        myc=vb(1024, 384),
        gate=vf(1024, 128),
        ggs=vf(1024, 128),
        gg_send=vf(8, 1024),
        gg_row=vf(8, 1024),
        gg_sum=vf(8, 1024),
        gg_col=vf(8, 1024),
        cland_n=vb(1024, 768),
        yland_n=vb(512, 768),
        ysend_n=vb(512, 768),
        ysend_o=vb(512, 768),
        goo=vb(512, 768),
        gyo=vb(512, 768),
        got=vb(512, 768),
        gyt=vb(512, 768),
        gmid=vf(512, 768),
        stat=vf(512, 128),
        stat_one=vf(512, 128),
        stat_two=vf(512, 128),
        gain_part=vf(8, 768),
        gain_row=vf(8, 768),
        gain_x=vf(8, 768),
        gain_land=vf(nz + 1, 8, 768),
        kept=vb(*chunk),
        came=vb(*chunk),
        sums=vb(2, *chunk),
        stage_ka=vb(*chunk_a),
        stage_sa=vb(*chunk_a),
        far_b_send=vb(w, 640),
        far_b_here=vb(w, 640),
        wsem=dma((2, 6)),
        lsem=dma((24,)),
        esend=dma((TRADES,)),
        erecv=dma((TRADES,)),
        msend=dma((3 * MINE,)),
        mrecv=dma((3 * MINE,)),
        gsend=dma((n,)),
        grecv=dma((n,)),
        hsend=dma((nz,)),
        hrecv=dma((nz,)),
        fsend=dma((MINE,)),
        frecv=dma((MINE,)),
        xsend=dma((10,)),
        xarrive=dma((10,)),
        zsend=dma((10 * (nz - 1),)),
        zarrive=dma((10 * (nz - 1),)),
    )
    anywhere, inside = pl.BlockSpec(memory_space=pl.ANY), pl.BlockSpec(memory_space=pltpu.VMEM)
    results = pl.pallas_call(
        functools.partial(layer_kernel, n, tuple(values), tuple(shapes), tuple(scratch)),
        out_shape=tuple(shapes.values()),
        in_specs=[anywhere] * 10 + [inside] * 5,
        out_specs=tuple(anywhere for _ in shapes),
        scratch_shapes=list(scratch.values()),
        compiler_params=pltpu.CompilerParams(
            vmem_limit_bytes=63 * MIB, collective_id=0, has_side_effects=True
        ),
        cost_estimate=pl.CostEstimate(
            flops=80 * 10**9, bytes_accessed=150 * MIB, transcendentals=0
        ),
        name="layer",
    )(*values.values())
    gains, router = results[2], results[7]
    moved = [*results[:2], *results[3:7], *results[8:11]]
    gain = sds((768,), f32)
    done = pl.pallas_call(
        hand_over_kernel,
        out_shape=(gain, gain, sds((E, w), f32)) + tuple(sds(x.shape, x.dtype) for x in moved),
        in_specs=[inside] * 2 + [anywhere] * 9,
        out_specs=(inside,) * 3 + (anywhere,) * 9,
        scratch_shapes=[pltpu.VMEM(x.shape, x.dtype) for x in moved] + [dma((2, 9))],
        compiler_params=pltpu.CompilerParams(vmem_limit_bytes=62 * MIB),
        name="hand_over",
    )(gains, router, *moved)
    gain_one, gain_two, router, output, input_grad = done[:5]
    heads, experts = [x.T for x in done[5:9]], [x.swapaxes(1, 2) for x in done[9:]]
    return output, input_grad, gain_one, *heads, gain_two, router, *experts


def solution(mesh):
    in_specs = (
        P(("dp", "row"), "col"),
        P(("dp", "row"), "col"),
        P("col"),
        P("row", "col"),
        P("row", "col"),
        P("row", "col"),
        P("col", "row"),
        P("col"),
        P(None, "col"),
        P(None, "row", "col"),
        P(None, "row", "col"),
        P(None, "row", "col"),
        P("dp", None),
        P("dp", None),
    )
    out_specs = (
        P(("dp", "row"), "col"),
        P(("dp", "row"), "col"),
        P("col"),
        P("row", ("col", "dp")),
        P("row", ("col", "dp")),
        P("row", ("col", "dp")),
        P("col", ("row", "dp")),
        P("col"),
        P(None, ("col", "dp")),
        P(None, "row", ("col", "dp")),
        P(None, "row", ("col", "dp")),
        P(None, "row", ("col", "dp")),
    )
    return jax.shard_map(
        functools.partial(local, mesh.shape["dp"]),
        mesh=mesh,
        in_specs=in_specs,
        out_specs=out_specs,
        check_vma=False,
    )
```

```python
import functools
import math

import jax
import jax.numpy as jnp
from jax import lax
from jax.experimental import pallas as pl
from jax.experimental.pallas import tpu as pltpu
from jax.sharding import PartitionSpec as P

WIDTH = 1536
HEAD = 64
E = 16
MINE = 8
EPS = 1e-06
SCALE = HEAD ** (-0.5)
NEG = -1e30
f32 = jnp.float32
bf16 = jnp.bfloat16
MIB = 1 << 20
MESH = pl.DeviceIdType.MESH
A, B = object(), object()


def dot_nt(a, b):
    return lax.dot_general(a, b, (((1,), (1,)), ((), ())), preferred_element_type=f32)


def dot_nn(a, b):
    return lax.dot_general(a, b, (((1,), (0,)), ((), ())), preferred_element_type=f32)


def dot_tn(a, b):
    return lax.dot_general(a, b, (((0,), (0,)), ((), ())), preferred_element_type=f32)


def rotate(u, cosine, sine):
    lane = lax.broadcasted_iota(jnp.int32, u.shape, 1)
    turned = jnp.where((lane & 63) < 32, pltpu.roll(u, 96, 1), pltpu.roll(u, 32, 1))
    return u * cosine + turned * sine


def paired(u, t):
    return jnp.concatenate(
        [u[:, t * 64 : t * 64 + 64], u[:, 192 + t * 64 : 192 + t * 64 + 64]], axis=1
    )


def flip_block(values):
    eye = (
        lax.broadcasted_iota(jnp.int32, (256, 256), 0)
        == lax.broadcasted_iota(jnp.int32, (256, 256), 1)
    ).astype(bf16)
    return jnp.concatenate(
        [dot_nt(eye, values[:, i * 256 : i * 256 + 256]) for i in range(3)], axis=0
    ).astype(bf16)


def load_keys(pairs):
    lane = lax.broadcasted_iota(jnp.int32, (1024, 128), 1)
    for source, first, second in pairs:
        value = source[...].astype(f32)
        first[...] = jnp.where(lane < 64, value, 0.0).astype(bf16)
        second[...] = jnp.where(lane < 64, 0.0, value).astype(bf16)


def key_bias(a, first, start):
    key = first + lax.broadcasted_iota(jnp.int32, (768, 256), 0)
    query = a * 256 + lax.broadcasted_iota(jnp.int32, (768, 256), 1)
    return jnp.where((key <= query) & (key >= start), 0.0, NEG)


def position(piece, order):
    places = len(order)
    return sum(((piece >> bit) & 1) << (places - 1 - j) for j, bit in enumerate(order))


def split_shards(values, part, lanes, i, order, stage, other=None, use_other=None):
    w = stage.shape[2]
    for d in range(stage.shape[0]):
        piece = jnp.bitwise_xor(d, i)
        place = position(piece, order)
        if other is not None:
            place = place + use_other * (position(piece, other) - place)
        stage[place, part, :, lanes] = values[d * w : (d + 1) * w].astype(bf16)


(
    TOK_C,
    WQ,
    WK,
    WV,
    GAIN,
    ROUTER,
    COT_Y,
    COT_C,
    COT_YC,
    W_PART,
    W_C,
    W_YC,
    GG_ROW,
    GG_COL,
    N_COL,
    N_ROW,
    O_COL,
    O_ROW,
    STAT_TWO,
    G_ROW,
    G_COL,
    G_ROW_COL,
    P_COL,
    P_ROW,
    STAT_ONE,
    GAIN_ROW,
    GAIN_X,
    FAR_B,
) = range(28)
TOK_Y, TOK_YC, MIX_Y, MIX_C, MIX_YC, TRADES = 28, 30, 32, 36, 40, 44


class Refs:
    def __init__(self, names, refs):
        self.__dict__.update(zip(names, refs))


def layer_kernel(n, inputs, outputs, scratch, *refs):
    nz, w = n // 2, 768 // n
    sliced = w % 16 == 0
    a = Refs(inputs, refs[: len(inputs)])
    refs = refs[len(inputs) :]
    o = Refs(outputs, refs[: len(outputs)])
    b = Refs(scratch, refs[len(outputs) :])
    i, r, c = lax.axis_index("dp"), lax.axis_index("row"), lax.axis_index("col")
    stages = n.bit_length() - 1
    near_first = tuple(range(stages))
    far_first = near_first[1:] + near_first[:1]

    def block(at, size):
        return pl.ds(pl.multiple_of(at * size, size), size)

    own_rows, far_rows = block(r, 512), block(1 - r, 512)
    to_x, to_row, to_col = {"dp": jnp.bitwise_xor(i, 1)}, {"row": 1 - r}, {"col": 1 - c}

    def to_dp(bits):
        return {"dp": jnp.bitwise_xor(i, bits)}

    def remote(src, dst, sems, at, target):
        return pltpu.make_async_remote_copy(
            src_ref=src,
            dst_ref=dst,
            send_sem=sems[0].at[at],
            recv_sem=sems[1].at[at],
            device_id=target,
            device_id_type=MESH,
        )

    def trade(name, src, dst, target):
        return remote(src, dst, (b.esend, b.erecv), name, target)

    def load(src, dst, at):
        return pltpu.make_async_copy(src, dst, b.lsem.at[at])

    def run(*copies):
        for copy in copies:
            copy.start()
        for copy in copies:
            copy.wait()

    vb = lambda *shape: pltpu.VMEM(shape, bf16)
    vf = lambda *shape: pltpu.VMEM(shape, f32)


    def moe_copies(e):
        return [
            remote(src.at[MINE * (1 - c) + e], dst.at[e], (b.msend, b.mrecv), 3 * e + k, to_col)
            for k, (src, dst) in enumerate(((a.wg, o.rg), (a.wu, o.ru), (a.wd, o.rd)))
        ]

    def weight_loads(e, slot):
        pairs = (
            (a.wg, MINE * c + e),
            (o.rg, e),
            (a.wu, MINE * c + e),
            (o.ru, e),
            (a.wd, MINE * c + e),
            (o.rd, e),
        )
        return [
            pltpu.make_async_copy(ref.at[at], b.weights.at[slot, k], b.wsem.at[slot, k])
            for k, (ref, at) in enumerate(pairs)
        ]


    def chunk(k):
        if k is A:
            return o.grad_a, o.land_a, b.sum_a, b.came_a, MINE, near_first
        if k is B:
            return o.grad_b, o.land_b, b.sum_b, b.came_b, MINE + 1, far_first
        if isinstance(k, int) and k == 0:
            return o.grad.at[0], o.land.at[0], b.sums.at[stages], b.came, 0, far_first
        return o.grad.at[k], o.land.at[k], b.sums.at[k % stages], b.came, k, near_first

    def stage(k, j):
        grad, land, total, _, number, order = chunk(k)
        size = n >> (j + 1)
        return remote(
            (grad if j == 0 else total).at[pl.ds(size, size)],
            land.at[pl.ds(n - 2 * size, size)],
            (b.xsend, b.xarrive),
            number * stages + j,
            to_dp(1 << order[j]),
        )

    def begin(k, j):
        stage(k, j).wait_recv()
        grad, land, total, came, _, _ = chunk(k)
        size = n >> (j + 1)
        at = 0 if (k is A or k is B) else n - 2 * size
        loads = [load(land.at[pl.ds(n - 2 * size, size)], came.at[pl.ds(at, size)], 24 + j)]
        if j == 0:
            loads.append(load(grad.at[pl.ds(0, size)], total, 23))
        for copy in loads:
            copy.start()
        return loads

    def end(k, j, loads):
        _, _, total, came, _, _ = chunk(k)
        size = n >> (j + 1)
        at = 0 if (k is A or k is B) else n - 2 * size
        for copy in loads:
            copy.wait()
        if j == stages - 1:
            for earlier in range(1, stages):
                stage(k, earlier).wait_send()
            return total[0].astype(f32) + came[at].astype(f32)
        for piece in range(size - 1, -1, -1):
            total[piece] = (total[piece].astype(f32) + came[at + piece].astype(f32)).astype(bf16)
            if piece == size // 2:
                stage(k, j + 1).start()

    def advance(k, j):
        return end(k, j, begin(k, j))

    def far_copy(k):
        place = k % 2 if k else 2
        return remote(b.far_send.at[place], o.far.at[k], (b.fsend, b.frecv), k, to_col)

    def puts(which, at):
        outs = (o.grad_gate, o.grad_up, o.grad_down)
        return [load(b.expert_out.at[which, m], outs[m].at[at], 32 + 3 * which + m) for m in range(3)]

    def put(which, values, at, wait):
        if wait:
            for copy in puts(which, at):
                copy.wait()
        for m in range(3):
            b.expert_out[which, m] = values[:, m * 256 : m * 256 + 256]
        for copy in puts(which, at):
            copy.start()

    def finish(q, total):
        if q > 2:
            far_copy(q - 2).wait_send()
        b.far_send[q % 2 if q else 2] = total[1].astype(bf16)
        far_copy(q).start()
        put(0, total[0], MINE * c + q, q != 1)

    def begin_far(q):
        far_copy(q).wait_recv()
        copy = load(o.far.at[q], b.far_here, 22)
        copy.start()
        return copy

    def end_far(q, copy):
        copy.wait()
        put(1, b.far_here[...].astype(f32), MINE * (1 - c) + q, q != 1)

    def tick(k):
        jobs = [(k - j, j) for j in range(stages) if 1 <= k - j < MINE]
        loads = [begin(*job) for job in jobs]
        far = k - stages
        far_load = begin_far(far) if 1 <= far < MINE else None
        for (q, j), copies in zip(jobs, loads):
            total = end(q, j, copies)
            if j == stages - 1:
                finish(q, total)
        if far_load is not None:
            end_far(far, far_load)


    tok_y = [
        trade(TOK_Y + h, a.tok.at[pl.ds(h * 256, 256)], b.gyo.at[pl.ds(h * 256, 256)], to_row)
        for h in range(2)
    ]
    tok_yc = [
        trade(TOK_YC + h, b.gyo.at[pl.ds(h * 256, 256)], b.gyt.at[pl.ds(h * 256, 256)], to_col)
        for h in range(2)
    ]
    tok_c = trade(TOK_C, a.tok, b.got, to_col)
    heads = [
        trade(WQ, a.wq.at[block(1 - c, 384)], b.wr.at[pl.ds(0, 384)], to_col),
        trade(WK, a.wkey.at[block(1 - c, 128)], b.wr.at[pl.ds(384, 128)], to_col),
        trade(WV, a.wval.at[block(1 - c, 128)], b.wr.at[pl.ds(512, 128)], to_col),
    ]
    gain_copy = trade(GAIN, b.gain_send, b.gain_far, to_col)
    router_copy = trade(ROUTER, a.router, b.router_far, to_col)
    cot_y = trade(COT_Y, a.cot, o.cot_y, to_row)
    cot_c = trade(COT_C, a.cot, o.cot_c, to_col)
    cot_yc = trade(COT_YC, o.cot_y, o.cot_yc, to_col)
    w_part = trade(
        W_PART,
        a.wparts.at[i] if sliced else a.wout,
        o.wy.at[i] if sliced else o.wy,
        to_row,
    )
    w_gather = [
        remote(o.wy.at[i], o.wy.at[i], (b.gsend, b.grecv), bits, to_dp(bits))
        for bits in (range(1, n) if sliced else ())
    ]
    w_c = trade(W_C, a.wout, o.wc, to_col)
    w_yc = trade(W_YC, o.wy, o.wyc, to_col)

    def front_scope(
        tok, w00, wc, wy, wyc, mixed, k0, k1, vt, n1oo, n1ot, n1yo, n1yt, mrow
    ):
        locals_ = [
            load(a.tok, tok, 0),
            load(a.wq.at[block(c, 384)], b.wk.at[pl.ds(0, 384)], 1),
            load(a.wkey.at[block(c, 128)], b.wk.at[pl.ds(384, 128)], 2),
            load(a.wval.at[block(c, 128)], b.wk.at[pl.ds(512, 128)], 3),
        ]
        late = [
            load(a.wout, w00, 10),
            load(a.cot, b.go.at[own_rows], 11),
        ]
        for copy in locals_ + late:
            copy.start()
        b.gain_send[...] = jnp.zeros_like(b.gain_send)
        b.gain_send[0:1, :] = a.g1[...].reshape(1, 768)
        b.gain_send[1:2, :] = a.g2[...].reshape(1, 768)
        barrier = pltpu.get_barrier_semaphore()
        partners = [to_row, to_col] + [to_dp(bits) for bits in range(1, n)]
        for target in partners:
            pl.semaphore_signal(barrier, inc=1, device_id=target, device_id_type=MESH)
        pl.semaphore_wait(barrier, len(partners))
        for copy in [w_part] + tok_y + [tok_c] + heads + [gain_copy, router_copy, cot_y, cot_c, w_c]:
            copy.start()
        for e in range(2):
            for copy in moe_copies(e):
                copy.start()

        w_part.wait()
        for copy in w_gather:
            copy.start()

        seg = a.seg[...].astype(f32)
        seg_column = jnp.broadcast_to(seg, (8, 1024)).T[:, 0:1]
        start, start_column = jnp.zeros_like(seg), jnp.zeros_like(seg_column)
        for number in range(1, 4):
            count = jnp.sum(jnp.where(seg < number, 1.0, 0.0), axis=1, keepdims=True)
            start = jnp.where(seg == number, count, start)
            start_column = jnp.where(seg_column == number, count, start_column)
        b.start[...] = start.astype(jnp.int32)
        lane = lax.broadcasted_iota(jnp.int32, (1024, 128), 1)
        place = lax.broadcasted_iota(jnp.int32, (1024, 128), 0).astype(f32)
        frequency = jnp.exp((lane & 31).astype(f32) * (-2.0 * math.log(10000.0) / HEAD))
        angles = (place - start_column) * frequency
        b.cs[...] = jnp.cos(angles)
        sine = jnp.sin(angles)
        b.sn[...] = jnp.where((lane & 63) < 32, -sine, sine)

        number = jnp.where(lane < MINE, lane + MINE * c, lane - MINE * c)
        number = jnp.where((lane >= MINE) & (c == 1), lane - MINE, number)
        number = jnp.where(lane < E, number, -1)
        used = jnp.zeros((1024, 128), f32)
        routes, number = a.routes[...].astype(f32).T, number.astype(f32)
        for k in range(8):
            used = jnp.where(routes[:, k : k + 1] == number, 1.0, used)
        b.gate[...] = used

        gain_copy.wait()

        def project(x_own, x_oth, place, rows, n_own, n_oth):
            u, v = x_own.astype(f32), x_oth.astype(f32)
            total = jnp.sum(u * u, axis=1, keepdims=True) + jnp.sum(v * v, axis=1, keepdims=True)
            s = lax.rsqrt(total / WIDTH + EPS)
            u = (u * s * b.gain_send[0:1, :]).astype(bf16)
            v = (v * s * b.gain_far[0:1, :]).astype(bf16)
            n_own[rows, :] = u
            n_oth[rows, :] = v
            raw = dot_nt(u, b.wk[...]) + dot_nt(v, b.wr[...])
            cs, sn = b.cs[place, :], b.sn[place, :]
            for t in range(3):
                b.q[place, t * 128 : t * 128 + 128] = rotate(paired(raw, t), cs, sn).astype(bf16)
            b.k[place, :] = rotate(raw[:, 384:512], cs, sn).astype(bf16)
            b.v[place, :] = raw[:, 512:640].astype(bf16)
            return s

        for copy in locals_ + [tok_c] + heads:
            copy.wait()
        for h in range(2):
            rows = slice(h * 256, h * 256 + 256)
            b.s1[rows, :] = project(
                tok[rows, :], b.got[rows, :], block(2 * r + h, 256), rows, n1oo, n1ot
            )
        for h in range(2):
            tok_y[h].wait()
            tok_yc[h].start()
        for h in range(2):
            rows = slice(h * 256, h * 256 + 256)
            tok_yc[h].wait()
            project(
                b.gyo[rows, :], b.gyt[rows, :], block(2 * (1 - r) + h, 256), rows, n1yo, n1yt
            )
        saves = [
            load(n1oo, o.n1oo, 12),
            load(n1ot, o.n1ot, 13),
            load(n1yo, o.n1yo, 14),
            load(n1yt, o.n1yt, 15),
        ]
        for copy in saves:
            copy.start()
        for e in range(2, 4):
            for copy in moe_copies(e):
                copy.start()

        load_keys([(b.k, k0, k1)])
        vt[...] = b.v[...].astype(f32).T.astype(bf16)
        mix_y, mix_c, mix_yc = [], [], []
        for at in range(4):
            rows = pl.ds(at * 256, 256)
            mix_y.append(
                trade(MIX_Y + at, mixed.at[rows], b.cland_n.at[rows, pl.ds(0, 384)], to_row)
            )
            mix_c.append(
                trade(MIX_C + at, mixed.at[rows], b.cland_n.at[rows, pl.ds(384, 384)], to_col)
            )
            mix_yc.append(
                trade(
                    MIX_YC + at, b.cland_n.at[rows, pl.ds(0, 384)], b.myc.at[rows], to_col
                )
            )

        def attend(at):
            rows = slice(at * 256, at * 256 + 256)
            first = max(at - 2, 0) * 256
            window = slice(first, first + 768)
            bias = key_bias(at, first, b.start[:, rows])
            outs = [None] * 6
            for t in range(3):
                q = b.q[rows, t * 128 : t * 128 + 128] * jnp.asarray(SCALE, bf16)
                for j in range(2):
                    s = dot_nt((k0, k1)[j][window, :], q) + bias
                    top = jnp.max(s, axis=0, keepdims=True)
                    p = jnp.exp(s - top)
                    total = jnp.sum(p, axis=0, keepdims=True)
                    head = t + 3 * j
                    outs[head] = dot_nn(vt[j * 64 : j * 64 + 64, window], p.astype(bf16)) / total
                    b.lse[head : head + 1, rows] = top + jnp.log(total)
            mixed[rows, :] = jnp.concatenate(outs, axis=0).T.astype(bf16)
            mix_y[at].start()
            mix_c[at].start()

        attend(0)
        attend(1)
        for copy in w_gather:
            copy.wait()
        w_yc.start()
        loads = [load(o.wy, wy, 16)]
        loads[0].start()
        attend(2)
        attend(3)

        cot_y.wait()
        cot_yc.start()
        cot_c.wait()
        w_c.wait()
        w_yc.wait()
        loads += [
            load(o.cot_y, b.go.at[far_rows], 17),
            load(o.cot_c, b.gt.at[own_rows], 18),
            load(o.wc, wc, 19),
            load(o.wyc, wyc, 20),
        ]
        for copy in loads[1:]:
            copy.start()
        mix_y[0].wait()
        mix_yc[0].start()
        cot_yc.wait()
        loads.append(load(o.cot_yc, b.gt.at[far_rows], 21))
        loads[-1].start()
        for copy in late + loads:
            copy.wait()
        for at in range(4):
            rows = slice(at * 256, at * 256 + 256)
            b.gf[0:768, rows] = flip_block(b.go[rows, :])
            b.gf[768:1536, rows] = flip_block(b.gt[rows, :])

        router_copy.wait()
        for source, target in ((a.router, b.wro), (b.router_far, b.wrt)):
            value = source[...].astype(f32)
            low, high = value[0:MINE], value[MINE:E]
            target[...] = jnp.concatenate(
                [
                    jnp.where(c == 0, low, high),
                    jnp.where(c == 0, high, low),
                    jnp.zeros((128 - E, 768), f32),
                ],
                axis=0,
            ).astype(bf16)

        flat = (768, 768)
        for at in range(4):
            rows = slice(at * 256, at * 256 + 256)
            mix_c[at].wait()
            mix_yc[at].wait()
            here, there = mixed[rows, :], b.cland_n[rows, 384:768]
            near = jnp.concatenate(
                [jnp.where(c == 0, here, there), jnp.where(c == 0, there, here)], axis=1
            )
            here, there = b.cland_n[rows, 0:384], b.myc[rows, :]
            far = jnp.concatenate(
                [jnp.where(c == 0, here, there), jnp.where(c == 0, there, here)], axis=1
            )
            mrow[rows, :] = near
            half = slice((at % 2) * 256, (at % 2) * 256 + 256)
            mine = (at // 2) == r
            x_own = jnp.where(mine, tok[half, :], b.gyo[half, :]).astype(f32)
            x_oth = jnp.where(mine, b.got[half, :], b.gyt[half, :]).astype(f32)
            mid_own = x_own + (
                dot_nt(near, w00[...]) + dot_nt(far, wy[...].reshape(flat))
            )
            if at < 3:
                mix_y[at + 1].wait()
                mix_yc[at + 1].start()
            mid_oth = x_oth + (dot_nt(near, wc[...]) + dot_nt(far, wyc[...].reshape(flat)))
            total = jnp.sum(mid_own * mid_own, axis=1, keepdims=True) + jnp.sum(
                mid_oth * mid_oth, axis=1, keepdims=True
            )
            s = lax.rsqrt(total / WIDTH + EPS)

            @pl.when(mine)
            def _():
                b.mid[half, :] = mid_own
                b.s2[half, :] = s

            no = (mid_own * s * b.gain_send[1:2, :]).astype(bf16)
            nt = (mid_oth * s * b.gain_far[1:2, :]).astype(bf16)
            b.n2o[rows, :] = no
            b.n2t[rows, :] = nt
            b.n2f[0:768, rows] = flip_block(no)
            b.n2f[768:1536, rows] = flip_block(nt)
            logits = dot_nt(no, b.wro[...]) + dot_nt(nt, b.wrt[...])
            used = b.gate[rows, :]
            top = jnp.max(jnp.where(used > 0.0, logits, NEG), axis=1, keepdims=True)
            weight = jnp.where(used > 0.0, jnp.exp(jnp.minimum(logits - top, 0.0)), 0.0)
            b.gate[rows, :] = weight / jnp.sum(weight, axis=1, keepdims=True)
        saves.append(load(mrow, o.mrow, 22))
        saves[-1].start()
        for copy in saves:
            copy.wait()
        for e in range(4, MINE):
            for copy in moe_copies(e):
                copy.start()

    pl.run_scoped(
        front_scope,
        vb(512, 768),
        vb(768, 768),
        vb(768, 768),
        vb(n, w, 768) if sliced else vb(768, 768),
        vb(n, w, 768) if sliced else vb(768, 768),
        vb(1024, 384),
        vb(1024, 128),
        vb(1024, 128),
        vb(128, 1024),
        vb(512, 768),
        vb(512, 768),
        vb(512, 768),
        vb(512, 768),
        vb(1024, 768),
    )


    n_col = trade(N_COL, b.n2t, b.cland_n, to_col)
    o_col = trade(O_COL, b.gt, o.cland_o, to_col)

    def experts_scope(
        weights, gu_all, hs_all, acc_no, acc_nt, acc_oo, acc_ot, shards
    ):
        b.weights = weights
        for copy in moe_copies(0):
            copy.wait_recv()
        for copy in weight_loads(0, 0):
            copy.start()
        b.ggs[...] = jnp.zeros_like(b.ggs)

        def one(e, carry):
            slot = lax.rem(e, 2)

            @pl.when(e < MINE - 1)
            def _():
                for copy in moe_copies(e + 1):
                    copy.wait_recv()
                for copy in weight_loads(e + 1, 1 - slot):
                    copy.start()

            for copy in weight_loads(e, slot):
                copy.wait()
            wgk, wgr, wuk, wur, wdk, wdr = [b.weights.at[slot, k] for k in range(6)]
            for t in range(2):
                rows = slice(t * 512, t * 512 + 512)
                no, nt = b.n2o[rows, :], b.n2t[rows, :]
                gate_act = dot_nt(no, wgk[...]) + dot_nt(nt, wgr[...])
                up_act = dot_nt(no, wuk[...]) + dot_nt(nt, wur[...])
                grad = dot_nt(b.go[rows, :], wdk[...]) + dot_nt(b.gt[rows, :], wdr[...])
                lane = lax.broadcasted_iota(jnp.int32, (512, 128), 1)
                weight = jnp.sum(
                    jnp.where(lane == e, b.gate[rows, :], 0.0), axis=1, keepdims=True
                )
                s = 1.0 / (1.0 + jnp.exp(-gate_act))
                silu = gate_act * s
                hidden = (silu * up_act).astype(bf16).astype(f32)
                inner = jnp.sum(hidden * grad, axis=1, keepdims=True)
                b.ggs[rows, :] += jnp.where(lane == e, inner, 0.0)
                hs_all[rows, :] = (hidden * weight).astype(bf16)
                grad = grad * weight
                gu_all[rows, 0:256] = (
                    grad * up_act * s * (1.0 + gate_act * (1.0 - s))
                ).astype(bf16)
                gu_all[rows, 256:512] = (grad * silu).astype(bf16)
            first = 1 - lax.div(e + MINE - 1, MINE)
            for half in range(2):
                rows = slice(half * 768, half * 768 + 768)
                gates = dot_nn(b.n2f[rows, :], gu_all[...])
                split_shards(gates, half, slice(0, 512), i, near_first, shards, far_first, first)
                downs = dot_nn(b.gf[rows, :], hs_all[...])
                split_shards(downs, half, slice(512, 768), i, near_first, shards, far_first, first)
            save = load(shards, o.grad.at[e], 8)
            save.start()

            @pl.when(e == 0)
            def _():
                save.wait()
                stage(0, 0).start()
                for total in (acc_no, acc_nt, acc_oo, acc_ot):
                    total[...] = jnp.zeros_like(total)

            gu, hs = gu_all[...], hs_all[...]
            acc_no[...] += dot_nn(gu, jnp.concatenate([wgk[...], wuk[...]], axis=0))
            acc_nt[...] += dot_nn(gu, jnp.concatenate([wgr[...], wur[...]], axis=0))
            acc_oo[...] += dot_nn(hs, wdk[...])
            acc_ot[...] += dot_nn(hs, wdr[...])

            @pl.when(e > 0)
            def _():
                save.wait()
                stage(e, 0).start()

            @pl.when(e == 4)
            def _():
                advance(0, 0)

            @pl.when(e == 5)
            def _():
                tick(1)

            @pl.when(e == 7)
            def _():
                advance(0, 1)

            return carry

        lax.fori_loop(0, MINE, one, 0)

        b.gg_send[...] = b.ggs[...].T[0:8]
        row_copy = trade(GG_ROW, b.gg_send, b.gg_row, to_row)
        row_copy.start()
        b.n2t[...] = acc_nt[...].astype(bf16)
        n_col.start()
        b.gt[...] = acc_ot[...].astype(bf16)
        o_col.start()
        b.n2o[...] = acc_no[...].astype(bf16)
        b.go[...] = acc_oo[...].astype(bf16)
        row_copy.wait()
        b.gg_sum[...] = b.gg_send[...] + b.gg_row[...]
        col_copy = trade(GG_COL, b.gg_sum, b.gg_col, to_col)
        col_copy.start()
        col_copy.wait()
        gate_grad = jnp.concatenate(
            [b.gg_sum[...], b.gg_col[...], jnp.zeros((112, 1024), f32)], axis=0
        ).T
        weighted = b.gate[...] * gate_grad
        grad_logits = weighted - b.gate[...] * jnp.sum(weighted, axis=1, keepdims=True)
        b.ggs[...] = grad_logits
        routers = dot_nn(b.n2f[0:768, :], grad_logits.astype(bf16))
        split_shards(routers, 0, slice(768, 896), i, near_first, b.shards_a)

    pl.run_scoped(
        experts_scope,
        vb(2, 6, 256, 768),
        vb(1024, 512),
        vb(1024, 256),
        vf(1024, 768),
        vf(1024, 768),
        vf(1024, 768),
        vf(1024, 768),
        vb(n, 2, w, 768),
    )


    def rest_scope(
        wmo, wmt, cot, tok, land_y, k0, k1, v0, v1, kt, sumk0, sumk1, sumv0, sumv1,
        grads, shards_b, in_stage, came_a, sum_a, came_b, sum_b, far_send, far_here, expert_out,
        out_out, router_out,
    ):
        b.came_a, b.sum_a, b.came_b, b.sum_b = came_a, sum_a, came_b, sum_b
        b.far_send, b.far_here, b.expert_out = far_send, far_here, expert_out
        thirds = [(pl.ds(k * 512, 512), pl.ds(0, 768)) for k in range(3)]
        n1oo, n1ot, n1yo = [b.n2f.at[at] for at in thirds]
        n1yt, mro, mry = [b.gf.at[at] for at in thirds]
        early = [load(a.cot, cot, 10), load(a.tok, tok, 11)]
        late = [
            load(o.n1oo, n1oo, 12),
            load(o.n1ot, n1ot, 13),
            load(o.n1yo, n1yo, 14),
            load(o.n1yt, n1yt, 15),
            load(o.mrow.at[own_rows], mro, 16),
            load(o.mrow.at[far_rows], mry, 17),
            load(a.wout.at[:, block(c, 384)], wmo, 18),
            load(o.wc.at[:, block(c, 384)], wmt, 19),
        ]
        for copy in early + late:
            copy.start()

        def norm_back(values, scale, gain, gradient, name, land):
            weighted = gradient * gain
            b.stat[...] = jnp.broadcast_to(
                jnp.sum(weighted * values, axis=1, keepdims=True), (512, 128)
            )
            copy = trade(name, b.stat, land, to_col)
            copy.start()
            gain_grad = jnp.sum(gradient * values * scale, axis=0, keepdims=True)
            copy.wait()
            inner = (b.stat[...] + land[...])[:, 0:1]
            grad = scale * weighted - values * (scale * scale * scale) * (inner / WIDTH)
            return grad, gain_grad

        n_col.wait()
        b.ysend_n[...] = (
            b.n2o[far_rows, :].astype(f32) + b.cland_n[far_rows, :].astype(f32)
        ).astype(bf16)
        y_n = trade(N_ROW, b.ysend_n, b.yland_n, to_row)
        y_n.start()
        gl = b.ggs[own_rows, :]
        gl_high = gl.astype(bf16)
        gl_low = (gl - gl_high.astype(f32)).astype(bf16)
        b.gmid[...] = (
            b.n2o[own_rows, :].astype(f32)
            + b.cland_n[own_rows, :].astype(f32)
            + dot_nn(gl_high, b.wro[...])
            + dot_nn(gl_low, b.wro[...])
        )
        tick(2)
        for copy in early:
            copy.wait()
        y_n.wait()
        grad, gain_grad = norm_back(
            b.mid[...],
            b.s2[...],
            b.gain_send[1:2, :],
            b.gmid[...] + b.yland_n[...].astype(f32),
            STAT_TWO,
            b.stat_land,
        )
        b.gain_part[...] = jnp.zeros_like(b.gain_part)
        b.gain_part[1:2, :] = gain_grad
        b.gmid[...] = cot[...].astype(f32) + grad
        b.goo[...] = b.gmid[...].astype(bf16)
        y_g = trade(G_ROW, b.goo, b.gyo, to_row)
        c_g = trade(G_COL, b.goo, b.got, to_col)
        y_g.start()
        c_g.start()

        o_col.wait()
        run(load(o.cland_o, b.gt, 4))
        b.ysend_o[...] = (
            b.go[far_rows, :].astype(f32) + b.gt[far_rows, :].astype(f32)
        ).astype(bf16)
        y_o = trade(O_ROW, b.ysend_o, o.yland_o, to_row)
        y_o.start()
        b.mid[...] = (
            b.mid[...] + b.go[own_rows, :].astype(f32) + b.gt[own_rows, :].astype(f32)
        )
        tick(3)

        y_g.wait()
        c_gy = trade(G_ROW_COL, b.gyo, b.gyt, to_col)
        c_gy.start()
        for copy in late:
            copy.wait()
        outs = dot_tn(mro[...], b.goo[...]) + dot_tn(mry[...], b.gyo[...])
        split_shards(outs, 0, slice(0, 768), i, near_first, b.shards_a)
        save = load(b.shards_a, o.grad_a, 4)
        save.start()
        load_keys([(b.k, k0, k1), (b.v, v0, v1)])
        kt[...] = b.k[...].astype(f32).T.astype(bf16)
        for total in (sumk0, sumk1, sumv0, sumv1):
            total[...] = jnp.zeros_like(total)
        save.wait()
        stage(A, 0).start()
        c_g.wait()
        c_gy.wait()

        def one_block(at, carry):
            near = lax.div(at, 2) == r
            rows = block(lax.rem(at, 2), 256)
            place = block(at, 256)
            g_own = jnp.where(near, b.goo[rows, :], b.gyo[rows, :])
            g_oth = jnp.where(near, b.got[rows, :], b.gyt[rows, :])
            gm = (dot_nn(g_own, wmo[...]) + dot_nn(g_oth, wmt[...])).astype(bf16)
            first = pl.multiple_of(jnp.maximum(at - 2, 0) * 256, 256)
            window = pl.ds(first, 768)
            bias = key_bias(at, first, b.start[:, place])
            parts = [None] * 6
            for t in range(3):
                qt = b.q[place, t * 128 : t * 128 + 128] * jnp.asarray(SCALE, bf16)
                gmt = paired(gm, t)
                for j in range(2):
                    head = t + 3 * j
                    s = dot_nt((k0, k1)[j][window, :], qt) + bias
                    p = jnp.exp(s - b.lse[head : head + 1, place])
                    gp = dot_nt((v0, v1)[j][window, :], gmt)
                    inner = jnp.sum(p * gp, axis=0, keepdims=True)
                    gs = (p * (gp - inner)).astype(bf16)
                    (sumv0, sumv1)[j][window, :] += dot_nn(p.astype(bf16), gmt)
                    (sumk0, sumk1)[j][window, :] += dot_nn(gs, qt)
                    parts[head] = dot_nn(kt[j * 64 : j * 64 + 64, window], gs) * SCALE
            gq = jnp.concatenate(parts, axis=0).T
            cosine, sine = b.cs[place, :], b.sn[place, :]
            for t in range(3):
                grads[place, t * 128 : t * 128 + 128] = rotate(
                    gq[:, t * 128 : t * 128 + 128], cosine, -sine
                ).astype(bf16)
            return carry

        lax.fori_loop(0, 2, one_block, 0)
        tick(4)
        lax.fori_loop(2, 4, one_block, 0)
        tick(5)
        lane = lax.broadcasted_iota(jnp.int32, (1024, 128), 1)
        gk = jnp.where(lane < 64, sumk0[...], sumk1[...])
        gv = jnp.where(lane < 64, sumv0[...], sumv1[...])
        grads[:, 384:512] = rotate(gk, b.cs[...], -b.sn[...]).astype(bf16)
        grads[:, 512:640] = gv.astype(bf16)

        b.n2t[...] = dot_nn(grads[...], b.wr[...]).astype(bf16)
        c_p = trade(P_COL, b.n2t, o.cland_p, to_col)
        c_p.start()
        b.n2o[...] = dot_nn(grads[...], b.wk[...]).astype(bf16)
        for part, (left, far) in enumerate(((n1oo, n1yo), (n1ot, n1yt))):
            heads_grad = dot_tn(left[...], grads[own_rows, :]) + dot_tn(
                far[...], grads[far_rows, :]
            )
            split_shards(heads_grad, part, slice(0, 640), i, far_first, shards_b)
        run(load(shards_b, o.grad_b, 4))
        stage(B, 0).start()
        c_p.wait()
        run(load(o.cland_p, b.gt, 4))
        b.ysend_n[...] = (
            b.n2o[far_rows, :].astype(f32) + b.gt[far_rows, :].astype(f32)
        ).astype(bf16)
        y_p = trade(P_ROW, b.ysend_n, o.yland_p, to_row)
        y_p.start()
        tick(6)

        y_o.wait()
        run(load(o.yland_o, land_y, 4))
        land_y[...] = (b.mid[...] + land_y[...].astype(f32)).astype(bf16)
        run(load(land_y, o.output, 7))
        y_p.wait()
        run(load(o.yland_p, land_y, 4))
        grad, gain_grad = norm_back(
            tok[...].astype(f32),
            b.s1[...],
            b.gain_send[0:1, :],
            b.n2o[own_rows, :].astype(f32)
            + b.gt[own_rows, :].astype(f32)
            + land_y[...].astype(f32),
            STAT_ONE,
            b.stat_land,
        )
        in_stage[...] = b.gmid[...] + grad
        last = load(in_stage, o.input_grad, 7)
        last.start()
        b.gain_part[0:1, :] = gain_grad
        advance(B, 0)

        step = trade(GAIN_ROW, b.gain_part, b.gain_land.at[0], to_row)
        step.start()
        step.wait()
        b.gain_row[...] = b.gain_part[...] + b.gain_land[0]
        step = trade(GAIN_X, b.gain_row, b.gain_land.at[1], to_x)
        step.start()
        step.wait()
        b.gain_x[...] = b.gain_row[...] + b.gain_land[1]
        steps = [
            remote(b.gain_x, b.gain_land.at[1 + s], (b.hsend, b.hrecv), s, to_dp(2 * s))
            for s in range(1, nz)
        ]
        for step in steps:
            step.start()
        total = b.gain_x[...]
        for step in steps:
            step.wait()
        for s in range(1, nz):
            total = total + b.gain_land[1 + s]
        last.wait()
        b.gain_row[...] = total
        run(load(b.gain_row, o.gains, 7))
        tick(7)
        finish(0, advance(0, stages - 1))
        for j in range(1, stages - 1):
            advance(B, j)
        advance(A, 0)
        total = advance(B, stages - 1)
        b.far_b_send[...] = total[1].astype(bf16)
        copy = trade(FAR_B, b.far_b_send, o.far_b, to_col)
        copy.start()

        def put_heads(values, which, wait):
            copies = [
                load(out_out.at[:, pl.ds(0, 384)], o.grad_query.at[:, block(which, 384)], 4),
                load(out_out.at[:, pl.ds(384, 128)], o.grad_key.at[:, block(which, 128)], 5),
                load(out_out.at[:, pl.ds(512, 128)], o.grad_value.at[:, block(which, 128)], 6),
            ]
            if wait:
                for copy in copies:
                    copy.wait()
            out_out[:, 0:640] = values
            for copy in copies:
                copy.start()
            return copies

        put_heads(total[0], c, False)
        tick(8)
        copy.wait()
        run(load(o.far_b, b.far_b_here, 21))
        heads_last = put_heads(b.far_b_here[...].astype(f32), 1 - c, True)
        end_far(0, begin_far(0))
        for j in range(1, stages - 1):
            advance(A, j)
        tick(9)
        total = advance(A, stages - 1)[0]
        for copy in heads_last:
            copy.wait()
        out_out[...] = total[:, 0:768]
        router_out[...] = total[:, 768:896]
        lasts = [load(out_out, o.grad_out, 4), load(router_out, o.grad_router, 5)]
        for copy in lasts:
            copy.start()
        for k in range(10, MINE + stages):
            tick(k)
        for copy in lasts:
            copy.wait()

        for e in range(MINE):
            for copy in moe_copies(e):
                copy.wait_send()
        for k in list(range(MINE)) + [A, B]:
            stage(k, 0).wait_send()
        far_copy(0).wait_send()
        far_copy(MINE - 2).wait_send()
        far_copy(MINE - 1).wait_send()
        for which in range(2):
            for copy in puts(which, 0):
                copy.wait()

    pl.run_scoped(
        rest_scope,
        *[vb(768, 384)] * 2,
        vb(512, 768),
        vb(512, 768),
        vb(512, 768),
        *[vb(1024, 128)] * 4,
        vb(128, 1024),
        *[vf(1024, 128)] * 4,
        vb(1024, 640),
        vb(n, 2, w, 640),
        vf(512, 768),
        *[vb(nz, 1, w, 896)] * 2,
        *[vb(nz, 2, w, 640)] * 2,
        vb(3, w, 768),
        vb(w, 768),
        vf(2, 3, w, 256),
        vf(w, 768),
        vf(w, 128),
    )


def hand_over_kernel(gains, router, *refs):
    sources, gain_one, gain_two, router_out = refs[:9], refs[9], refs[10], refs[11]
    targets, places, sems = refs[12:21], refs[21:30], refs[30]
    copies = [
        pltpu.make_async_copy(source, place, sems.at[0, k])
        for k, (source, place) in enumerate(zip(sources, places))
    ]
    for copy in copies:
        copy.start()
    gain_one[...] = gains[0, :]
    gain_two[...] = gains[1, :]
    c, w = lax.axis_index("col"), router.shape[0]
    value = jnp.concatenate([router[...], jnp.zeros((128 - w, 128), f32)], axis=0).T[0:E, 0:w]
    low, high = value[0:MINE], value[MINE:E]
    router_out[...] = jnp.concatenate(
        [jnp.where(c == 0, low, high), jnp.where(c == 0, high, low)], axis=0
    )
    for k in range(9):
        copies[k].wait()
        copies[k] = pltpu.make_async_copy(places[k], targets[k], sems.at[1, k])
        copies[k].start()
    for copy in copies:
        copy.wait()


def local(
    n,
    tokens,
    cotangent,
    gain_one,
    w_query,
    key_weight,
    value_weight,
    w_out,
    gain_two,
    w_router,
    w_gate,
    w_up,
    w_down,
    routes,
    segments,
):
    nz, w = n // 2, 768 // n
    sliced = w % 16 == 0

    def sds(shape, dtype):
        return jax.ShapeDtypeStruct(shape, dtype)

    values = dict(
        tok=tokens,
        cot=cotangent,
        wq=w_query,
        wkey=key_weight,
        wval=value_weight,
        wout=w_out,
        wparts=w_out.reshape(n, w, 768) if sliced else w_out,
        wg=w_gate,
        wu=w_up,
        wd=w_down,
        g1=gain_one,
        g2=gain_two,
        router=w_router,
        routes=routes.T,
        seg=segments,
    )
    shapes = dict(
        output=sds((512, 768), bf16),
        input_grad=sds((512, 768), f32),
        gains=sds((8, 768), f32),
        grad_query=sds((w, 768), f32),
        grad_key=sds((w, 256), f32),
        grad_value=sds((w, 256), f32),
        grad_out=sds((w, 768), f32),
        grad_router=sds((w, 128), f32),
        grad_gate=sds((E, w, 256), f32),
        grad_up=sds((E, w, 256), f32),
        grad_down=sds((E, w, 256), f32),
        far=sds((MINE, w, 768), bf16),
        far_b=sds((w, 640), bf16),
    )
    stages = n.bit_length() - 1
    piece, piece_a, piece_b = (2, w, 768), (1, w, 896), (2, w, 640)
    halves, whole = sds((512, 768), bf16), sds((1024, 768), bf16)
    expert_weight = sds((MINE, 256, 768), bf16)
    parts = sds((n, w, 768) if sliced else (768, 768), bf16)
    shapes.update(
        grad=sds((MINE, n) + piece, bf16),
        land=sds((MINE, n - 1) + piece, bf16),
        grad_a=sds((n,) + piece_a, bf16),
        land_a=sds((n - 1,) + piece_a, bf16),
        grad_b=sds((n,) + piece_b, bf16),
        land_b=sds((n - 1,) + piece_b, bf16),
        cland_o=whole,
        cland_p=whole,
        yland_o=halves,
        yland_p=halves,
        cot_y=halves,
        cot_c=halves,
        cot_yc=halves,
        n1oo=halves,
        n1ot=halves,
        n1yo=halves,
        n1yt=halves,
        rg=expert_weight,
        ru=expert_weight,
        rd=expert_weight,
        wy=parts,
        wyc=parts,
        wc=sds((768, 768), bf16),
        mrow=whole,
    )

    vb = lambda *shape: pltpu.VMEM(shape, bf16)
    vf = lambda *shape: pltpu.VMEM(shape, f32)
    dma = pltpu.SemaphoreType.DMA
    scratch = dict(
        n2o=vb(1024, 768),
        n2t=vb(1024, 768),
        go=vb(1024, 768),
        gt=vb(1024, 768),
        n2f=vb(1536, 1024),
        gf=vb(1536, 1024),
        q=vb(1024, 384),
        k=vb(1024, 128),
        v=vb(1024, 128),
        lse=vf(8, 1024),
        start=pltpu.VMEM((1, 1024), jnp.int32),
        cs=vf(1024, 128),
        sn=vf(1024, 128),
        wk=vb(640, 768),
        wr=vb(640, 768),
        wro=vb(128, 768),
        wrt=vb(128, 768),
        router_far=vb(E, 768),
        gain_send=vf(8, 768),
        gain_far=vf(8, 768),
        mid=vf(512, 768),
        s1=vf(512, 1),
        s2=vf(512, 1),
        myc=vb(1024, 384),
        gate=vf(1024, 128),
        ggs=vf(1024, 128),
        gg_send=vf(8, 1024),
        gg_row=vf(8, 1024),
        gg_sum=vf(8, 1024),
        gg_col=vf(8, 1024),
        cland_n=vb(1024, 768),
        yland_n=vb(512, 768),
        ysend_n=vb(512, 768),
        ysend_o=vb(512, 768),
        goo=vb(512, 768),
        gyo=vb(512, 768),
        got=vb(512, 768),
        gyt=vb(512, 768),
        gmid=vf(512, 768),
        stat=vf(512, 128),
        stat_land=vf(512, 128),
        gain_part=vf(8, 768),
        gain_row=vf(8, 768),
        gain_x=vf(8, 768),
        gain_land=vf(nz + 1, 8, 768),
        came=vb(n - 1, *piece),
        sums=vb(stages + 1, nz, *piece),
        shards_a=vb(n, *piece_a),
        far_b_send=vb(w, 640),
        far_b_here=vb(w, 640),
        wsem=dma((2, 6)),
        lsem=dma((38,)),
        esend=dma((TRADES,)),
        erecv=dma((TRADES,)),
        msend=dma((3 * MINE,)),
        mrecv=dma((3 * MINE,)),
        gsend=dma((n,)),
        grecv=dma((n,)),
        hsend=dma((nz,)),
        hrecv=dma((nz,)),
        fsend=dma((MINE,)),
        frecv=dma((MINE,)),
        xsend=dma(((MINE + 2) * stages,)),
        xarrive=dma(((MINE + 2) * stages,)),
    )
    anywhere, inside = pl.BlockSpec(memory_space=pl.ANY), pl.BlockSpec(memory_space=pltpu.VMEM)
    results = pl.pallas_call(
        functools.partial(layer_kernel, n, tuple(values), tuple(shapes), tuple(scratch)),
        out_shape=tuple(shapes.values()),
        in_specs=[anywhere] * 10 + [inside] * 5,
        out_specs=tuple(anywhere for _ in shapes),
        scratch_shapes=list(scratch.values()),
        compiler_params=pltpu.CompilerParams(
            vmem_limit_bytes=63 * MIB, collective_id=0, has_side_effects=True
        ),
        cost_estimate=pl.CostEstimate(
            flops=80 * 10**9, bytes_accessed=150 * MIB, transcendentals=0
        ),
        name="layer",
    )(*values.values())
    gains, router = results[2], results[7]
    moved = [*results[:2], *results[3:7], *results[8:11]]
    gain = sds((768,), f32)
    done = pl.pallas_call(
        hand_over_kernel,
        out_shape=(gain, gain, sds((E, w), f32)) + tuple(sds(x.shape, x.dtype) for x in moved),
        in_specs=[inside] * 2 + [anywhere] * 9,
        out_specs=(inside,) * 3 + (anywhere,) * 9,
        scratch_shapes=[pltpu.VMEM(x.shape, x.dtype) for x in moved] + [dma((2, 9))],
        compiler_params=pltpu.CompilerParams(vmem_limit_bytes=62 * MIB),
        name="hand_over",
    )(gains, router, *moved)
    gain_one, gain_two, router, output, input_grad = done[:5]
    heads, experts = [x.T for x in done[5:9]], [x.swapaxes(1, 2) for x in done[9:]]
    return output, input_grad, gain_one, *heads, gain_two, router, *experts


def solution(mesh):
    in_specs = (
        P(("dp", "row"), "col"),
        P(("dp", "row"), "col"),
        P("col"),
        P("row", "col"),
        P("row", "col"),
        P("row", "col"),
        P("col", "row"),
        P("col"),
        P(None, "col"),
        P(None, "row", "col"),
        P(None, "row", "col"),
        P(None, "row", "col"),
        P("dp", None),
        P("dp", None),
    )
    out_specs = (
        P(("dp", "row"), "col"),
        P(("dp", "row"), "col"),
        P("col"),
        P("row", ("col", "dp")),
        P("row", ("col", "dp")),
        P("row", ("col", "dp")),
        P("col", ("row", "dp")),
        P("col"),
        P(None, ("col", "dp")),
        P(None, "row", ("col", "dp")),
        P(None, "row", ("col", "dp")),
        P(None, "row", ("col", "dp")),
    )
    return jax.shard_map(
        functools.partial(local, mesh.shape["dp"]),
        mesh=mesh,
        in_specs=in_specs,
        out_specs=out_specs,
        check_vma=False,
    )
```

```python
import functools
import math

import jax
import jax.numpy as jnp
from jax import lax
from jax.experimental import pallas as pl
from jax.experimental.pallas import tpu as pltpu
from jax.sharding import PartitionSpec as P

WIDTH = 1536
HEAD = 64
E = 16
MINE = 8
EPS = 1e-06
SCALE = HEAD ** (-0.5)
NEG = -1e30
f32 = jnp.float32
bf16 = jnp.bfloat16
MIB = 1 << 20
MESH = pl.DeviceIdType.MESH
A, B, C = object(), object(), object()


def dot_nt(a, b):
    return lax.dot_general(a, b, (((1,), (1,)), ((), ())), preferred_element_type=f32)


def dot_nn(a, b):
    return lax.dot_general(a, b, (((1,), (0,)), ((), ())), preferred_element_type=f32)


def dot_tn(a, b):
    return lax.dot_general(a, b, (((0,), (0,)), ((), ())), preferred_element_type=f32)


def rotate(u, cosine, sine):
    lane = lax.broadcasted_iota(jnp.int32, u.shape, 1)
    turned = jnp.where((lane & 63) < 32, pltpu.roll(u, 96, 1), pltpu.roll(u, 32, 1))
    return u * cosine + turned * sine


def paired(u, t):
    return jnp.concatenate(
        [u[:, t * 64 : t * 64 + 64], u[:, 192 + t * 64 : 192 + t * 64 + 64]], axis=1
    )


def flip_block(values):
    eye = (
        lax.broadcasted_iota(jnp.int32, (256, 256), 0)
        == lax.broadcasted_iota(jnp.int32, (256, 256), 1)
    ).astype(bf16)
    return jnp.concatenate(
        [dot_nt(eye, values[:, i * 256 : i * 256 + 256]) for i in range(3)], axis=0
    ).astype(bf16)


def load_keys(pairs):
    lane = lax.broadcasted_iota(jnp.int32, (1024, 128), 1)
    for source, first, second in pairs:
        value = source[...].astype(f32)
        first[...] = jnp.where(lane < 64, value, 0.0).astype(bf16)
        second[...] = jnp.where(lane < 64, 0.0, value).astype(bf16)


def key_window(a):
    return max(a - 2, 0) * 256, a * 256 + 256


def key_bias(a, start):
    first, last = key_window(a)
    key = first + lax.broadcasted_iota(jnp.int32, (last - first, 256), 0)
    query = a * 256 + lax.broadcasted_iota(jnp.int32, (last - first, 256), 1)
    return jnp.where((key <= query) & (key >= start), 0.0, NEG)


def position(piece, order):
    places = len(order)
    return sum(((piece >> bit) & 1) << (places - 1 - j) for j, bit in enumerate(order))


def split_shards(values, part, lanes, i, order, stage, other=None, use_other=None):
    w = stage.shape[2]
    for d in range(stage.shape[0]):
        piece = jnp.bitwise_xor(d, i)
        place = position(piece, order)
        if other is not None:
            place = place + use_other * (position(piece, other) - place)
        stage[place, part, :, lanes] = values[d * w : (d + 1) * w].astype(bf16)


(
    TOK_C,
    WQ,
    WK,
    WV,
    GAIN,
    ROUTER,
    COT_C,
    W_PART,
    W_C,
    W_YC,
    GG_ROW,
    GG_COL,
    N_COL,
    N_ROW,
    O_COL,
    O_ROW,
    STAT_TWO,
    G_ROW,
    G_COL,
    G_ROW_COL,
    P_COL,
    P_ROW,
    STAT_ONE,
    GAIN_ROW,
    GAIN_X,
    FAR_B,
) = range(26)
TOK_Y, TOK_YC, MIX_Y, MIX_C, MIX_YC, COT_Y, COT_YC, TRADES = 28, 30, 32, 36, 40, 44, 46, 48


def early_experts(n):
    return 2 if n < 16 else 1


class Refs:
    def __init__(self, names, refs):
        self.__dict__.update(zip(names, refs))


def layer_kernel(n, inputs, outputs, scratch, *refs):
    nz, w = n // 2, 768 // n
    sliced = w % 16 == 0
    a = Refs(inputs, refs[: len(inputs)])
    refs = refs[len(inputs) :]
    o = Refs(outputs, refs[: len(outputs)])
    b = Refs(scratch, refs[len(outputs) :])
    i, r, c = lax.axis_index("dp"), lax.axis_index("row"), lax.axis_index("col")
    stages = n.bit_length() - 1
    near_first = tuple(range(stages))
    far_first = near_first[1:] + near_first[:1]
    early_count = early_experts(n)

    def block(at, size):
        return pl.ds(pl.multiple_of(at * size, size), size)

    own_rows, far_rows = block(r, 512), block(1 - r, 512)
    to_x, to_row, to_col = {"dp": jnp.bitwise_xor(i, 1)}, {"row": 1 - r}, {"col": 1 - c}

    def to_dp(bits):
        return {"dp": jnp.bitwise_xor(i, bits)}

    def remote(src, dst, sems, at, target):
        return pltpu.make_async_remote_copy(
            src_ref=src,
            dst_ref=dst,
            send_sem=sems[0].at[at],
            recv_sem=sems[1].at[at],
            device_id=target,
            device_id_type=MESH,
        )

    def trade(name, src, dst, target):
        return remote(src, dst, (b.esend, b.erecv), name, target)

    def load(src, dst, at):
        return pltpu.make_async_copy(src, dst, b.lsem.at[at])

    def run(*copies):
        for copy in copies:
            copy.start()
        for copy in copies:
            copy.wait()

    vb = lambda *shape: pltpu.VMEM(shape, bf16)
    vf = lambda *shape: pltpu.VMEM(shape, f32)


    def moe_copies(e):
        return [
            remote(src.at[MINE * (1 - c) + e], dst.at[e], (b.msend, b.mrecv), 3 * e + k, to_col)
            for k, (src, dst) in enumerate(((a.wg, o.rg), (a.wu, o.ru), (a.wd, o.rd)))
        ]

    def weight_loads(e, slot):
        pairs = (
            (a.wg, MINE * c + e),
            (o.rg, e),
            (a.wu, MINE * c + e),
            (o.ru, e),
            (a.wd, MINE * c + e),
            (o.rd, e),
        )
        return [
            pltpu.make_async_copy(ref.at[at], b.weights.at[slot, k], b.wsem.at[slot, k])
            for k, (ref, at) in enumerate(pairs)
        ]


    def chunk(k):
        if k is A:
            return o.grad_a, o.land_a, b.sum_a, b.came_a, MINE, near_first
        if k is B:
            return o.grad_b, o.land_b, b.sum_b, b.came_b, MINE + 1, far_first
        if k is C:
            return o.grad_c, o.land_c, b.sum_c, b.came_c, MINE + 2, near_first
        if isinstance(k, int) and k < early_count:
            return o.grad.at[k], o.land.at[k], b.sums.at[stages + k], b.came, k, far_first
        return o.grad.at[k], o.land.at[k], b.sums.at[k % stages], b.came, k, near_first

    def stage(k, j):
        grad, land, total, _, number, order = chunk(k)
        size = n >> (j + 1)
        return remote(
            (grad if j == 0 else total).at[pl.ds(size, size)],
            land.at[pl.ds(n - 2 * size, size)],
            (b.xsend, b.xarrive),
            number * stages + j,
            to_dp(1 << order[j]),
        )

    def begin(k, j):
        stage(k, j).wait_recv()
        grad, land, total, came, _, _ = chunk(k)
        size = n >> (j + 1)
        at = 0 if (k is A or k is B or k is C) else n - 2 * size
        loads = [load(land.at[pl.ds(n - 2 * size, size)], came.at[pl.ds(at, size)], 24 + j)]
        if j == 0:
            loads.append(load(grad.at[pl.ds(0, size)], total, 23))
        for copy in loads:
            copy.start()
        return loads

    def end(k, j, loads):
        _, _, total, came, _, _ = chunk(k)
        size = n >> (j + 1)
        at = 0 if (k is A or k is B or k is C) else n - 2 * size
        for copy in loads:
            copy.wait()
        if j == stages - 1:
            for earlier in range(1, stages):
                stage(k, earlier).wait_send()
            return total[0].astype(f32) + came[at].astype(f32)
        for piece in range(size - 1, -1, -1):
            total[piece] = total[piece] + came[at + piece]
            if piece == size // 2:
                stage(k, j + 1).start()

    def advance(k, j):
        return end(k, j, begin(k, j))

    def far_copy(k):
        place = k % 2 if k >= early_count else 2 + k
        return remote(b.far_send.at[place], o.far.at[k], (b.fsend, b.frecv), k, to_col)

    def puts(which, at):
        outs = (o.grad_gate, o.grad_up, o.grad_down)
        return [load(b.expert_out.at[which, m], outs[m].at[at], 32 + 3 * which + m) for m in range(3)]

    def put(which, values, at, wait):
        if wait:
            for copy in puts(which, at):
                copy.wait()
        for m in range(3):
            b.expert_out[which, m] = values[:, m * 256 : m * 256 + 256]
        for copy in puts(which, at):
            copy.start()

    def finish(q, total):
        if q >= early_count + 2:
            far_copy(q - 2).wait_send()
        b.far_send[q % 2 if q >= early_count else 2 + q] = total[1].astype(bf16)
        far_copy(q).start()
        put(0, total[0], MINE * c + q, q != early_count)

    def begin_far(q):
        far_copy(q).wait_recv()
        copy = load(o.far.at[q], b.far_here, 22)
        copy.start()
        return copy

    def end_far(q, copy):
        copy.wait()
        put(1, b.far_here[...].astype(f32), MINE * (1 - c) + q, q != early_count)

    def tick(k):
        jobs = [(k - j, j) for j in range(stages) if early_count <= k - j < MINE]
        loads = [begin(*job) for job in jobs]
        far = k - stages
        far_load = begin_far(far) if early_count <= far < MINE else None
        for (q, j), copies in zip(jobs, loads):
            total = end(q, j, copies)
            if j == stages - 1:
                finish(q, total)
        if far_load is not None:
            end_far(far, far_load)


    tok_y = [
        trade(TOK_Y + h, a.tok.at[pl.ds(h * 256, 256)], b.gyo.at[pl.ds(h * 256, 256)], to_row)
        for h in range(2)
    ]
    tok_yc = [
        trade(TOK_YC + h, b.gyo.at[pl.ds(h * 256, 256)], b.gyt.at[pl.ds(h * 256, 256)], to_col)
        for h in range(2)
    ]
    tok_c = trade(TOK_C, a.tok, b.got, to_col)
    heads = [
        trade(WQ, a.wq.at[block(1 - c, 384)], b.wr.at[pl.ds(0, 384)], to_col),
        trade(WK, a.wkey.at[block(1 - c, 128)], b.wr.at[pl.ds(384, 128)], to_col),
        trade(WV, a.wval.at[block(1 - c, 128)], b.wr.at[pl.ds(512, 128)], to_col),
    ]
    gain_copy = trade(GAIN, b.gain_send, b.gain_far, to_col)
    router_copy = trade(ROUTER, a.router, b.router_far, to_col)
    cot_rows = [pl.ds(h * 256, 256) for h in range(2)]
    cot_y = [
        trade(COT_Y + h, a.cot.at[cot_rows[h]], o.cot_y.at[cot_rows[h]], to_row) for h in range(2)
    ]
    cot_c = trade(COT_C, a.cot, o.cot_c, to_col)
    cot_yc = [
        trade(COT_YC + h, o.cot_y.at[cot_rows[h]], o.cot_yc.at[cot_rows[h]], to_col)
        for h in range(2)
    ]
    w_part = trade(
        W_PART,
        a.wparts.at[i] if sliced else a.wout,
        o.wy.at[i] if sliced else o.wy,
        to_row,
    )
    w_gather = [
        remote(o.wy.at[i], o.wy.at[i], (b.gsend, b.grecv), bits, to_dp(bits))
        for bits in (range(1, n) if sliced else ())
    ]
    w_c = trade(W_C, a.wout, o.wc, to_col)
    w_yc = trade(W_YC, o.wy, o.wyc, to_col)

    def front_scope(
        tok, w00, wc, wy, wyc, mixed, k0, k1, vt, n1oo, n1ot, n1yo, n1yt, mrow
    ):
        locals_ = [
            load(a.tok, tok, 0),
            load(a.wq.at[block(c, 384)], b.wk.at[pl.ds(0, 384)], 1),
            load(a.wkey.at[block(c, 128)], b.wk.at[pl.ds(384, 128)], 2),
            load(a.wval.at[block(c, 128)], b.wk.at[pl.ds(512, 128)], 3),
        ]
        late = [
            load(a.wout, w00, 10),
            load(a.cot, b.go.at[own_rows], 11),
        ]
        for copy in locals_ + late:
            copy.start()
        b.gain_send[...] = jnp.zeros_like(b.gain_send)
        b.gain_send[0:1, :] = a.g1[...].reshape(1, 768)
        b.gain_send[1:2, :] = a.g2[...].reshape(1, 768)
        barrier = pltpu.get_barrier_semaphore()
        partners = [to_row, to_col] + [to_dp(bits) for bits in range(1, n)]
        for target in partners:
            pl.semaphore_signal(barrier, inc=1, device_id=target, device_id_type=MESH)
        pl.semaphore_wait(barrier, len(partners))
        for copy in [w_part] + tok_y + [tok_c] + heads + [gain_copy, router_copy, cot_y[0], cot_c, w_c]:
            copy.start()
        for e in range(2):
            for copy in moe_copies(e):
                copy.start()

        w_part.wait()
        for copy in w_gather:
            copy.start()

        seg = a.seg[...].astype(f32)
        seg_column = jnp.broadcast_to(seg, (8, 1024)).T[:, 0:1]
        start, start_column = jnp.zeros_like(seg), jnp.zeros_like(seg_column)
        for number in range(1, 4):
            count = jnp.sum(jnp.where(seg < number, 1.0, 0.0), axis=1, keepdims=True)
            start = jnp.where(seg == number, count, start)
            start_column = jnp.where(seg_column == number, count, start_column)
        b.start[...] = start.astype(jnp.int32)
        lane = lax.broadcasted_iota(jnp.int32, (1024, 128), 1)
        place = lax.broadcasted_iota(jnp.int32, (1024, 128), 0).astype(f32)
        frequency = jnp.exp((lane & 31).astype(f32) * (-2.0 * math.log(10000.0) / HEAD))
        angles = (place - start_column) * frequency
        b.cs[...] = jnp.cos(angles)
        sine = jnp.sin(angles)
        b.sn[...] = jnp.where((lane & 63) < 32, -sine, sine)

        number = jnp.where(lane < MINE, lane + MINE * c, lane - MINE * c)
        number = jnp.where((lane >= MINE) & (c == 1), lane - MINE, number)
        number = jnp.where(lane < E, number, -1)
        used = jnp.zeros((1024, 128), f32)
        routes, number = a.routes[...].astype(f32).T, number.astype(f32)
        for k in range(8):
            used = jnp.where(routes[:, k : k + 1] == number, 1.0, used)
        b.gate[...] = used

        gain_copy.wait()

        def project(x_own, x_oth, place, rows, n_own, n_oth):
            u, v = x_own.astype(f32), x_oth.astype(f32)
            total = jnp.sum(u * u, axis=1, keepdims=True) + jnp.sum(v * v, axis=1, keepdims=True)
            s = lax.rsqrt(total / WIDTH + EPS)
            u = (u * s * b.gain_send[0:1, :]).astype(bf16)
            v = (v * s * b.gain_far[0:1, :]).astype(bf16)
            n_own[rows, :] = u
            n_oth[rows, :] = v
            raw = dot_nt(u, b.wk[...]) + dot_nt(v, b.wr[...])
            cs, sn = b.cs[place, :], b.sn[place, :]
            for t in range(3):
                b.q[place, t * 128 : t * 128 + 128] = rotate(paired(raw, t), cs, sn).astype(bf16)
            b.k[place, :] = rotate(raw[:, 384:512], cs, sn).astype(bf16)
            b.v[place, :] = raw[:, 512:640].astype(bf16)
            return s

        for copy in locals_ + [tok_c] + heads:
            copy.wait()
        for h in range(2):
            rows = slice(h * 256, h * 256 + 256)
            b.s1[rows, :] = project(
                tok[rows, :], b.got[rows, :], block(2 * r + h, 256), rows, n1oo, n1ot
            )
        def flip_cotangent(at):
            rows = block(at, 256)
            b.gf[0:768, rows] = flip_block(b.go[rows, :])
            b.gf[768:1536, rows] = flip_block(b.gt[rows, :])

        cot_c.wait()
        run(load(o.cot_c, b.gt.at[own_rows], 18))
        late[1].wait()
        for h in range(2):
            flip_cotangent(2 * r + h)
        for h in range(2):
            tok_y[h].wait()
            tok_yc[h].start()
        for h in range(2):
            rows = slice(h * 256, h * 256 + 256)
            tok_yc[h].wait()
            project(
                b.gyo[rows, :], b.gyt[rows, :], block(2 * (1 - r) + h, 256), rows, n1yo, n1yt
            )
        saves = [
            load(n1oo, o.n1oo, 12),
            load(n1ot, o.n1ot, 13),
            load(n1yo, o.n1yo, 14),
            load(n1yt, o.n1yt, 15),
        ]
        for copy in saves:
            copy.start()
        for e in range(2, 4):
            for copy in moe_copies(e):
                copy.start()

        load_keys([(b.k, k0, k1)])
        vt[...] = b.v[...].astype(f32).T.astype(bf16)
        mix_y, mix_c, mix_yc = [], [], []
        for at in range(4):
            rows = pl.ds(at * 256, 256)
            mix_y.append(
                trade(MIX_Y + at, mixed.at[rows], b.cland_n.at[rows, pl.ds(0, 384)], to_row)
            )
            mix_c.append(
                trade(MIX_C + at, mixed.at[rows], b.cland_n.at[rows, pl.ds(384, 384)], to_col)
            )
            mix_yc.append(
                trade(
                    MIX_YC + at, b.cland_n.at[rows, pl.ds(0, 384)], b.myc.at[rows], to_col
                )
            )

        def attend(at):
            rows = slice(at * 256, at * 256 + 256)
            window = slice(*key_window(at))
            bias = key_bias(at, b.start[:, rows])
            outs = [None] * 6
            for t in range(3):
                q = b.q[rows, t * 128 : t * 128 + 128] * jnp.asarray(SCALE, bf16)
                for j in range(2):
                    s = dot_nt((k0, k1)[j][window, :], q) + bias
                    top = jnp.max(s, axis=0, keepdims=True)
                    p = jnp.exp(s - top)
                    total = jnp.sum(p, axis=0, keepdims=True)
                    head = t + 3 * j
                    outs[head] = dot_nn(vt[j * 64 : j * 64 + 64, window], p.astype(bf16)) / total
                    b.lse[head : head + 1, rows] = top + jnp.log(total)
            mixed[rows, :] = jnp.concatenate(outs, axis=0).T.astype(bf16)
            mix_y[at].start()
            mix_c[at].start()

        attend(0)
        attend(1)
        for copy in w_gather:
            copy.wait()
        w_yc.start()
        loads = [load(o.wy, wy, 16)]
        loads[0].start()
        attend(2)
        attend(3)

        cot_y[1].start()
        cot_y[0].wait()
        cot_yc[0].start()
        for at in range(2):
            mix_y[at].wait()
            mix_yc[at].start()
        w_c.wait()
        w_yc.wait()
        far_blocks = [block(2 * (1 - r) + h, 256) for h in range(2)]
        loads += [
            load(o.cot_y.at[cot_rows[0]], b.go.at[far_blocks[0]], 17),
            load(o.wc, wc, 19),
            load(o.wyc, wyc, 20),
        ]
        for copy in loads[1:]:
            copy.start()
        cot_yc[0].wait()
        loads.append(load(o.cot_yc.at[cot_rows[0]], b.gt.at[far_blocks[0]], 21))
        loads[-1].start()
        for copy in late[:1] + loads:
            copy.wait()
        flip_cotangent(2 * (1 - r))

        router_copy.wait()
        for source, target in ((a.router, b.wro), (b.router_far, b.wrt)):
            value = source[...].astype(f32)
            low, high = value[0:MINE], value[MINE:E]
            target[...] = jnp.concatenate(
                [
                    jnp.where(c == 0, low, high),
                    jnp.where(c == 0, high, low),
                    jnp.zeros((128 - E, 768), f32),
                ],
                axis=0,
            ).astype(bf16)

        flat = (768, 768)
        for at in range(2):
            rows = slice(at * 512, at * 512 + 512)
            for piece in (2 * at, 2 * at + 1):
                mix_c[piece].wait()
                mix_yc[piece].wait()
            here, there = mixed[rows, :], b.cland_n[rows, 384:768]
            near = jnp.concatenate(
                [jnp.where(c == 0, here, there), jnp.where(c == 0, there, here)], axis=1
            )
            here, there = b.cland_n[rows, 0:384], b.myc[rows, :]
            far = jnp.concatenate(
                [jnp.where(c == 0, here, there), jnp.where(c == 0, there, here)], axis=1
            )
            mrow[rows, :] = near
            mine = r == at
            x_own = jnp.where(mine, tok[...], b.gyo[...]).astype(f32)
            x_oth = jnp.where(mine, b.got[...], b.gyt[...]).astype(f32)
            mid_own = x_own + (
                dot_nt(near, w00[...]) + dot_nt(far, wy[...].reshape(flat))
            )
            if at == 0:
                for piece in (2, 3):
                    mix_y[piece].wait()
                    mix_yc[piece].start()
            mid_oth = x_oth + (dot_nt(near, wc[...]) + dot_nt(far, wyc[...].reshape(flat)))
            total = jnp.sum(mid_own * mid_own, axis=1, keepdims=True) + jnp.sum(
                mid_oth * mid_oth, axis=1, keepdims=True
            )
            s = lax.rsqrt(total / WIDTH + EPS)

            @pl.when(mine)
            def _():
                b.mid[...] = mid_own
                b.s2[...] = s

            no = (mid_own * s * b.gain_send[1:2, :]).astype(bf16)
            nt = (mid_oth * s * b.gain_far[1:2, :]).astype(bf16)
            b.n2o[rows, :] = no
            b.n2t[rows, :] = nt
            for piece in range(2):
                part = slice(piece * 256, piece * 256 + 256)
                place = slice(at * 512 + piece * 256, at * 512 + piece * 256 + 256)
                b.n2f[0:768, place] = flip_block(no[part, :])
                b.n2f[768:1536, place] = flip_block(nt[part, :])
            logits = dot_nt(no, b.wro[...]) + dot_nt(nt, b.wrt[...])
            used = b.gate[rows, :]
            top = jnp.max(jnp.where(used > 0.0, logits, NEG), axis=1, keepdims=True)
            weight = jnp.where(used > 0.0, jnp.exp(jnp.minimum(logits - top, 0.0)), 0.0)
            b.gate[rows, :] = weight / jnp.sum(weight, axis=1, keepdims=True)
        cot_y[1].wait()
        cot_yc[1].start()
        run(load(o.cot_y.at[cot_rows[1]], b.go.at[far_blocks[1]], 17))
        cot_yc[1].wait()
        run(load(o.cot_yc.at[cot_rows[1]], b.gt.at[far_blocks[1]], 21))
        flip_cotangent(2 * (1 - r) + 1)
        saves.append(load(mrow, o.mrow, 22))
        saves[-1].start()
        for copy in saves:
            copy.wait()
        for e in range(4, MINE):
            for copy in moe_copies(e):
                copy.start()

    pl.run_scoped(
        front_scope,
        vb(512, 768),
        vb(768, 768),
        vb(768, 768),
        vb(n, w, 768) if sliced else vb(768, 768),
        vb(n, w, 768) if sliced else vb(768, 768),
        vb(1024, 384),
        vb(1024, 128),
        vb(1024, 128),
        vb(128, 1024),
        vb(512, 768),
        vb(512, 768),
        vb(512, 768),
        vb(512, 768),
        vb(1024, 768),
    )


    n_col = trade(N_COL, b.n2t, b.cland_n, to_col)
    o_col = trade(O_COL, b.gt, o.cland_o, to_col)

    def experts_scope(
        weights, gu_all, hs_all, acc_no, acc_nt, acc_oo, acc_ot, shards
    ):
        b.weights = weights
        for copy in moe_copies(0):
            copy.wait_recv()
        for copy in weight_loads(0, 0):
            copy.start()
        b.ggs[...] = jnp.zeros_like(b.ggs)

        def one(e, carry):
            slot = lax.rem(e, 2)

            @pl.when(e < MINE - 1)
            def _():
                for copy in moe_copies(e + 1):
                    copy.wait_recv()
                for copy in weight_loads(e + 1, 1 - slot):
                    copy.start()

            for copy in weight_loads(e, slot):
                copy.wait()
            wgk, wgr, wuk, wur, wdk, wdr = [b.weights.at[slot, k] for k in range(6)]
            for t in range(2):
                rows = slice(t * 512, t * 512 + 512)
                no, nt = b.n2o[rows, :], b.n2t[rows, :]
                gate_act = dot_nt(no, wgk[...]) + dot_nt(nt, wgr[...])
                up_act = dot_nt(no, wuk[...]) + dot_nt(nt, wur[...])
                grad = dot_nt(b.go[rows, :], wdk[...]) + dot_nt(b.gt[rows, :], wdr[...])
                lane = lax.broadcasted_iota(jnp.int32, (512, 128), 1)
                weight = jnp.sum(
                    jnp.where(lane == e, b.gate[rows, :], 0.0), axis=1, keepdims=True
                )
                s = 1.0 / (1.0 + jnp.exp(-gate_act))
                silu = gate_act * s
                hidden = (silu * up_act).astype(bf16).astype(f32)
                inner = jnp.sum(hidden * grad, axis=1, keepdims=True)
                b.ggs[rows, :] += jnp.where(lane == e, inner, 0.0)
                hs_all[rows, :] = (hidden * weight).astype(bf16)
                grad = grad * weight
                gu_all[rows, 0:256] = (
                    grad * up_act * s * (1.0 + gate_act * (1.0 - s))
                ).astype(bf16)
                gu_all[rows, 256:512] = (grad * silu).astype(bf16)
            first = 1 - lax.div(e + MINE - early_count, MINE)
            for half in range(2):
                rows = slice(half * 768, half * 768 + 768)
                gates = dot_nn(b.n2f[rows, :], gu_all[...])
                split_shards(gates, half, slice(0, 512), i, near_first, shards, far_first, first)
                downs = dot_nn(b.gf[rows, :], hs_all[...])
                split_shards(downs, half, slice(512, 768), i, near_first, shards, far_first, first)
            save = load(shards, o.grad.at[e], 8)
            save.start()

            for early in range(early_count):

                @pl.when(e == early)
                def _():
                    save.wait()
                    stage(early, 0).start()

            @pl.when(e == 0)
            def _():
                for total in (acc_no, acc_nt, acc_oo, acc_ot):
                    total[...] = jnp.zeros_like(total)

            gu, hs = gu_all[...], hs_all[...]
            acc_no[...] += dot_nn(gu, jnp.concatenate([wgk[...], wuk[...]], axis=0))
            acc_nt[...] += dot_nn(gu, jnp.concatenate([wgr[...], wur[...]], axis=0))
            acc_oo[...] += dot_nn(hs, wdk[...])
            acc_ot[...] += dot_nn(hs, wdr[...])

            @pl.when(e >= early_count)
            def _():
                save.wait()
                stage(e, 0).start()

            @pl.when(e == 3)
            def _():
                advance(0, 0)

            @pl.when(e == 5)
            def _():
                if early_count == 1:
                    tick(1)
                tick(2)

            @pl.when(e == 6)
            def _():
                if early_count == 2:
                    advance(1, 0)

            @pl.when(e == 7)
            def _():
                advance(0, 1)
                tick(3)

            return carry

        lax.fori_loop(0, MINE, one, 0)

        b.gg_send[...] = b.ggs[...].T[0:8]
        row_copy = trade(GG_ROW, b.gg_send, b.gg_row, to_row)
        row_copy.start()
        b.n2t[...] = acc_nt[...].astype(bf16)
        n_col.start()
        b.gt[...] = acc_ot[...].astype(bf16)
        o_col.start()
        b.n2o[...] = acc_no[...].astype(bf16)
        b.go[...] = acc_oo[...].astype(bf16)
        row_copy.wait()
        b.gg_sum[...] = b.gg_send[...] + b.gg_row[...]
        col_copy = trade(GG_COL, b.gg_sum, b.gg_col, to_col)
        col_copy.start()
        col_copy.wait()
        gate_grad = jnp.concatenate(
            [b.gg_sum[...], b.gg_col[...], jnp.zeros((112, 1024), f32)], axis=0
        ).T
        weighted = b.gate[...] * gate_grad
        grad_logits = weighted - b.gate[...] * jnp.sum(weighted, axis=1, keepdims=True)
        b.ggs[...] = grad_logits
        routers = dot_nn(b.n2f[0:768, :], grad_logits.astype(bf16))
        split_shards(routers, 0, slice(768, 896), i, near_first, b.shards_a)

    pl.run_scoped(
        experts_scope,
        vb(2, 6, 256, 768),
        vb(1024, 512),
        vb(1024, 256),
        vf(1024, 768),
        vf(1024, 768),
        vf(1024, 768),
        vf(1024, 768),
        vb(n, 2, w, 768),
    )


    def rest_scope(
        wmo, wmt, cot, tok, land_y, k0, k1, v0, v1, kt, sumk0, sumk1, sumv0, sumv1,
        grads, shards_b, shards_c, in_stage, came_a, sum_a, came_b, sum_b, came_c, sum_c,
        far_send, far_here, expert_out,
        out_out, router_out,
    ):
        b.came_a, b.sum_a, b.came_b, b.sum_b = came_a, sum_a, came_b, sum_b
        b.came_c, b.sum_c = came_c, sum_c
        b.far_send, b.far_here, b.expert_out = far_send, far_here, expert_out
        thirds = [(pl.ds(k * 512, 512), pl.ds(0, 768)) for k in range(3)]
        n1oo, n1ot, n1yo = [b.n2f.at[at] for at in thirds]
        n1yt, mro, mry = [b.gf.at[at] for at in thirds]
        early = [load(a.cot, cot, 10), load(a.tok, tok, 11)]
        late = [
            load(o.n1oo, n1oo, 12),
            load(o.n1ot, n1ot, 13),
            load(o.n1yo, n1yo, 14),
            load(o.n1yt, n1yt, 15),
            load(o.mrow.at[own_rows], mro, 16),
            load(o.mrow.at[far_rows], mry, 17),
            load(a.wout.at[:, block(c, 384)], wmo, 18),
            load(o.wc.at[:, block(c, 384)], wmt, 19),
        ]
        for copy in early + late:
            copy.start()

        def norm_back(values, scale, gain, gradient, name, land):
            weighted = gradient * gain
            b.stat[...] = jnp.broadcast_to(
                jnp.sum(weighted * values, axis=1, keepdims=True), (512, 128)
            )
            copy = trade(name, b.stat, land, to_col)
            copy.start()
            gain_grad = jnp.sum(gradient * values * scale, axis=0, keepdims=True)
            copy.wait()
            inner = (b.stat[...] + land[...])[:, 0:1]
            grad = scale * weighted - values * (scale * scale * scale) * (inner / WIDTH)
            return grad, gain_grad

        n_col.wait()
        b.ysend_n[...] = (
            b.n2o[far_rows, :].astype(f32) + b.cland_n[far_rows, :].astype(f32)
        ).astype(bf16)
        y_n = trade(N_ROW, b.ysend_n, b.yland_n, to_row)
        y_n.start()
        gl = b.ggs[own_rows, :]
        gl_high = gl.astype(bf16)
        gl_low = (gl - gl_high.astype(f32)).astype(bf16)
        b.gmid[...] = (
            b.n2o[own_rows, :].astype(f32)
            + b.cland_n[own_rows, :].astype(f32)
            + dot_nn(gl_high, b.wro[...])
            + dot_nn(gl_low, b.wro[...])
        )
        if early_count == 2:
            advance(1, 1)
        tick(4)
        for copy in early:
            copy.wait()
        y_n.wait()
        grad, gain_grad = norm_back(
            b.mid[...],
            b.s2[...],
            b.gain_send[1:2, :],
            b.gmid[...] + b.yland_n[...].astype(f32),
            STAT_TWO,
            b.stat_land,
        )
        b.gain_part[...] = jnp.zeros_like(b.gain_part)
        b.gain_part[1:2, :] = gain_grad
        b.gmid[...] = cot[...].astype(f32) + grad
        b.goo[...] = b.gmid[...].astype(bf16)
        y_g = trade(G_ROW, b.goo, b.gyo, to_row)
        c_g = trade(G_COL, b.goo, b.got, to_col)
        y_g.start()
        c_g.start()

        o_col.wait()
        run(load(o.cland_o, b.gt, 4))
        b.ysend_o[...] = (
            b.go[far_rows, :].astype(f32) + b.gt[far_rows, :].astype(f32)
        ).astype(bf16)
        y_o = trade(O_ROW, b.ysend_o, o.yland_o, to_row)
        y_o.start()
        b.mid[...] = (
            b.mid[...] + b.go[own_rows, :].astype(f32) + b.gt[own_rows, :].astype(f32)
        )
        tick(5)

        y_g.wait()
        c_gy = trade(G_ROW_COL, b.gyo, b.gyt, to_col)
        c_gy.start()
        for copy in late:
            copy.wait()
        outs = dot_tn(mro[...], b.goo[...]) + dot_tn(mry[...], b.gyo[...])
        split_shards(outs, 0, slice(0, 768), i, near_first, b.shards_a)
        save = load(b.shards_a, o.grad_a, 4)
        save.start()
        load_keys([(b.k, k0, k1), (b.v, v0, v1)])
        kt[...] = b.k[...].astype(f32).T.astype(bf16)
        for total in (sumk0, sumk1, sumv0, sumv1):
            total[...] = jnp.zeros_like(total)
        save.wait()
        stage(A, 0).start()
        c_g.wait()
        c_gy.wait()

        def one_block(at):
            near = at // 2 == r
            rows = slice((at % 2) * 256, (at % 2) * 256 + 256)
            place = slice(at * 256, at * 256 + 256)
            g_own = jnp.where(near, b.goo[rows, :], b.gyo[rows, :])
            g_oth = jnp.where(near, b.got[rows, :], b.gyt[rows, :])
            gm = (dot_nn(g_own, wmo[...]) + dot_nn(g_oth, wmt[...])).astype(bf16)
            window = slice(*key_window(at))
            bias = key_bias(at, b.start[:, place])
            parts = [None] * 6
            for t in range(3):
                qt = b.q[place, t * 128 : t * 128 + 128] * jnp.asarray(SCALE, bf16)
                gmt = paired(gm, t)
                for j in range(2):
                    head = t + 3 * j
                    s = dot_nt((k0, k1)[j][window, :], qt) + bias
                    p = jnp.exp(s - b.lse[head : head + 1, place])
                    gp = dot_nt((v0, v1)[j][window, :], gmt)
                    inner = jnp.sum(p * gp, axis=0, keepdims=True)
                    gs = (p * (gp - inner)).astype(bf16)
                    (sumv0, sumv1)[j][window, :] += dot_nn(p.astype(bf16), gmt)
                    (sumk0, sumk1)[j][window, :] += dot_nn(gs, qt)
                    parts[head] = dot_nn(kt[j * 64 : j * 64 + 64, window], gs) * SCALE
            gq = jnp.concatenate(parts, axis=0).T
            cosine, sine = b.cs[place, :], b.sn[place, :]
            for t in range(3):
                grads[place, t * 128 : t * 128 + 128] = rotate(
                    gq[:, t * 128 : t * 128 + 128], cosine, -sine
                ).astype(bf16)

        for at in range(4):
            one_block(at)
        tick(6)
        lane = lax.broadcasted_iota(jnp.int32, (1024, 128), 1)
        gk = jnp.where(lane < 64, sumk0[...], sumk1[...])
        gv = jnp.where(lane < 64, sumv0[...], sumv1[...])
        grads[:, 384:512] = rotate(gk, b.cs[...], -b.sn[...]).astype(bf16)
        grads[:, 512:640] = gv.astype(bf16)

        b.n2t[...] = dot_nn(grads[...], b.wr[...]).astype(bf16)
        c_p = trade(P_COL, b.n2t, o.cland_p, to_col)
        c_p.start()
        b.n2o[...] = dot_nn(grads[...], b.wk[...]).astype(bf16)
        for shards, left, far, k, order in (
            (shards_b, n1ot, n1yt, B, far_first),
            (shards_c, n1oo, n1yo, C, near_first),
        ):
            heads_grad = dot_tn(left[...], grads[own_rows, :]) + dot_tn(
                far[...], grads[far_rows, :]
            )
            split_shards(heads_grad, 0, slice(0, 640), i, order, shards)
            run(load(shards, o.grad_b if k is B else o.grad_c, 4))
            stage(k, 0).start()
        c_p.wait()
        run(load(o.cland_p, b.gt, 4))
        b.ysend_n[...] = (
            b.n2o[far_rows, :].astype(f32) + b.gt[far_rows, :].astype(f32)
        ).astype(bf16)
        y_p = trade(P_ROW, b.ysend_n, o.yland_p, to_row)
        y_p.start()
        tick(7)

        y_o.wait()
        run(load(o.yland_o, land_y, 4))
        land_y[...] = (b.mid[...] + land_y[...].astype(f32)).astype(bf16)
        run(load(land_y, o.output, 7))
        y_p.wait()
        run(load(o.yland_p, land_y, 4))
        grad, gain_grad = norm_back(
            tok[...].astype(f32),
            b.s1[...],
            b.gain_send[0:1, :],
            b.n2o[own_rows, :].astype(f32)
            + b.gt[own_rows, :].astype(f32)
            + land_y[...].astype(f32),
            STAT_ONE,
            b.stat_land,
        )
        in_stage[...] = b.gmid[...] + grad
        last = load(in_stage, o.input_grad, 7)
        last.start()
        b.gain_part[0:1, :] = gain_grad
        advance(B, 0)

        step = trade(GAIN_ROW, b.gain_part, b.gain_land.at[0], to_row)
        step.start()
        step.wait()
        b.gain_row[...] = b.gain_part[...] + b.gain_land[0]
        step = trade(GAIN_X, b.gain_row, b.gain_land.at[1], to_x)
        step.start()
        step.wait()
        b.gain_x[...] = b.gain_row[...] + b.gain_land[1]
        steps = [
            remote(b.gain_x, b.gain_land.at[1 + s], (b.hsend, b.hrecv), s, to_dp(2 * s))
            for s in range(1, nz)
        ]
        for step in steps:
            step.start()
        total = b.gain_x[...]
        for step in steps:
            step.wait()
        for s in range(1, nz):
            total = total + b.gain_land[1 + s]
        last.wait()
        b.gain_row[...] = total
        run(load(b.gain_row, o.gains, 7))
        tick(8)
        for early in range(early_count):
            for j in range(2, stages - 1):
                advance(early, j)
            finish(early, advance(early, stages - 1))
        for j in range(1, stages - 1):
            advance(B, j)
        advance(A, 0)
        for early in range(early_count):
            end_far(early, begin_far(early))
        tick(9)
        advance(C, 0)
        for j in range(1, stages - 1):
            advance(A, j)
        b.far_b_send[...] = advance(B, stages - 1)[0].astype(bf16)
        copy = trade(FAR_B, b.far_b_send, o.far_b, to_col)
        copy.start()
        for k in range(10, MINE + stages):
            tick(k)
        for j in range(1, stages - 1):
            advance(C, j)
        total = advance(A, stages - 1)[0]
        out_out[...] = total[:, 0:768]
        router_out[...] = total[:, 768:896]
        run(load(out_out, o.grad_out, 4), load(router_out, o.grad_router, 5))

        def put_heads(values, which):
            out_out[:, 0:640] = values
            run(
                load(out_out.at[:, pl.ds(0, 384)], o.grad_query.at[:, block(which, 384)], 4),
                load(out_out.at[:, pl.ds(384, 128)], o.grad_key.at[:, block(which, 128)], 5),
                load(out_out.at[:, pl.ds(512, 128)], o.grad_value.at[:, block(which, 128)], 6),
            )

        copy.wait()
        run(load(o.far_b, b.far_b_here, 21))
        put_heads(b.far_b_here[...].astype(f32), 1 - c)
        put_heads(advance(C, stages - 1)[0], c)

        for e in range(MINE):
            for copy in moe_copies(e):
                copy.wait_send()
        for k in list(range(MINE)) + [A, B, C]:
            stage(k, 0).wait_send()
        for early in range(early_count):
            far_copy(early).wait_send()
        far_copy(MINE - 2).wait_send()
        far_copy(MINE - 1).wait_send()
        for which in range(2):
            for copy in puts(which, 0):
                copy.wait()

    pl.run_scoped(
        rest_scope,
        *[vb(768, 384)] * 2,
        vb(512, 768),
        vb(512, 768),
        vb(512, 768),
        *[vb(1024, 128)] * 4,
        vb(128, 1024),
        *[vf(1024, 128)] * 4,
        vb(1024, 640),
        vb(n, 1, w, 640),
        vb(n, 1, w, 640),
        vf(512, 768),
        *[vb(nz, 1, w, 896)] * 2,
        *[vb(nz, 1, w, 640)] * 4,
        vb(2 + early_count, w, 768),
        vb(w, 768),
        vf(2, 3, w, 256),
        vf(w, 768),
        vf(w, 128),
    )


def hand_over_kernel(gains, router, *refs):
    sources, gain_one, gain_two, router_out = refs[:9], refs[9], refs[10], refs[11]
    targets, places, sems = refs[12:21], refs[21:30], refs[30]
    copies = [
        pltpu.make_async_copy(source, place, sems.at[0, k])
        for k, (source, place) in enumerate(zip(sources, places))
    ]
    for copy in copies:
        copy.start()
    gain_one[...] = gains[0, :]
    gain_two[...] = gains[1, :]
    c, w = lax.axis_index("col"), router.shape[0]
    value = jnp.concatenate([router[...], jnp.zeros((128 - w, 128), f32)], axis=0).T[0:E, 0:w]
    low, high = value[0:MINE], value[MINE:E]
    router_out[...] = jnp.concatenate(
        [jnp.where(c == 0, low, high), jnp.where(c == 0, high, low)], axis=0
    )
    for k in range(9):
        copies[k].wait()
        copies[k] = pltpu.make_async_copy(places[k], targets[k], sems.at[1, k])
        copies[k].start()
    for copy in copies:
        copy.wait()


def local(
    n,
    tokens,
    cotangent,
    gain_one,
    w_query,
    key_weight,
    value_weight,
    w_out,
    gain_two,
    w_router,
    w_gate,
    w_up,
    w_down,
    routes,
    segments,
):
    nz, w = n // 2, 768 // n
    sliced = w % 16 == 0

    def sds(shape, dtype):
        return jax.ShapeDtypeStruct(shape, dtype)

    values = dict(
        tok=tokens,
        cot=cotangent,
        wq=w_query,
        wkey=key_weight,
        wval=value_weight,
        wout=w_out,
        wparts=w_out.reshape(n, w, 768) if sliced else w_out,
        wg=w_gate,
        wu=w_up,
        wd=w_down,
        g1=gain_one,
        g2=gain_two,
        router=w_router,
        routes=routes.T,
        seg=segments,
    )
    shapes = dict(
        output=sds((512, 768), bf16),
        input_grad=sds((512, 768), f32),
        gains=sds((8, 768), f32),
        grad_query=sds((w, 768), f32),
        grad_key=sds((w, 256), f32),
        grad_value=sds((w, 256), f32),
        grad_out=sds((w, 768), f32),
        grad_router=sds((w, 128), f32),
        grad_gate=sds((E, w, 256), f32),
        grad_up=sds((E, w, 256), f32),
        grad_down=sds((E, w, 256), f32),
        far=sds((MINE, w, 768), bf16),
        far_b=sds((w, 640), bf16),
    )
    stages = n.bit_length() - 1
    piece, piece_a, piece_b = (2, w, 768), (1, w, 896), (1, w, 640)
    halves, whole = sds((512, 768), bf16), sds((1024, 768), bf16)
    expert_weight = sds((MINE, 256, 768), bf16)
    parts = sds((n, w, 768) if sliced else (768, 768), bf16)
    shapes.update(
        grad=sds((MINE, n) + piece, bf16),
        land=sds((MINE, n - 1) + piece, bf16),
        grad_a=sds((n,) + piece_a, bf16),
        land_a=sds((n - 1,) + piece_a, bf16),
        grad_b=sds((n,) + piece_b, bf16),
        land_b=sds((n - 1,) + piece_b, bf16),
        grad_c=sds((n,) + piece_b, bf16),
        land_c=sds((n - 1,) + piece_b, bf16),
        cland_o=whole,
        cland_p=whole,
        yland_o=halves,
        yland_p=halves,
        cot_y=halves,
        cot_c=halves,
        cot_yc=halves,
        n1oo=halves,
        n1ot=halves,
        n1yo=halves,
        n1yt=halves,
        rg=expert_weight,
        ru=expert_weight,
        rd=expert_weight,
        wy=parts,
        wyc=parts,
        wc=sds((768, 768), bf16),
        mrow=whole,
    )

    vb = lambda *shape: pltpu.VMEM(shape, bf16)
    vf = lambda *shape: pltpu.VMEM(shape, f32)
    dma = pltpu.SemaphoreType.DMA
    scratch = dict(
        n2o=vb(1024, 768),
        n2t=vb(1024, 768),
        go=vb(1024, 768),
        gt=vb(1024, 768),
        n2f=vb(1536, 1024),
        gf=vb(1536, 1024),
        q=vb(1024, 384),
        k=vb(1024, 128),
        v=vb(1024, 128),
        lse=vf(8, 1024),
        start=pltpu.VMEM((1, 1024), jnp.int32),
        cs=vf(1024, 128),
        sn=vf(1024, 128),
        wk=vb(640, 768),
        wr=vb(640, 768),
        wro=vb(128, 768),
        wrt=vb(128, 768),
        router_far=vb(E, 768),
        gain_send=vf(8, 768),
        gain_far=vf(8, 768),
        mid=vf(512, 768),
        s1=vf(512, 1),
        s2=vf(512, 1),
        myc=vb(1024, 384),
        gate=vf(1024, 128),
        ggs=vf(1024, 128),
        gg_send=vf(8, 1024),
        gg_row=vf(8, 1024),
        gg_sum=vf(8, 1024),
        gg_col=vf(8, 1024),
        cland_n=vb(1024, 768),
        yland_n=vb(512, 768),
        ysend_n=vb(512, 768),
        ysend_o=vb(512, 768),
        goo=vb(512, 768),
        gyo=vb(512, 768),
        got=vb(512, 768),
        gyt=vb(512, 768),
        gmid=vf(512, 768),
        stat=vf(512, 128),
        stat_land=vf(512, 128),
        gain_part=vf(8, 768),
        gain_row=vf(8, 768),
        gain_x=vf(8, 768),
        gain_land=vf(nz + 1, 8, 768),
        came=vb(n - 1, *piece),
        sums=vb(stages + early_experts(n), nz, *piece),
        shards_a=vb(n, *piece_a),
        far_b_send=vb(w, 640),
        far_b_here=vb(w, 640),
        wsem=dma((2, 6)),
        lsem=dma((38,)),
        esend=dma((TRADES,)),
        erecv=dma((TRADES,)),
        msend=dma((3 * MINE,)),
        mrecv=dma((3 * MINE,)),
        gsend=dma((n,)),
        grecv=dma((n,)),
        hsend=dma((nz,)),
        hrecv=dma((nz,)),
        fsend=dma((MINE,)),
        frecv=dma((MINE,)),
        xsend=dma(((MINE + 3) * stages,)),
        xarrive=dma(((MINE + 3) * stages,)),
    )
    anywhere, inside = pl.BlockSpec(memory_space=pl.ANY), pl.BlockSpec(memory_space=pltpu.VMEM)
    results = pl.pallas_call(
        functools.partial(layer_kernel, n, tuple(values), tuple(shapes), tuple(scratch)),
        out_shape=tuple(shapes.values()),
        in_specs=[anywhere] * 10 + [inside] * 5,
        out_specs=tuple(anywhere for _ in shapes),
        scratch_shapes=list(scratch.values()),
        compiler_params=pltpu.CompilerParams(
            vmem_limit_bytes=63 * MIB, collective_id=0, has_side_effects=True
        ),
        cost_estimate=pl.CostEstimate(
            flops=80 * 10**9, bytes_accessed=150 * MIB, transcendentals=0
        ),
        name="layer",
    )(*values.values())
    gains, router = results[2], results[7]
    moved = [*results[:2], *results[3:7], *results[8:11]]
    gain = sds((768,), f32)
    done = pl.pallas_call(
        hand_over_kernel,
        out_shape=(gain, gain, sds((E, w), f32)) + tuple(sds(x.shape, x.dtype) for x in moved),
        in_specs=[inside] * 2 + [anywhere] * 9,
        out_specs=(inside,) * 3 + (anywhere,) * 9,
        scratch_shapes=[pltpu.VMEM(x.shape, x.dtype) for x in moved] + [dma((2, 9))],
        compiler_params=pltpu.CompilerParams(vmem_limit_bytes=62 * MIB),
        name="hand_over",
    )(gains, router, *moved)
    gain_one, gain_two, router, output, input_grad = done[:5]
    heads, experts = [x.T for x in done[5:9]], [x.swapaxes(1, 2) for x in done[9:]]
    return output, input_grad, gain_one, *heads, gain_two, router, *experts


def solution(mesh):
    in_specs = (
        P(("dp", "row"), "col"),
        P(("dp", "row"), "col"),
        P("col"),
        P("row", "col"),
        P("row", "col"),
        P("row", "col"),
        P("col", "row"),
        P("col"),
        P(None, "col"),
        P(None, "row", "col"),
        P(None, "row", "col"),
        P(None, "row", "col"),
        P("dp", None),
        P("dp", None),
    )
    out_specs = (
        P(("dp", "row"), "col"),
        P(("dp", "row"), "col"),
        P("col"),
        P("row", ("col", "dp")),
        P("row", ("col", "dp")),
        P("row", ("col", "dp")),
        P("col", ("row", "dp")),
        P("col"),
        P(None, ("col", "dp")),
        P(None, "row", ("col", "dp")),
        P(None, "row", ("col", "dp")),
        P(None, "row", ("col", "dp")),
    )
    return jax.shard_map(
        functools.partial(local, mesh.shape["dp"]),
        mesh=mesh,
        in_specs=in_specs,
        out_specs=out_specs,
        check_vma=False,
    )
```

```python
import functools
import math

import jax
import jax.numpy as jnp
from jax import lax
from jax.experimental import pallas as pl
from jax.experimental.pallas import tpu as pltpu
from jax.sharding import PartitionSpec as P

WIDTH = 1536
HEAD = 64
E = 16
MINE = 8
EPS = 1e-06
SCALE = HEAD ** (-0.5)
NEG = -1e30
f32 = jnp.float32
bf16 = jnp.bfloat16
MIB = 1 << 20
MESH = pl.DeviceIdType.MESH
A, B, C = object(), object(), object()


def dot_nt(a, b):
    return lax.dot_general(a, b, (((1,), (1,)), ((), ())), preferred_element_type=f32)


def dot_nn(a, b):
    return lax.dot_general(a, b, (((1,), (0,)), ((), ())), preferred_element_type=f32)


def dot_tn(a, b):
    return lax.dot_general(a, b, (((0,), (0,)), ((), ())), preferred_element_type=f32)


def rotate(u, cosine, sine):
    lane = lax.broadcasted_iota(jnp.int32, u.shape, 1)
    turned = jnp.where((lane & 63) < 32, pltpu.roll(u, 96, 1), pltpu.roll(u, 32, 1))
    return u * cosine + turned * sine


def paired(u, t):
    return jnp.concatenate(
        [u[:, t * 64 : t * 64 + 64], u[:, 192 + t * 64 : 192 + t * 64 + 64]], axis=1
    )


def flip_block(values):
    eye = (
        lax.broadcasted_iota(jnp.int32, (256, 256), 0)
        == lax.broadcasted_iota(jnp.int32, (256, 256), 1)
    ).astype(bf16)
    return jnp.concatenate(
        [dot_nt(eye, values[:, i * 256 : i * 256 + 256]) for i in range(3)], axis=0
    ).astype(bf16)


def load_keys(pairs):
    lane = lax.broadcasted_iota(jnp.int32, (1024, 128), 1)
    for source, first, second in pairs:
        value = source[...].astype(f32)
        first[...] = jnp.where(lane < 64, value, 0.0).astype(bf16)
        second[...] = jnp.where(lane < 64, 0.0, value).astype(bf16)


def key_window(a):
    return max(a - 2, 0) * 256, a * 256 + 256


def key_bias(a, start):
    first, last = key_window(a)
    key = first + lax.broadcasted_iota(jnp.int32, (last - first, 256), 0)
    query = a * 256 + lax.broadcasted_iota(jnp.int32, (last - first, 256), 1)
    return jnp.where((key <= query) & (key >= start), 0.0, NEG)


def position(piece, order):
    places = len(order)
    return sum(((piece >> bit) & 1) << (places - 1 - j) for j, bit in enumerate(order))


def split_shards(values, part, lanes, i, order, stage, other=None, use_other=None):
    w = stage.shape[2]
    for d in range(stage.shape[0]):
        piece = jnp.bitwise_xor(d, i)
        place = position(piece, order)
        if other is not None:
            place = place + use_other * (position(piece, other) - place)
        stage[place, part, :, lanes] = values[d * w : (d + 1) * w].astype(bf16)


(
    TOK_C,
    WQ,
    WK,
    WV,
    GAIN,
    ROUTER,
    COT_C,
    W_PART,
    W_C,
    W_YC,
    GG_ROW,
    GG_COL,
    N_COL,
    N_ROW,
    O_COL,
    O_ROW,
    STAT_TWO,
    G_ROW,
    G_COL,
    G_ROW_COL,
    P_COL,
    P_ROW,
    STAT_ONE,
    GAIN_ROW,
    GAIN_X,
    FAR_B,
) = range(26)
TOK_Y, TOK_YC, MIX_Y, MIX_C, MIX_YC, COT_Y, COT_YC, TRADES = 28, 30, 32, 36, 40, 44, 46, 48


def early_experts(n):
    return 2 if n < 16 else 1


class Refs:
    def __init__(self, names, refs):
        self.__dict__.update(zip(names, refs))


def layer_kernel(n, inputs, outputs, scratch, *refs):
    nz, w = n // 2, 768 // n
    sliced = w % 16 == 0
    a = Refs(inputs, refs[: len(inputs)])
    refs = refs[len(inputs) :]
    o = Refs(outputs, refs[: len(outputs)])
    b = Refs(scratch, refs[len(outputs) :])
    i, r, c = lax.axis_index("dp"), lax.axis_index("row"), lax.axis_index("col")
    stages = n.bit_length() - 1
    near_first = tuple(range(stages))
    far_first = near_first[1:] + near_first[:1]
    early_count = early_experts(n)

    def block(at, size):
        return pl.ds(pl.multiple_of(at * size, size), size)

    own_rows, far_rows = block(r, 512), block(1 - r, 512)
    to_x, to_row, to_col = {"dp": jnp.bitwise_xor(i, 1)}, {"row": 1 - r}, {"col": 1 - c}

    def to_dp(bits):
        return {"dp": jnp.bitwise_xor(i, bits)}

    def remote(src, dst, sems, at, target):
        return pltpu.make_async_remote_copy(
            src_ref=src,
            dst_ref=dst,
            send_sem=sems[0].at[at],
            recv_sem=sems[1].at[at],
            device_id=target,
            device_id_type=MESH,
        )

    def trade(name, src, dst, target):
        return remote(src, dst, (b.esend, b.erecv), name, target)

    def load(src, dst, at):
        return pltpu.make_async_copy(src, dst, b.lsem.at[at])

    def run(*copies):
        for copy in copies:
            copy.start()
        for copy in copies:
            copy.wait()

    vb = lambda *shape: pltpu.VMEM(shape, bf16)
    vf = lambda *shape: pltpu.VMEM(shape, f32)


    def moe_copies(e):
        return [
            remote(src.at[MINE * (1 - c) + e], dst.at[e], (b.msend, b.mrecv), 3 * e + k, to_col)
            for k, (src, dst) in enumerate(((a.wg, o.rg), (a.wu, o.ru), (a.wd, o.rd)))
        ]

    def weight_loads(e, slot):
        pairs = (
            (a.wg, MINE * c + e),
            (o.rg, e),
            (a.wu, MINE * c + e),
            (o.ru, e),
            (a.wd, MINE * c + e),
            (o.rd, e),
        )
        return [
            pltpu.make_async_copy(ref.at[at], b.weights.at[slot, k], b.wsem.at[slot, k])
            for k, (ref, at) in enumerate(pairs)
        ]


    def chunk(k):
        if k is A:
            return o.grad_a, o.land_a, b.sum_a, b.came_a, MINE, near_first
        if k is B:
            return o.grad_b, o.land_b, b.sum_b, b.came_b, MINE + 1, far_first
        if k is C:
            return o.grad_c, o.land_c, b.sum_c, b.came_c, MINE + 2, near_first
        if isinstance(k, int) and k < early_count:
            return o.grad.at[k], o.land.at[k], b.sums.at[stages + k], b.came, k, far_first
        return o.grad.at[k], o.land.at[k], b.sums.at[k % stages], b.came, k, near_first

    def stage(k, j):
        grad, land, total, _, number, order = chunk(k)
        size = n >> (j + 1)
        return remote(
            (grad if j == 0 else total).at[pl.ds(size, size)],
            land.at[pl.ds(n - 2 * size, size)],
            (b.xsend, b.xarrive),
            number * stages + j,
            to_dp(1 << order[j]),
        )

    def begin(k, j):
        stage(k, j).wait_recv()
        grad, land, total, came, _, _ = chunk(k)
        size = n >> (j + 1)
        at = 0 if (k is A or k is B or k is C) else n - 2 * size
        loads = [load(land.at[pl.ds(n - 2 * size, size)], came.at[pl.ds(at, size)], 24 + j)]
        if j == 0:
            loads.append(load(grad.at[pl.ds(0, size)], total, 23))
        for copy in loads:
            copy.start()
        return loads

    def end(k, j, loads):
        _, _, total, came, _, _ = chunk(k)
        size = n >> (j + 1)
        at = 0 if (k is A or k is B or k is C) else n - 2 * size
        for copy in loads:
            copy.wait()
        if j == stages - 1:
            for earlier in range(1, stages):
                stage(k, earlier).wait_send()
            return total[0].astype(f32) + came[at].astype(f32)
        for piece in range(size - 1, -1, -1):
            total[piece] = total[piece] + came[at + piece]
            if piece == size // 2:
                stage(k, j + 1).start()

    def advance(k, j):
        return end(k, j, begin(k, j))

    def far_copy(k):
        place = k % 2 if k >= early_count else 2 + k
        return remote(b.far_send.at[place], o.far.at[k], (b.fsend, b.frecv), k, to_col)

    def puts(which, at):
        outs = (o.grad_gate, o.grad_up, o.grad_down)
        return [load(b.expert_out.at[which, m], outs[m].at[at], 32 + 3 * which + m) for m in range(3)]

    def put(which, values, at, wait):
        if wait:
            for copy in puts(which, at):
                copy.wait()
        for m in range(3):
            b.expert_out[which, m] = values[:, m * 256 : m * 256 + 256]
        for copy in puts(which, at):
            copy.start()

    def finish(q, total):
        if q >= early_count + 2:
            far_copy(q - 2).wait_send()
        b.far_send[q % 2 if q >= early_count else 2 + q] = total[1].astype(bf16)
        far_copy(q).start()
        put(0, total[0], MINE * c + q, q != early_count)

    def begin_far(q):
        far_copy(q).wait_recv()
        copy = load(o.far.at[q], b.far_here, 22)
        copy.start()
        return copy

    def end_far(q, copy):
        copy.wait()
        put(1, b.far_here[...].astype(f32), MINE * (1 - c) + q, q != early_count)

    def tick(k):
        jobs = [(k - j, j) for j in range(stages) if early_count <= k - j < MINE]
        loads = [begin(*job) for job in jobs]
        far = k - stages
        far_load = begin_far(far) if early_count <= far < MINE else None
        for (q, j), copies in zip(jobs, loads):
            total = end(q, j, copies)
            if j == stages - 1:
                finish(q, total)
        if far_load is not None:
            end_far(far, far_load)


    tok_y = [
        trade(TOK_Y + h, a.tok.at[pl.ds(h * 256, 256)], b.gyo.at[pl.ds(h * 256, 256)], to_row)
        for h in range(2)
    ]
    tok_yc = [
        trade(TOK_YC + h, b.gyo.at[pl.ds(h * 256, 256)], b.gyt.at[pl.ds(h * 256, 256)], to_col)
        for h in range(2)
    ]
    tok_c = trade(TOK_C, a.tok, b.got, to_col)
    heads = [
        trade(WQ, a.wq.at[block(1 - c, 384)], b.wr.at[pl.ds(0, 384)], to_col),
        trade(WK, a.wkey.at[block(1 - c, 128)], b.wr.at[pl.ds(384, 128)], to_col),
        trade(WV, a.wval.at[block(1 - c, 128)], b.wr.at[pl.ds(512, 128)], to_col),
    ]
    gain_copy = trade(GAIN, b.gain_send, b.gain_far, to_col)
    router_copy = trade(ROUTER, a.router, b.router_far, to_col)
    cot_rows = [pl.ds(h * 256, 256) for h in range(2)]
    cot_y = [
        trade(COT_Y + h, a.cot.at[cot_rows[h]], o.cot_y.at[cot_rows[h]], to_row) for h in range(2)
    ]
    cot_c = trade(COT_C, a.cot, o.cot_c, to_col)
    cot_yc = [
        trade(COT_YC + h, o.cot_y.at[cot_rows[h]], o.cot_yc.at[cot_rows[h]], to_col)
        for h in range(2)
    ]
    w_part = trade(
        W_PART,
        a.wparts.at[i] if sliced else a.wout,
        o.wy.at[i] if sliced else o.wy,
        to_row,
    )
    w_gather = [
        remote(o.wy.at[i], o.wy.at[i], (b.gsend, b.grecv), bits, to_dp(bits))
        for bits in (range(1, n) if sliced else ())
    ]
    w_c = trade(W_C, a.wout, o.wc, to_col)
    w_yc = trade(W_YC, o.wy, o.wyc, to_col)

    def front_scope(
        tok, w00, wc, wy, wyc, mixed, k0, k1, vt, n1oo, n1ot, n1yo, n1yt, mrow
    ):
        locals_ = [
            load(a.tok, tok, 0),
            load(a.wq.at[block(c, 384)], b.wk.at[pl.ds(0, 384)], 1),
            load(a.wkey.at[block(c, 128)], b.wk.at[pl.ds(384, 128)], 2),
            load(a.wval.at[block(c, 128)], b.wk.at[pl.ds(512, 128)], 3),
        ]
        late = [
            load(a.wout, w00, 10),
            load(a.cot, b.go.at[own_rows], 11),
        ]
        for copy in locals_ + late:
            copy.start()
        b.gain_send[...] = jnp.zeros_like(b.gain_send)
        b.gain_send[0:1, :] = a.g1[...].reshape(1, 768)
        b.gain_send[1:2, :] = a.g2[...].reshape(1, 768)
        barrier = pltpu.get_barrier_semaphore()
        partners = [to_row, to_col] + [to_dp(bits) for bits in range(1, n)]
        for target in partners:
            pl.semaphore_signal(barrier, inc=1, device_id=target, device_id_type=MESH)
        pl.semaphore_wait(barrier, len(partners))
        for copy in [w_part] + tok_y + [tok_c] + heads + [gain_copy, router_copy, cot_y[0], cot_c, w_c]:
            copy.start()
        for e in range(2):
            for copy in moe_copies(e):
                copy.start()

        w_part.wait()
        for copy in w_gather:
            copy.start()

        seg = a.seg[...].astype(f32)
        seg_column = jnp.broadcast_to(seg, (8, 1024)).T[:, 0:1]
        start, start_column = jnp.zeros_like(seg), jnp.zeros_like(seg_column)
        for number in range(1, 4):
            count = jnp.sum(jnp.where(seg < number, 1.0, 0.0), axis=1, keepdims=True)
            start = jnp.where(seg == number, count, start)
            start_column = jnp.where(seg_column == number, count, start_column)
        b.start[...] = start.astype(jnp.int32)
        lane = lax.broadcasted_iota(jnp.int32, (1024, 128), 1)
        place = lax.broadcasted_iota(jnp.int32, (1024, 128), 0).astype(f32)
        frequency = jnp.exp((lane & 31).astype(f32) * (-2.0 * math.log(10000.0) / HEAD))
        angles = (place - start_column) * frequency
        b.cs[...] = jnp.cos(angles)
        sine = jnp.sin(angles)
        b.sn[...] = jnp.where((lane & 63) < 32, -sine, sine)

        number = jnp.where(lane < MINE, lane + MINE * c, lane - MINE * c)
        number = jnp.where((lane >= MINE) & (c == 1), lane - MINE, number)
        number = jnp.where(lane < E, number, -1)
        used = jnp.zeros((1024, 128), f32)
        routes, number = a.routes[...].astype(f32).T, number.astype(f32)
        for k in range(8):
            used = jnp.where(routes[:, k : k + 1] == number, 1.0, used)
        b.gate[...] = used

        gain_copy.wait()

        def project(x_own, x_oth, place, rows, n_own, n_oth):
            u, v = x_own.astype(f32), x_oth.astype(f32)
            total = jnp.sum(u * u, axis=1, keepdims=True) + jnp.sum(v * v, axis=1, keepdims=True)
            s = lax.rsqrt(total / WIDTH + EPS)
            u = (u * s * b.gain_send[0:1, :]).astype(bf16)
            v = (v * s * b.gain_far[0:1, :]).astype(bf16)
            n_own[rows, :] = u
            n_oth[rows, :] = v
            raw = dot_nt(u, b.wk[...]) + dot_nt(v, b.wr[...])
            cs, sn = b.cs[place, :], b.sn[place, :]
            for t in range(3):
                b.q[place, t * 128 : t * 128 + 128] = rotate(paired(raw, t), cs, sn).astype(bf16)
            b.k[place, :] = rotate(raw[:, 384:512], cs, sn).astype(bf16)
            b.v[place, :] = raw[:, 512:640].astype(bf16)
            return s

        for copy in locals_ + [tok_c] + heads:
            copy.wait()
        for h in range(2):
            rows = slice(h * 256, h * 256 + 256)
            b.s1[rows, :] = project(
                tok[rows, :], b.got[rows, :], block(2 * r + h, 256), rows, n1oo, n1ot
            )
        def flip_cotangent(at):
            rows = block(at, 256)
            b.gf[0:768, rows] = flip_block(b.go[rows, :])
            b.gf[768:1536, rows] = flip_block(b.gt[rows, :])

        cot_c.wait()
        run(load(o.cot_c, b.gt.at[own_rows], 18))
        late[1].wait()
        for h in range(2):
            flip_cotangent(2 * r + h)
        for h in range(2):
            tok_y[h].wait()
            tok_yc[h].start()
        for h in range(2):
            rows = slice(h * 256, h * 256 + 256)
            tok_yc[h].wait()
            project(
                b.gyo[rows, :], b.gyt[rows, :], block(2 * (1 - r) + h, 256), rows, n1yo, n1yt
            )
        saves = [
            load(n1oo, o.n1oo, 12),
            load(n1ot, o.n1ot, 13),
            load(n1yo, o.n1yo, 14),
            load(n1yt, o.n1yt, 15),
        ]
        for copy in saves:
            copy.start()
        for e in range(2, 4):
            for copy in moe_copies(e):
                copy.start()

        load_keys([(b.k, k0, k1)])
        vt[...] = b.v[...].astype(f32).T.astype(bf16)
        mix_y, mix_c, mix_yc = [], [], []
        for at in range(4):
            rows = pl.ds(at * 256, 256)
            mix_y.append(
                trade(MIX_Y + at, mixed.at[rows], b.cland_n.at[rows, pl.ds(0, 384)], to_row)
            )
            mix_c.append(
                trade(MIX_C + at, mixed.at[rows], b.cland_n.at[rows, pl.ds(384, 384)], to_col)
            )
            mix_yc.append(
                trade(
                    MIX_YC + at, b.cland_n.at[rows, pl.ds(0, 384)], b.myc.at[rows], to_col
                )
            )

        def attend(at):
            rows = slice(at * 256, at * 256 + 256)
            window = slice(*key_window(at))
            bias = key_bias(at, b.start[:, rows])
            outs = [None] * 6
            for t in range(3):
                q = b.q[rows, t * 128 : t * 128 + 128] * jnp.asarray(SCALE, bf16)
                for j in range(2):
                    s = dot_nt((k0, k1)[j][window, :], q) + bias
                    top = jnp.max(s, axis=0, keepdims=True)
                    p = jnp.exp(s - top)
                    total = jnp.sum(p, axis=0, keepdims=True)
                    head = t + 3 * j
                    outs[head] = dot_nn(vt[j * 64 : j * 64 + 64, window], p.astype(bf16)) / total
                    b.lse[head : head + 1, rows] = top + jnp.log(total)
            mixed[rows, :] = jnp.concatenate(outs, axis=0).T.astype(bf16)
            mix_y[at].start()
            mix_c[at].start()

        attend(0)
        attend(1)
        for copy in w_gather:
            copy.wait()
        w_yc.start()
        loads = [load(o.wy, wy, 16)]
        loads[0].start()
        attend(2)
        attend(3)

        cot_y[1].start()
        cot_y[0].wait()
        cot_yc[0].start()
        for at in range(2):
            mix_y[at].wait()
            mix_yc[at].start()
        w_c.wait()
        w_yc.wait()
        far_blocks = [block(2 * (1 - r) + h, 256) for h in range(2)]
        loads += [
            load(o.cot_y.at[cot_rows[0]], b.go.at[far_blocks[0]], 17),
            load(o.wc, wc, 19),
            load(o.wyc, wyc, 20),
        ]
        for copy in loads[1:]:
            copy.start()
        cot_yc[0].wait()
        loads.append(load(o.cot_yc.at[cot_rows[0]], b.gt.at[far_blocks[0]], 21))
        loads[-1].start()
        for copy in late[:1] + loads:
            copy.wait()
        flip_cotangent(2 * (1 - r))

        router_copy.wait()
        for source, target in ((a.router, b.wro), (b.router_far, b.wrt)):
            value = source[...].astype(f32)
            low, high = value[0:MINE], value[MINE:E]
            target[...] = jnp.concatenate(
                [
                    jnp.where(c == 0, low, high),
                    jnp.where(c == 0, high, low),
                    jnp.zeros((128 - E, 768), f32),
                ],
                axis=0,
            ).astype(bf16)

        flat = (768, 768)
        for at in range(2):
            rows = slice(at * 512, at * 512 + 512)
            for piece in (2 * at, 2 * at + 1):
                mix_c[piece].wait()
                mix_yc[piece].wait()
            here, there = mixed[rows, :], b.cland_n[rows, 384:768]
            near = jnp.concatenate(
                [jnp.where(c == 0, here, there), jnp.where(c == 0, there, here)], axis=1
            )
            here, there = b.cland_n[rows, 0:384], b.myc[rows, :]
            far = jnp.concatenate(
                [jnp.where(c == 0, here, there), jnp.where(c == 0, there, here)], axis=1
            )
            mrow[rows, :] = near
            mine = r == at
            x_own = jnp.where(mine, tok[...], b.gyo[...]).astype(f32)
            x_oth = jnp.where(mine, b.got[...], b.gyt[...]).astype(f32)
            mid_own = x_own + (
                dot_nt(near, w00[...]) + dot_nt(far, wy[...].reshape(flat))
            )
            if at == 0:
                for piece in (2, 3):
                    mix_y[piece].wait()
                    mix_yc[piece].start()
            mid_oth = x_oth + (dot_nt(near, wc[...]) + dot_nt(far, wyc[...].reshape(flat)))
            total = jnp.sum(mid_own * mid_own, axis=1, keepdims=True) + jnp.sum(
                mid_oth * mid_oth, axis=1, keepdims=True
            )
            s = lax.rsqrt(total / WIDTH + EPS)

            @pl.when(mine)
            def _():
                b.mid[...] = mid_own
                b.s2[...] = s

            no = (mid_own * s * b.gain_send[1:2, :]).astype(bf16)
            nt = (mid_oth * s * b.gain_far[1:2, :]).astype(bf16)
            b.n2o[rows, :] = no
            b.n2t[rows, :] = nt
            for piece in range(2):
                part = slice(piece * 256, piece * 256 + 256)
                place = slice(at * 512 + piece * 256, at * 512 + piece * 256 + 256)
                b.n2f[0:768, place] = flip_block(no[part, :])
                b.n2f[768:1536, place] = flip_block(nt[part, :])
            logits = dot_nt(no, b.wro[...]) + dot_nt(nt, b.wrt[...])
            used = b.gate[rows, :]
            top = jnp.max(jnp.where(used > 0.0, logits, NEG), axis=1, keepdims=True)
            weight = jnp.where(used > 0.0, jnp.exp(jnp.minimum(logits - top, 0.0)), 0.0)
            b.gate[rows, :] = weight / jnp.sum(weight, axis=1, keepdims=True)
        cot_y[1].wait()
        cot_yc[1].start()
        run(load(o.cot_y.at[cot_rows[1]], b.go.at[far_blocks[1]], 17))
        cot_yc[1].wait()
        run(load(o.cot_yc.at[cot_rows[1]], b.gt.at[far_blocks[1]], 21))
        flip_cotangent(2 * (1 - r) + 1)
        saves.append(load(mrow, o.mrow, 22))
        saves[-1].start()
        for copy in saves:
            copy.wait()
        for e in range(4, MINE):
            for copy in moe_copies(e):
                copy.start()

    pl.run_scoped(
        front_scope,
        vb(512, 768),
        vb(768, 768),
        vb(768, 768),
        vb(n, w, 768) if sliced else vb(768, 768),
        vb(n, w, 768) if sliced else vb(768, 768),
        vb(1024, 384),
        vb(1024, 128),
        vb(1024, 128),
        vb(128, 1024),
        vb(512, 768),
        vb(512, 768),
        vb(512, 768),
        vb(512, 768),
        vb(1024, 768),
    )


    n_col = trade(N_COL, b.n2t, b.cland_n, to_col)
    o_col = trade(O_COL, b.gt, o.cland_o, to_col)

    def experts_scope(
        weights, gu_all, hs_all, acc_no, acc_nt, acc_oo, acc_ot, shards
    ):
        b.weights = weights
        for copy in moe_copies(0):
            copy.wait_recv()
        for copy in weight_loads(0, 0):
            copy.start()
        b.ggs[...] = jnp.zeros_like(b.ggs)

        def one(e, carry):
            slot = lax.rem(e, 2)

            @pl.when(e < MINE - 1)
            def _():
                for copy in moe_copies(e + 1):
                    copy.wait_recv()
                for copy in weight_loads(e + 1, 1 - slot):
                    copy.start()

            for copy in weight_loads(e, slot):
                copy.wait()
            wgk, wgr, wuk, wur, wdk, wdr = [b.weights.at[slot, k] for k in range(6)]
            for t in range(2):
                rows = slice(t * 512, t * 512 + 512)
                no, nt = b.n2o[rows, :], b.n2t[rows, :]
                gate_act = dot_nt(no, wgk[...]) + dot_nt(nt, wgr[...])
                up_act = dot_nt(no, wuk[...]) + dot_nt(nt, wur[...])
                grad = dot_nt(b.go[rows, :], wdk[...]) + dot_nt(b.gt[rows, :], wdr[...])
                lane = lax.broadcasted_iota(jnp.int32, (512, 128), 1)
                weight = jnp.sum(
                    jnp.where(lane == e, b.gate[rows, :], 0.0), axis=1, keepdims=True
                )
                s = 1.0 / (1.0 + jnp.exp(-gate_act))
                silu = gate_act * s
                hidden = (silu * up_act).astype(bf16).astype(f32)
                inner = jnp.sum(hidden * grad, axis=1, keepdims=True)
                b.ggs[rows, :] += jnp.where(lane == e, inner, 0.0)
                hs_all[rows, :] = (hidden * weight).astype(bf16)
                grad = grad * weight
                gu_all[rows, 0:256] = (
                    grad * up_act * s * (1.0 + gate_act * (1.0 - s))
                ).astype(bf16)
                gu_all[rows, 256:512] = (grad * silu).astype(bf16)
            first = 1 - lax.div(e + MINE - early_count, MINE)
            for half in range(2):
                rows = slice(half * 768, half * 768 + 768)
                gates = dot_nn(b.n2f[rows, :], gu_all[...])
                split_shards(gates, half, slice(0, 512), i, near_first, shards, far_first, first)
                downs = dot_nn(b.gf[rows, :], hs_all[...])
                split_shards(downs, half, slice(512, 768), i, near_first, shards, far_first, first)
            save = load(shards, o.grad.at[e], 8)
            save.start()

            for early in range(early_count):

                @pl.when(e == early)
                def _():
                    save.wait()
                    stage(early, 0).start()

            @pl.when(e == 0)
            def _():
                for total in (acc_no, acc_nt, acc_oo, acc_ot):
                    total[...] = jnp.zeros_like(total)

            gu, hs = gu_all[...], hs_all[...]
            acc_no[...] += dot_nn(gu, jnp.concatenate([wgk[...], wuk[...]], axis=0))
            acc_nt[...] += dot_nn(gu, jnp.concatenate([wgr[...], wur[...]], axis=0))
            acc_oo[...] += dot_nn(hs, wdk[...])
            acc_ot[...] += dot_nn(hs, wdr[...])

            @pl.when(e >= early_count)
            def _():
                save.wait()
                stage(e, 0).start()

            @pl.when(e == 3)
            def _():
                advance(0, 0)

            @pl.when(e == 5)
            def _():
                if early_count == 1:
                    tick(1)
                tick(2)

            @pl.when(e == 6)
            def _():
                if early_count == 2:
                    advance(1, 0)

            @pl.when(e == 7)
            def _():
                advance(0, 1)
                tick(3)

            return carry

        lax.fori_loop(0, MINE, one, 0)

        b.gg_send[...] = b.ggs[...].T[0:8]
        row_copy = trade(GG_ROW, b.gg_send, b.gg_row, to_row)
        row_copy.start()
        b.n2t[...] = acc_nt[...].astype(bf16)
        n_col.start()
        b.gt[...] = acc_ot[...].astype(bf16)
        o_col.start()
        b.n2o[...] = acc_no[...].astype(bf16)
        b.go[...] = acc_oo[...].astype(bf16)
        row_copy.wait()
        b.gg_sum[...] = b.gg_send[...] + b.gg_row[...]
        col_copy = trade(GG_COL, b.gg_sum, b.gg_col, to_col)
        col_copy.start()
        col_copy.wait()
        gate_grad = jnp.concatenate(
            [b.gg_sum[...], b.gg_col[...], jnp.zeros((112, 1024), f32)], axis=0
        ).T
        weighted = b.gate[...] * gate_grad
        grad_logits = weighted - b.gate[...] * jnp.sum(weighted, axis=1, keepdims=True)
        b.ggs[...] = grad_logits
        routers = dot_nn(b.n2f[0:768, :], grad_logits.astype(bf16))
        split_shards(routers, 0, slice(768, 896), i, near_first, b.shards_a)

    pl.run_scoped(
        experts_scope,
        vb(2, 6, 256, 768),
        vb(1024, 512),
        vb(1024, 256),
        vf(1024, 768),
        vf(1024, 768),
        vf(1024, 768),
        vf(1024, 768),
        vb(n, 2, w, 768),
    )


    def rest_scope(
        wmo, wmt, cot, tok, land_y, k0, k1, v0, v1, kt, sumk0, sumk1, sumv0, sumv1,
        grads, shards_b, shards_c, in_stage, came_a, sum_a, came_b, sum_b, came_c, sum_c,
        far_send, far_here, expert_out,
        out_out, router_out,
    ):
        b.came_a, b.sum_a, b.came_b, b.sum_b = came_a, sum_a, came_b, sum_b
        b.came_c, b.sum_c = came_c, sum_c
        b.far_send, b.far_here, b.expert_out = far_send, far_here, expert_out
        thirds = [(pl.ds(k * 512, 512), pl.ds(0, 768)) for k in range(3)]
        n1oo, n1ot, n1yo = [b.n2f.at[at] for at in thirds]
        n1yt, mro, mry = [b.gf.at[at] for at in thirds]
        early = [load(a.cot, cot, 10), load(a.tok, tok, 11)]
        late = [
            load(o.n1oo, n1oo, 12),
            load(o.n1ot, n1ot, 13),
            load(o.n1yo, n1yo, 14),
            load(o.n1yt, n1yt, 15),
            load(o.mrow.at[own_rows], mro, 16),
            load(o.mrow.at[far_rows], mry, 17),
            load(a.wout.at[:, block(c, 384)], wmo, 18),
            load(o.wc.at[:, block(c, 384)], wmt, 19),
        ]
        for copy in early + late:
            copy.start()

        def norm_back(values, scale, gain, gradient, name, land):
            weighted = gradient * gain
            b.stat[...] = jnp.broadcast_to(
                jnp.sum(weighted * values, axis=1, keepdims=True), (512, 128)
            )
            copy = trade(name, b.stat, land, to_col)
            copy.start()
            gain_grad = jnp.sum(gradient * values * scale, axis=0, keepdims=True)
            copy.wait()
            inner = (b.stat[...] + land[...])[:, 0:1]
            grad = scale * weighted - values * (scale * scale * scale) * (inner / WIDTH)
            return grad, gain_grad

        n_col.wait()
        b.ysend_n[...] = (
            b.n2o[far_rows, :].astype(f32) + b.cland_n[far_rows, :].astype(f32)
        ).astype(bf16)
        y_n = trade(N_ROW, b.ysend_n, b.yland_n, to_row)
        y_n.start()
        gl = b.ggs[own_rows, :]
        gl_high = gl.astype(bf16)
        gl_low = (gl - gl_high.astype(f32)).astype(bf16)
        b.gmid[...] = (
            b.n2o[own_rows, :].astype(f32)
            + b.cland_n[own_rows, :].astype(f32)
            + dot_nn(gl_high, b.wro[...])
            + dot_nn(gl_low, b.wro[...])
        )
        if early_count == 2:
            advance(1, 1)
        tick(4)
        for copy in early:
            copy.wait()
        y_n.wait()
        grad, gain_grad = norm_back(
            b.mid[...],
            b.s2[...],
            b.gain_send[1:2, :],
            b.gmid[...] + b.yland_n[...].astype(f32),
            STAT_TWO,
            b.stat_land,
        )
        b.gain_part[...] = jnp.zeros_like(b.gain_part)
        b.gain_part[1:2, :] = gain_grad
        b.gmid[...] = cot[...].astype(f32) + grad
        b.goo[...] = b.gmid[...].astype(bf16)
        y_g = trade(G_ROW, b.goo, b.gyo, to_row)
        c_g = trade(G_COL, b.goo, b.got, to_col)
        y_g.start()
        c_g.start()

        o_col.wait()
        run(load(o.cland_o, b.gt, 4))
        b.ysend_o[...] = (
            b.go[far_rows, :].astype(f32) + b.gt[far_rows, :].astype(f32)
        ).astype(bf16)
        y_o = trade(O_ROW, b.ysend_o, o.yland_o, to_row)
        y_o.start()
        b.mid[...] = (
            b.mid[...] + b.go[own_rows, :].astype(f32) + b.gt[own_rows, :].astype(f32)
        )
        tick(5)

        y_g.wait()
        c_gy = trade(G_ROW_COL, b.gyo, b.gyt, to_col)
        c_gy.start()
        for copy in late:
            copy.wait()
        outs = dot_tn(mro[...], b.goo[...]) + dot_tn(mry[...], b.gyo[...])
        split_shards(outs, 0, slice(0, 768), i, near_first, b.shards_a)
        save = load(b.shards_a, o.grad_a, 4)
        save.start()
        load_keys([(b.k, k0, k1), (b.v, v0, v1)])
        kt[...] = b.k[...].astype(f32).T.astype(bf16)
        for total in (sumk0, sumk1, sumv0, sumv1):
            total[...] = jnp.zeros_like(total)
        save.wait()
        stage(A, 0).start()
        c_g.wait()
        c_gy.wait()

        def one_block(at):
            near = at // 2 == r
            rows = slice((at % 2) * 256, (at % 2) * 256 + 256)
            place = slice(at * 256, at * 256 + 256)
            g_own = jnp.where(near, b.goo[rows, :], b.gyo[rows, :])
            g_oth = jnp.where(near, b.got[rows, :], b.gyt[rows, :])
            gm = (dot_nn(g_own, wmo[...]) + dot_nn(g_oth, wmt[...])).astype(bf16)
            window = slice(*key_window(at))
            bias = key_bias(at, b.start[:, place])
            parts = [None] * 6
            for t in range(3):
                qt = b.q[place, t * 128 : t * 128 + 128] * jnp.asarray(SCALE, bf16)
                gmt = paired(gm, t)
                for j in range(2):
                    head = t + 3 * j
                    s = dot_nt((k0, k1)[j][window, :], qt) + bias
                    p = jnp.exp(s - b.lse[head : head + 1, place])
                    gp = dot_nt((v0, v1)[j][window, :], gmt)
                    inner = jnp.sum(p * gp, axis=0, keepdims=True)
                    gs = (p * (gp - inner)).astype(bf16)
                    (sumv0, sumv1)[j][window, :] += dot_nn(p.astype(bf16), gmt)
                    (sumk0, sumk1)[j][window, :] += dot_nn(gs, qt)
                    parts[head] = dot_nn(kt[j * 64 : j * 64 + 64, window], gs) * SCALE
            gq = jnp.concatenate(parts, axis=0).T
            cosine, sine = b.cs[place, :], b.sn[place, :]
            for t in range(3):
                grads[place, t * 128 : t * 128 + 128] = rotate(
                    gq[:, t * 128 : t * 128 + 128], cosine, -sine
                ).astype(bf16)

        for at in range(4):
            one_block(at)
        tick(6)
        lane = lax.broadcasted_iota(jnp.int32, (1024, 128), 1)
        gk = jnp.where(lane < 64, sumk0[...], sumk1[...])
        gv = jnp.where(lane < 64, sumv0[...], sumv1[...])
        grads[:, 384:512] = rotate(gk, b.cs[...], -b.sn[...]).astype(bf16)
        grads[:, 512:640] = gv.astype(bf16)

        b.n2t[...] = dot_nn(grads[...], b.wr[...]).astype(bf16)
        c_p = trade(P_COL, b.n2t, o.cland_p, to_col)
        c_p.start()
        b.n2o[...] = dot_nn(grads[...], b.wk[...]).astype(bf16)
        for shards, left, far, k, order in (
            (shards_b, n1ot, n1yt, B, far_first),
            (shards_c, n1oo, n1yo, C, near_first),
        ):
            heads_grad = dot_tn(left[...], grads[own_rows, :]) + dot_tn(
                far[...], grads[far_rows, :]
            )
            split_shards(heads_grad, 0, slice(0, 640), i, order, shards)
            run(load(shards, o.grad_b if k is B else o.grad_c, 4))
            stage(k, 0).start()
        c_p.wait()
        run(load(o.cland_p, b.gt, 4))
        b.ysend_n[...] = (
            b.n2o[far_rows, :].astype(f32) + b.gt[far_rows, :].astype(f32)
        ).astype(bf16)
        y_p = trade(P_ROW, b.ysend_n, o.yland_p, to_row)
        y_p.start()
        tick(7)

        y_o.wait()
        run(load(o.yland_o, land_y, 4))
        land_y[...] = (b.mid[...] + land_y[...].astype(f32)).astype(bf16)
        run(load(land_y, o.output, 7))
        y_p.wait()
        run(load(o.yland_p, land_y, 4))
        grad, gain_grad = norm_back(
            tok[...].astype(f32),
            b.s1[...],
            b.gain_send[0:1, :],
            b.n2o[own_rows, :].astype(f32)
            + b.gt[own_rows, :].astype(f32)
            + land_y[...].astype(f32),
            STAT_ONE,
            b.stat_land,
        )
        in_stage[...] = b.gmid[...] + grad
        last = load(in_stage, o.input_grad, 7)
        last.start()
        b.gain_part[0:1, :] = gain_grad
        advance(B, 0)

        tick(8)
        for early in range(early_count):
            for j in range(2, stages - 1):
                advance(early, j)
            finish(early, advance(early, stages - 1))
        for j in range(1, stages - 1):
            advance(B, j)
        advance(A, 0)
        for early in range(early_count):
            end_far(early, begin_far(early))
        tick(9)

        step = trade(GAIN_ROW, b.gain_part, b.gain_land.at[0], to_row)
        step.start()
        step.wait()
        b.gain_row[...] = b.gain_part[...] + b.gain_land[0]
        step = trade(GAIN_X, b.gain_row, b.gain_land.at[1], to_x)
        step.start()
        step.wait()
        b.gain_x[...] = b.gain_row[...] + b.gain_land[1]
        steps = [
            remote(b.gain_x, b.gain_land.at[1 + s], (b.hsend, b.hrecv), s, to_dp(2 * s))
            for s in range(1, nz)
        ]
        for step in steps:
            step.start()
        total = b.gain_x[...]
        for step in steps:
            step.wait()
        for s in range(1, nz):
            total = total + b.gain_land[1 + s]
        last.wait()
        b.gain_row[...] = total
        run(load(b.gain_row, o.gains, 7))

        advance(C, 0)
        for j in range(1, stages - 1):
            advance(A, j)
        b.far_b_send[...] = advance(B, stages - 1)[0].astype(bf16)
        copy = trade(FAR_B, b.far_b_send, o.far_b, to_col)
        copy.start()
        for k in range(10, MINE + stages):
            tick(k)
        for j in range(1, stages - 1):
            advance(C, j)
        total = advance(A, stages - 1)[0]
        out_out[...] = total[:, 0:768]
        router_out[...] = total[:, 768:896]
        run(load(out_out, o.grad_out, 4), load(router_out, o.grad_router, 5))

        def put_heads(values, which):
            out_out[:, 0:640] = values
            run(
                load(out_out.at[:, pl.ds(0, 384)], o.grad_query.at[:, block(which, 384)], 4),
                load(out_out.at[:, pl.ds(384, 128)], o.grad_key.at[:, block(which, 128)], 5),
                load(out_out.at[:, pl.ds(512, 128)], o.grad_value.at[:, block(which, 128)], 6),
            )

        copy.wait()
        run(load(o.far_b, b.far_b_here, 21))
        put_heads(b.far_b_here[...].astype(f32), 1 - c)
        put_heads(advance(C, stages - 1)[0], c)

        for e in range(MINE):
            for copy in moe_copies(e):
                copy.wait_send()
        for k in list(range(MINE)) + [A, B, C]:
            stage(k, 0).wait_send()
        for early in range(early_count):
            far_copy(early).wait_send()
        far_copy(MINE - 2).wait_send()
        far_copy(MINE - 1).wait_send()
        for which in range(2):
            for copy in puts(which, 0):
                copy.wait()

    pl.run_scoped(
        rest_scope,
        *[vb(768, 384)] * 2,
        vb(512, 768),
        vb(512, 768),
        vb(512, 768),
        *[vb(1024, 128)] * 4,
        vb(128, 1024),
        *[vf(1024, 128)] * 4,
        vb(1024, 640),
        vb(n, 1, w, 640),
        vb(n, 1, w, 640),
        vf(512, 768),
        *[vb(nz, 1, w, 896)] * 2,
        *[vb(nz, 1, w, 640)] * 4,
        vb(2 + early_count, w, 768),
        vb(w, 768),
        vf(2, 3, w, 256),
        vf(w, 768),
        vf(w, 128),
    )


def hand_over_kernel(gains, router, *refs):
    sources, gain_one, gain_two, router_out = refs[:9], refs[9], refs[10], refs[11]
    targets, places, sems = refs[12:21], refs[21:30], refs[30]
    copies = [
        pltpu.make_async_copy(source, place, sems.at[0, k])
        for k, (source, place) in enumerate(zip(sources, places))
    ]
    for copy in copies:
        copy.start()
    gain_one[...] = gains[0, :]
    gain_two[...] = gains[1, :]
    c, w = lax.axis_index("col"), router.shape[0]
    value = jnp.concatenate([router[...], jnp.zeros((128 - w, 128), f32)], axis=0).T[0:E, 0:w]
    low, high = value[0:MINE], value[MINE:E]
    router_out[...] = jnp.concatenate(
        [jnp.where(c == 0, low, high), jnp.where(c == 0, high, low)], axis=0
    )
    for k in range(9):
        copies[k].wait()
        copies[k] = pltpu.make_async_copy(places[k], targets[k], sems.at[1, k])
        copies[k].start()
    for copy in copies:
        copy.wait()


def local(
    n,
    tokens,
    cotangent,
    gain_one,
    w_query,
    key_weight,
    value_weight,
    w_out,
    gain_two,
    w_router,
    w_gate,
    w_up,
    w_down,
    routes,
    segments,
):
    nz, w = n // 2, 768 // n
    sliced = w % 16 == 0

    def sds(shape, dtype):
        return jax.ShapeDtypeStruct(shape, dtype)

    values = dict(
        tok=tokens,
        cot=cotangent,
        wq=w_query,
        wkey=key_weight,
        wval=value_weight,
        wout=w_out,
        wparts=w_out.reshape(n, w, 768) if sliced else w_out,
        wg=w_gate,
        wu=w_up,
        wd=w_down,
        g1=gain_one,
        g2=gain_two,
        router=w_router,
        routes=routes.T,
        seg=segments,
    )
    shapes = dict(
        output=sds((512, 768), bf16),
        input_grad=sds((512, 768), f32),
        gains=sds((8, 768), f32),
        grad_query=sds((w, 768), f32),
        grad_key=sds((w, 256), f32),
        grad_value=sds((w, 256), f32),
        grad_out=sds((w, 768), f32),
        grad_router=sds((w, 128), f32),
        grad_gate=sds((E, w, 256), f32),
        grad_up=sds((E, w, 256), f32),
        grad_down=sds((E, w, 256), f32),
        far=sds((MINE, w, 768), bf16),
        far_b=sds((w, 640), bf16),
    )
    stages = n.bit_length() - 1
    piece, piece_a, piece_b = (2, w, 768), (1, w, 896), (1, w, 640)
    halves, whole = sds((512, 768), bf16), sds((1024, 768), bf16)
    expert_weight = sds((MINE, 256, 768), bf16)
    parts = sds((n, w, 768) if sliced else (768, 768), bf16)
    shapes.update(
        grad=sds((MINE, n) + piece, bf16),
        land=sds((MINE, n - 1) + piece, bf16),
        grad_a=sds((n,) + piece_a, bf16),
        land_a=sds((n - 1,) + piece_a, bf16),
        grad_b=sds((n,) + piece_b, bf16),
        land_b=sds((n - 1,) + piece_b, bf16),
        grad_c=sds((n,) + piece_b, bf16),
        land_c=sds((n - 1,) + piece_b, bf16),
        cland_o=whole,
        cland_p=whole,
        yland_o=halves,
        yland_p=halves,
        cot_y=halves,
        cot_c=halves,
        cot_yc=halves,
        n1oo=halves,
        n1ot=halves,
        n1yo=halves,
        n1yt=halves,
        rg=expert_weight,
        ru=expert_weight,
        rd=expert_weight,
        wy=parts,
        wyc=parts,
        wc=sds((768, 768), bf16),
        mrow=whole,
    )

    vb = lambda *shape: pltpu.VMEM(shape, bf16)
    vf = lambda *shape: pltpu.VMEM(shape, f32)
    dma = pltpu.SemaphoreType.DMA
    scratch = dict(
        n2o=vb(1024, 768),
        n2t=vb(1024, 768),
        go=vb(1024, 768),
        gt=vb(1024, 768),
        n2f=vb(1536, 1024),
        gf=vb(1536, 1024),
        q=vb(1024, 384),
        k=vb(1024, 128),
        v=vb(1024, 128),
        lse=vf(8, 1024),
        start=pltpu.VMEM((1, 1024), jnp.int32),
        cs=vf(1024, 128),
        sn=vf(1024, 128),
        wk=vb(640, 768),
        wr=vb(640, 768),
        wro=vb(128, 768),
        wrt=vb(128, 768),
        router_far=vb(E, 768),
        gain_send=vf(8, 768),
        gain_far=vf(8, 768),
        mid=vf(512, 768),
        s1=vf(512, 1),
        s2=vf(512, 1),
        myc=vb(1024, 384),
        gate=vf(1024, 128),
        ggs=vf(1024, 128),
        gg_send=vf(8, 1024),
        gg_row=vf(8, 1024),
        gg_sum=vf(8, 1024),
        gg_col=vf(8, 1024),
        cland_n=vb(1024, 768),
        yland_n=vb(512, 768),
        ysend_n=vb(512, 768),
        ysend_o=vb(512, 768),
        goo=vb(512, 768),
        gyo=vb(512, 768),
        got=vb(512, 768),
        gyt=vb(512, 768),
        gmid=vf(512, 768),
        stat=vf(512, 128),
        stat_land=vf(512, 128),
        gain_part=vf(8, 768),
        gain_row=vf(8, 768),
        gain_x=vf(8, 768),
        gain_land=vf(nz + 1, 8, 768),
        came=vb(n - 1, *piece),
        sums=vb(stages + early_experts(n), nz, *piece),
        shards_a=vb(n, *piece_a),
        far_b_send=vb(w, 640),
        far_b_here=vb(w, 640),
        wsem=dma((2, 6)),
        lsem=dma((38,)),
        esend=dma((TRADES,)),
        erecv=dma((TRADES,)),
        msend=dma((3 * MINE,)),
        mrecv=dma((3 * MINE,)),
        gsend=dma((n,)),
        grecv=dma((n,)),
        hsend=dma((nz,)),
        hrecv=dma((nz,)),
        fsend=dma((MINE,)),
        frecv=dma((MINE,)),
        xsend=dma(((MINE + 3) * stages,)),
        xarrive=dma(((MINE + 3) * stages,)),
    )
    anywhere, inside = pl.BlockSpec(memory_space=pl.ANY), pl.BlockSpec(memory_space=pltpu.VMEM)
    results = pl.pallas_call(
        functools.partial(layer_kernel, n, tuple(values), tuple(shapes), tuple(scratch)),
        out_shape=tuple(shapes.values()),
        in_specs=[anywhere] * 10 + [inside] * 5,
        out_specs=tuple(anywhere for _ in shapes),
        scratch_shapes=list(scratch.values()),
        compiler_params=pltpu.CompilerParams(
            vmem_limit_bytes=63 * MIB, collective_id=0, has_side_effects=True
        ),
        cost_estimate=pl.CostEstimate(
            flops=80 * 10**9, bytes_accessed=150 * MIB, transcendentals=0
        ),
        name="layer",
    )(*values.values())
    gains, router = results[2], results[7]
    moved = [*results[:2], *results[3:7], *results[8:11]]
    gain = sds((768,), f32)
    done = pl.pallas_call(
        hand_over_kernel,
        out_shape=(gain, gain, sds((E, w), f32)) + tuple(sds(x.shape, x.dtype) for x in moved),
        in_specs=[inside] * 2 + [anywhere] * 9,
        out_specs=(inside,) * 3 + (anywhere,) * 9,
        scratch_shapes=[pltpu.VMEM(x.shape, x.dtype) for x in moved] + [dma((2, 9))],
        compiler_params=pltpu.CompilerParams(vmem_limit_bytes=62 * MIB),
        name="hand_over",
    )(gains, router, *moved)
    gain_one, gain_two, router, output, input_grad = done[:5]
    heads, experts = [x.T for x in done[5:9]], [x.swapaxes(1, 2) for x in done[9:]]
    return output, input_grad, gain_one, *heads, gain_two, router, *experts


def solution(mesh):
    in_specs = (
        P(("dp", "row"), "col"),
        P(("dp", "row"), "col"),
        P("col"),
        P("row", "col"),
        P("row", "col"),
        P("row", "col"),
        P("col", "row"),
        P("col"),
        P(None, "col"),
        P(None, "row", "col"),
        P(None, "row", "col"),
        P(None, "row", "col"),
        P("dp", None),
        P("dp", None),
    )
    out_specs = (
        P(("dp", "row"), "col"),
        P(("dp", "row"), "col"),
        P("col"),
        P("row", ("col", "dp")),
        P("row", ("col", "dp")),
        P("row", ("col", "dp")),
        P("col", ("row", "dp")),
        P("col"),
        P(None, ("col", "dp")),
        P(None, "row", ("col", "dp")),
        P(None, "row", ("col", "dp")),
        P(None, "row", ("col", "dp")),
    )
    return jax.shard_map(
        functools.partial(local, mesh.shape["dp"]),
        mesh=mesh,
        in_specs=in_specs,
        out_specs=out_specs,
        check_vma=False,
    )
```
